32 devices in a mesh: ctx: 8 (over z, x), grp: 4 (over y, core).
Axes of the slice: x: 2, y: 2, z: 4, core: 2. Of those that a mesh axis runs over, the one named last changes fastest.
Arguments:
- queries: bfloat16 [16384, 512], P('ctx', 'grp'), may hold values from -100 to 100
- kv_cache: bfloat16 [16384, 256], P(('ctx', 'grp')), may hold values from -6 to 6
- grad_out: bfloat16 [16384, 512], P('ctx', 'grp'), may hold values from -6 to 6
- doc_tiles: int32 [4], replicated, may hold values from 1 to 12, 32 in all
Outputs:
- grad_queries: bfloat16 [16384, 512], P('ctx', 'grp')
- grad_kv: bfloat16 [16384, 256], P(('ctx', 'grp'))
The draws below stay inside these ranges and needn't reach their ends.
All inputs are finite; a program needn't handle non-finite values.
Results may differ from the reference program's by a relative error of at most 0.0059.
Values may be sent and summed in bfloat16 or wider, within the bound.
No kernel may reach another device: no remote copies, remote signals or barrier semaphores. Data moves between devices by JAX's collectives and lax.ppermute only.
A program may use at most 64 MiB of HBM per device.

```python
import math
import jax
import jax.numpy as jnp
import numpy as np
from jax import lax

DH = 128
HQ = 4
TILE = 512
MAXT = 12
TOKENS = 16384
NDOCS = 4


def shared_keys(key):
    return jnp.clip(jax.random.normal(key, (TOKENS, DH), jnp.float32), -5.0, 5.0)


def draw_kv_cache(key, part):
    keys = shared_keys(key)
    key = jax.random.fold_in(key, 3)
    values = jnp.clip(jax.random.normal(key, (TOKENS, DH), jnp.float32), -6.0, 6.0)
    return jnp.concatenate([keys, values], axis=1).astype(jnp.bfloat16)


def draw_queries(key, part):
    key = jax.random.fold_in(key, 5)
    queries = jnp.clip(jax.random.normal(key, (TOKENS, HQ * DH), jnp.float32), -6.0, 6.0)
    return queries.astype(jnp.bfloat16)


def steps_of(own_key, dims, shards, smallest, top_value):
    loudness = 1.0
    for axis_at, parts in shards:
        draws = jax.random.uniform(jax.random.fold_in(jax.random.fold_in(own_key, 6), axis_at), (parts,), jnp.float32, smallest / len(shards), top_value / len(shards))
        loudness = loudness * jnp.repeat(jnp.exp(draws), dims[axis_at] // parts).reshape((-1,) + (1,) * (len(dims) - 1 - axis_at))
    return loudness


def length_profile(amount, total, reach, lean):
    portions = [(1 << 20) // math.isqrt(grade ** lean) + 1 for grade in range(2, amount + 1)]
    surplus, counts = total - reach - (amount - 1), [1] * (amount - 1)
    while surplus > 0:
        free = [i for i in range(amount - 1) if counts[i] < reach]
        pool, remaining = sum([portions[i] for i in free]), surplus
        for i in free:
            more = min(reach - counts[i], max(1, remaining * portions[i] // pool), surplus)
            counts[i] = counts[i] + more
            surplus = surplus - more
    return np.array([reach] + counts)


def ragged(stream_key, amount, total, limit, slope):
    if amount == 2:
        one = jax.random.randint(stream_key, (), max(1, total - limit), min(limit, total - 1) + 1)
        return jnp.stack([one, total - one])
    sizes = jnp.asarray(length_profile(amount, total, limit, slope), jnp.int32)
    twos = (amount - 1) // 2
    donor, taker = sizes[1:1 + 2 * twos:2], sizes[2:2 + 2 * twos:2]
    margin = jnp.minimum(donor - 1, limit - taker)
    shifted = jax.random.randint(jax.random.fold_in(stream_key, 1), (twos,), 0, 1 << 20) % (margin + 1)
    sizes = sizes.at[1:1 + 2 * twos:2].set(donor - shifted).at[2:2 + 2 * twos:2].set(taker + shifted)
    return sizes[jax.random.permutation(jax.random.fold_in(stream_key, 2), amount)]


def scatter_about(stream_key, shape, spread, limit, pieces=(), held_as=jnp.bfloat16):
    entries = spread * jax.random.normal(stream_key, shape, jnp.float32)
    if pieces:
        entries = entries * steps_of(stream_key, shape, pieces, -0.22, 0.18)
    return jnp.clip(entries, -limit, limit).astype(held_as)


def setup_inputs(seed: int = 0) -> dict:
    streams_of = jax.random.split(jax.random.key(seed), 5)
    queries = draw_queries(jax.random.fold_in(streams_of[4], 71), 0)
    kv_cache = draw_kv_cache(jax.random.fold_in(streams_of[4], 71), 0)
    grad_out = scatter_about(streams_of[2], (TOKENS, HQ * DH), 1.0, 6.0, ((0, 8), (1, 4)))
    doc_tiles = ragged(streams_of[3], NDOCS, TOKENS // TILE, MAXT, 1).astype(jnp.int32)
    return {"queries": queries, "kv_cache": kv_cache, "grad_out": grad_out, "doc_tiles": doc_tiles}


NEG_FILL = -1e+30

def document_starts(doc_tiles, tile_count):
    doc_ends = jnp.cumsum(doc_tiles).astype(jnp.int32)
    doc_begins = (doc_ends - doc_tiles).astype(jnp.int32)
    tile_ids = jnp.arange(tile_count, dtype=jnp.int32)
    inside = (tile_ids[:, None] >= doc_begins[None, :]) & (tile_ids[:, None] < doc_ends[None, :])
    return lax.optimization_barrier(jnp.sum(jnp.where(inside, doc_begins[None, :], 0), axis=1)).astype(jnp.int32)

def widen(array):
    return array.astype(jnp.float32)

def narrow_keep(array):
    return widen(lax.optimization_barrier(array.astype(jnp.bfloat16)))

def reference(queries, kv_cache, grad_out, doc_tiles):
    tile_count = TOKENS // TILE
    scale = 1.0 / math.sqrt(DH)
    starts = document_starts(doc_tiles, tile_count)
    query_tiles = queries.reshape(tile_count, TILE, HQ, DH)
    grad_tiles = grad_out.reshape(tile_count, TILE, HQ, DH)
    cache_tiles = kv_cache.reshape(tile_count, TILE, 2 * DH)
    row_ids = jnp.arange(TILE, dtype=jnp.int32)
    causal = row_ids[:, None] >= row_ids[None, :]

    def per_tile(grad_cache, inputs):
        q_tile, g_tile, tile_pos = inputs
        first_tile = starts[tile_pos]
        q_wide = widen(q_tile)
        g_wide = widen(g_tile)

        def scores_at(key_pos):
            kv_tile = widen(lax.dynamic_index_in_dim(cache_tiles, key_pos, 0, keepdims=False))
            raw = jnp.einsum('qhd,kd->hqk', q_wide, kv_tile[:, :DH]) * scale
            keep = jnp.logical_or(key_pos != tile_pos, causal)
            return (jnp.where(keep[None], raw, NEG_FILL), kv_tile)

        def first_pass(key_pos, carry):
            row_top, row_total = carry
            scores, _ = scores_at(key_pos)
            new_top = jnp.maximum(row_top, lax.optimization_barrier(jnp.max(scores, axis=2)))
            row_total = row_total * jnp.exp(row_top - new_top) + lax.optimization_barrier(jnp.sum(jnp.exp(scores - new_top[..., None]), axis=2))
            return (new_top, row_total)
        start_carry = (jnp.full((HQ, TILE), NEG_FILL, jnp.float32), jnp.zeros((HQ, TILE), jnp.float32))
        row_top, row_total = lax.fori_loop(first_tile, tile_pos + 1, first_pass, start_carry)
        log_norm = row_top + jnp.log(row_total)

        def second_pass(key_pos, attended):
            scores, kv_tile = scores_at(key_pos)
            probs_low = narrow_keep(jnp.exp(scores - log_norm[..., None]))
            return attended + jnp.einsum('hqk,kd->hqd', probs_low, kv_tile[:, DH:])
        attended = lax.fori_loop(first_tile, tile_pos + 1, second_pass, jnp.zeros((HQ, TILE, DH), jnp.float32))
        delta = jnp.einsum('qhd,hqd->hq', g_wide, attended)

        def third_pass(key_pos, carry):
            grad_q, cache_acc = carry
            scores, kv_tile = scores_at(key_pos)
            probs = jnp.exp(scores - log_norm[..., None])
            probs_low = narrow_keep(probs)
            dprobs = jnp.einsum('qhd,kd->hqk', g_wide, kv_tile[:, DH:])
            dscore = narrow_keep(probs * (dprobs - delta[..., None]))
            grad_q = grad_q + jnp.einsum('hqk,kd->qhd', dscore, kv_tile[:, :DH])
            grad_key = jnp.einsum('hqk,qhd->kd', dscore, q_wide)
            grad_value = jnp.einsum('hqk,qhd->kd', probs_low, g_wide)
            previous = lax.dynamic_index_in_dim(cache_acc, key_pos, 0, keepdims=False)
            updated = previous + jnp.concatenate([grad_key, grad_value], axis=1)
            cache_acc = lax.dynamic_update_index_in_dim(cache_acc, updated, key_pos, 0)
            return (grad_q, cache_acc)
        start_grad = (jnp.zeros((TILE, HQ, DH), jnp.float32), grad_cache)
        grad_q, grad_cache = lax.fori_loop(first_tile, tile_pos + 1, third_pass, start_grad)
        grad_q_low = (grad_q * scale).astype(jnp.bfloat16).reshape(TILE, HQ * DH)
        return (grad_cache, grad_q_low)
    grad_cache = jnp.zeros((tile_count, TILE, 2 * DH), jnp.float32)
    tile_positions = jnp.arange(tile_count, dtype=jnp.int32)
    grad_cache, grad_q_all = lax.scan(per_tile, grad_cache, (query_tiles, grad_tiles, tile_positions))
    grad_queries = grad_q_all.reshape(TOKENS, HQ * DH)
    grad_kv = jnp.concatenate([grad_cache[..., :DH] * scale, grad_cache[..., DH:]], axis=2)
    grad_kv = grad_kv.astype(jnp.bfloat16).reshape(TOKENS, 2 * DH)
    return (grad_queries, grad_kv)
```

```python
import math

import jax
import jax.numpy as jnp
from jax import lax
from jax.experimental import pallas as pl
from jax.experimental.pallas import tpu as pltpu
from jax.sharding import PartitionSpec as P

DH = 128
TILE = 512
MAXT = 12
NEG_FILL = -1e30
F32 = jnp.float32
BF16 = jnp.bfloat16


def to_bf16(x):
    return x.astype(BF16)


def first_tile_of(doc_ref, doc_count, tile):
    def step(d, carry):
        begin, found = carry
        found = jnp.where(begin <= tile, begin, found)
        return (begin + doc_ref[d], found)

    return lax.fori_loop(0, doc_count, step, (jnp.int32(0), jnp.int32(0)))[1]


def local_kernel(
    doc_ref, q_ref, g_ref, a_ref, b_ref, ca_ref, cb_ref,
    dq_ref, keep_ref, send_ref,
    win, kt, scores, dprobs, acc, dqt, sems,
    *, local_tiles, reach, scale,
):
    slots = (reach + 1) * local_tiles
    c = lax.axis_index("ctx")
    g = lax.axis_index("grp")
    base = (c - reach) * local_tiles
    log2e = math.log2(math.e)
    to_log2 = scale * log2e

    pieces = ((a_ref, g), (b_ref, g ^ 2), (ca_ref, g ^ 1), (cb_ref, g ^ 3))
    copies = []
    for i, (ref, owner) in enumerate(pieces):
        for b in range(reach + 1):
            copies.append(
                pltpu.make_async_copy(ref.at[b], win.at[b * local_tiles + owner], sems.at[i, b])
            )
    for copy in copies:
        copy.start()
    acc[...] = jnp.zeros_like(acc)
    for copy in copies:
        copy.wait()

    doc_count = doc_ref.shape[0]
    low = first_tile_of(doc_ref, doc_count, c * local_tiles) - base

    @pl.loop(low, slots)
    def _(j):
        kt[j] = win[j, :, :DH].T

    causal = lax.broadcasted_iota(jnp.int32, (TILE, TILE), 0) <= lax.broadcasted_iota(
        jnp.int32, (TILE, TILE), 1
    )

    @pl.loop(0, local_tiles)
    def _(t):
        rows = pl.ds(pl.multiple_of(t * TILE, TILE), TILE)
        q = q_ref[rows, :]
        go = g_ref[rows, :]
        qt = q.T
        gt = go.T
        diag = reach * local_tiles + t
        first = first_tile_of(doc_ref, doc_count, c * local_tiles + t) - base

        def raw_scores(j):
            return jnp.dot(win[j, :, :DH], qt, preferred_element_type=F32) * to_log2

        def score_pass(j, top):
            s = raw_scores(j)
            scores[j - first] = s
            return jnp.maximum(top, jnp.max(s.reshape(TILE // 8, 8, TILE), axis=0))

        top = lax.fori_loop(first, diag, score_pass, jnp.full((8, TILE), NEG_FILL, F32))
        s = jnp.where(causal, raw_scores(diag), NEG_FILL)
        scores[diag - first] = s
        top = jnp.maximum(top, jnp.max(s.reshape(TILE // 8, 8, TILE), axis=0))
        top = jnp.max(top, axis=0, keepdims=True)

        def prob_pass(j, carry):
            total, dsum = carry
            p = jnp.exp2(scores[j - first] - top)
            scores[j - first] = p
            dp = jnp.dot(win[j, :, DH:], gt, preferred_element_type=F32)
            dprobs[j - first] = dp
            total = total + jnp.sum(p.reshape(TILE // 8, 8, TILE), axis=0)
            dsum = dsum + jnp.sum((p * dp).reshape(TILE // 8, 8, TILE), axis=0)
            return (total, dsum)

        zero = jnp.zeros((8, TILE), F32)
        total, dsum = lax.fori_loop(first, diag + 1, prob_pass, (zero, zero))
        inv = 1.0 / jnp.sum(total, axis=0, keepdims=True)
        delta = jnp.sum(dsum, axis=0, keepdims=True) * inv
        dqt[...] = jnp.zeros_like(dqt)

        @pl.loop(first, diag + 1)
        def _(j):
            p = scores[j - first] * inv
            ds = to_bf16(p * (dprobs[j - first] - delta))
            acc[j, :, DH:] += jnp.dot(to_bf16(p), go, preferred_element_type=F32)
            acc[j, :, :DH] += jnp.dot(ds, q, preferred_element_type=F32)
            dqt[...] += jnp.dot(kt[j], ds, preferred_element_type=F32)

        dq_ref[rows, :] = to_bf16((dqt[...] * scale).T)

    core = g & 1

    @pl.loop(0, slots // 2)
    def _(i):
        keep_ref[i] = to_bf16(acc[2 * i + core])
        send_ref[i] = to_bf16(acc[2 * i + 1 - core])


def along_ctx(x, by):
    n = lax.axis_size("ctx")
    return lax.ppermute(x, "ctx", [(i, i + by) for i in range(n) if 0 <= i + by < n])


def swap_grp(x, bit):
    n = lax.axis_size("grp")
    return lax.ppermute(x, "grp", [(i, i ^ bit) for i in range(n)])


def shards(queries, kv_cache, grad_out, doc_tiles):
    local_tiles = queries.shape[0] // TILE
    reach = (MAXT - 2) // local_tiles + 1
    slots = (reach + 1) * local_tiles
    scale = 1.0 / math.sqrt(DH)
    width = 2 * DH

    a = jnp.stack([along_ctx(kv_cache, d) for d in range(reach, 0, -1)] + [kv_cache])
    b = swap_grp(a, 2)
    ca = swap_grp(a, 1)
    cb = swap_grp(b, 1)

    vmem = pl.BlockSpec(memory_space=pltpu.VMEM)
    hbm = pl.BlockSpec(memory_space=pl.ANY)
    grad_queries, keep, send = pl.pallas_call(
        lambda *refs: local_kernel(*refs, local_tiles=local_tiles, reach=reach, scale=scale),
        out_shape=(
            jax.ShapeDtypeStruct(queries.shape, BF16),
            jax.ShapeDtypeStruct((slots // 2, TILE, width), BF16),
            jax.ShapeDtypeStruct((slots // 2, TILE, width), BF16),
        ),
        in_specs=[pl.BlockSpec(memory_space=pltpu.SMEM), vmem, vmem, hbm, hbm, hbm, hbm],
        out_specs=(vmem, vmem, vmem),
        scratch_shapes=[
            pltpu.VMEM((slots, TILE, width), BF16),
            pltpu.VMEM((slots, DH, TILE), BF16),
            pltpu.VMEM((MAXT, TILE, TILE), F32),
            pltpu.VMEM((MAXT, TILE, TILE), F32),
            pltpu.VMEM((slots, TILE, width), F32),
            pltpu.VMEM((DH, TILE), F32),
            pltpu.SemaphoreType.DMA((4, reach + 1)),
        ],
        compiler_params=pltpu.CompilerParams(vmem_limit_bytes=56 * 1024 * 1024),
    )(doc_tiles, queries, grad_out, a, b, ca, cb)

    half = lax.axis_index("grp") // 2
    pair = keep.astype(F32) + swap_grp(send, 1).astype(F32)
    pair = pair.reshape(reach + 1, local_tiles // 2, TILE, width)
    mine = lax.dynamic_index_in_dim(pair, half, 1, keepdims=False)
    theirs = lax.dynamic_index_in_dim(pair, 1 - half, 1, keepdims=False)
    group = mine + swap_grp(to_bf16(theirs), 2).astype(F32)
    own = group[reach]
    low = to_bf16(group[:reach])
    for d in range(1, reach + 1):
        own = own + along_ctx(low[reach - d], -d).astype(F32)
    grad_kv = to_bf16(jnp.concatenate([own[:, :DH] * scale, own[:, DH:]], axis=1))
    return (grad_queries, grad_kv)


def solution(mesh):
    placed = (P("ctx", "grp"), P(("ctx", "grp"), None), P("ctx", "grp"), P())
    return jax.shard_map(
        shards,
        mesh=mesh,
        in_specs=placed,
        out_specs=(P("ctx", "grp"), P(("ctx", "grp"), None)),
        check_vma=False,
    )
```

```python
import math

import jax
import jax.numpy as jnp
from jax import lax
from jax.experimental import pallas as pl
from jax.experimental.pallas import tpu as pltpu
from jax.sharding import PartitionSpec as P

DH = 128
TILE = 512
MAXT = 12
NEG_FILL = -1e30
F32 = jnp.float32
BF16 = jnp.bfloat16


def to_bf16(x):
    return x.astype(BF16)


def fold_rows(x):
    return x.reshape(x.shape[0] // 8, 8, x.shape[1])


def first_tile_of(doc_ref, doc_count, tile):
    def step(d, carry):
        begin, found = carry
        found = jnp.where(begin <= tile, begin, found)
        return (begin + doc_ref[d], found)

    return lax.fori_loop(0, doc_count, step, (jnp.int32(0), jnp.int32(0)))[1]


def local_kernel(*refs, local_tiles, reach, scale):
    blocks = reach + 1
    doc_ref, q_ref, g_ref = refs[:3]
    piece_refs = refs[3 : 3 + 4 * blocks]
    dq_ref = refs[3 + 4 * blocks]
    out_refs = refs[4 + 4 * blocks : 4 + 6 * blocks]
    win, kt, scores, dprobs, tops, probs_low, ds_low, acc, dqt, sems = refs[4 + 6 * blocks :]

    slots = blocks * local_tiles
    c = lax.axis_index("ctx")
    g = lax.axis_index("grp")
    base = (c - reach) * local_tiles
    to_log2 = scale * math.log2(math.e)

    copies = []
    for b in range(blocks):
        for i in range(4):
            copies.append(
                pltpu.make_async_copy(
                    piece_refs[4 * b + i], win.at[b * local_tiles + (g ^ i)], sems.at[b, i]
                )
            )
    for copy in copies:
        copy.start()
    acc[...] = jnp.zeros_like(acc)
    for copy in copies:
        copy.wait()

    doc_count = doc_ref.shape[0]
    low = first_tile_of(doc_ref, doc_count, c * local_tiles) - base

    @pl.loop(low, slots)
    def _(j):
        kt[j] = win[j, :, :DH].T

    causal = lax.broadcasted_iota(jnp.int32, (TILE, TILE), 0) <= lax.broadcasted_iota(
        jnp.int32, (TILE, TILE), 1
    )

    @pl.loop(0, local_tiles)
    def _(t):
        rows = pl.ds(pl.multiple_of(t * TILE, TILE), TILE)
        q = q_ref[rows, :]
        go = g_ref[rows, :]
        qt = q.T
        gt = go.T
        diag = reach * local_tiles + t
        first = first_tile_of(doc_ref, doc_count, c * local_tiles + t) - base

        def make_scores(j, top, mask=None):
            s = jnp.dot(win[j, :, :DH], qt, preferred_element_type=F32) * to_log2
            if mask is not None:
                s = jnp.where(mask, s, NEG_FILL)
            scores[j - first] = s
            top = jnp.maximum(top, jnp.max(fold_rows(s), axis=0))
            tops[j - first] = top
            dprobs[j - first] = jnp.dot(win[j, :, DH:], gt, preferred_element_type=F32)
            return top

        def make_probs(j, older, newer, total, dsum):
            p = jnp.exp2(fold_rows(scores[j - first]) - newer[None])
            scores[j - first] = p.reshape(TILE, TILE)
            fade = jnp.exp2(older - newer)
            total = total * fade + jnp.sum(p, axis=0)
            dsum = dsum * fade + jnp.sum(p * fold_rows(dprobs[j - first]), axis=0)
            return total, dsum

        def forward_step(j, carry):
            last, older, newer, total, dsum = carry
            newest = make_scores(j, newer)
            total, dsum = make_probs(last, older, newer, total, dsum)
            return (j, newer, newest, total, dsum)

        zero = jnp.zeros((8, TILE), F32)
        floor = jnp.full((8, TILE), NEG_FILL, F32)
        carry = (diag, floor, make_scores(diag, floor, causal), zero, zero)
        last, older, newer, total, dsum = lax.fori_loop(first, diag, forward_step, carry)
        total, dsum = make_probs(last, older, newer, total, dsum)

        peak = jnp.max(newer, axis=0, keepdims=True)
        fade = jnp.exp2(newer - peak)
        inv = 1.0 / jnp.sum(total * fade, axis=0, keepdims=True)
        delta = jnp.sum(dsum * fade, axis=0, keepdims=True) * inv
        dqt[...] = jnp.zeros_like(dqt)

        def make_dscore(j, slot):
            factor = jnp.exp2(tops[j - first] - peak) * inv
            p = (fold_rows(scores[j - first]) * factor[None]).reshape(TILE, TILE)
            probs_low[slot] = to_bf16(p)
            ds_low[slot] = to_bf16(p * (dprobs[j - first] - delta))

        def make_grads(j, slot):
            ds = ds_low[slot]
            acc[j, :, DH:] += jnp.dot(probs_low[slot], go, preferred_element_type=F32)
            acc[j, :, :DH] += jnp.dot(ds, q, preferred_element_type=F32)
            dqt[...] += jnp.dot(kt[j], ds, preferred_element_type=F32)

        def backward_step(j, carry):
            last, slot = carry
            make_dscore(j, 1 - slot)
            make_grads(last, slot)
            return (j, 1 - slot)

        make_dscore(diag, 0)
        last, slot = lax.fori_loop(first, diag, backward_step, (diag, jnp.int32(0)))
        make_grads(last, slot)
        dq_ref[rows, :] = to_bf16((dqt[...] * scale).T)

    for b in range(blocks):
        for i in range(2):
            out_refs[2 * b][i] = to_bf16(acc[b * local_tiles + (g ^ (2 * i))])
            out_refs[2 * b + 1][i] = to_bf16(acc[b * local_tiles + (g ^ (2 * i + 1))])


def along_ctx(x, by):
    n = lax.axis_size("ctx")
    return lax.ppermute(x, "ctx", [(i, i + by) for i in range(n) if 0 <= i + by < n])


def swap_grp(x, bit):
    n = lax.axis_size("grp")
    return lax.ppermute(x, "grp", [(i, i ^ bit) for i in range(n)])


def shards(queries, kv_cache, grad_out, doc_tiles):
    local_tiles = queries.shape[0] // TILE
    reach = (MAXT - 2) // local_tiles + 1
    blocks = reach + 1
    slots = blocks * local_tiles
    scale = 1.0 / math.sqrt(DH)
    width = 2 * DH

    pieces = []
    for d in range(reach, -1, -1):
        x = along_ctx(kv_cache, d) if d else kv_cache
        y = swap_grp(x, 2)
        pieces += [x, swap_grp(x, 1), y, swap_grp(y, 1)]

    vmem = pl.BlockSpec(memory_space=pltpu.VMEM)
    hbm = pl.BlockSpec(memory_space=pl.ANY)
    half = jax.ShapeDtypeStruct((local_tiles // 2, TILE, width), BF16)
    grad_queries, *halves = pl.pallas_call(
        lambda *refs: local_kernel(*refs, local_tiles=local_tiles, reach=reach, scale=scale),
        out_shape=(jax.ShapeDtypeStruct(queries.shape, BF16),) + (half,) * (2 * blocks),
        in_specs=[pl.BlockSpec(memory_space=pltpu.SMEM), vmem, vmem] + [hbm] * (4 * blocks),
        out_specs=(vmem,) * (1 + 2 * blocks),
        scratch_shapes=[
            pltpu.VMEM((slots, TILE, width), BF16),
            pltpu.VMEM((slots, DH, TILE), BF16),
            pltpu.VMEM((MAXT, TILE, TILE), F32),
            pltpu.VMEM((MAXT, TILE, TILE), F32),
            pltpu.VMEM((MAXT, 8, TILE), F32),
            pltpu.VMEM((2, TILE, TILE), BF16),
            pltpu.VMEM((2, TILE, TILE), BF16),
            pltpu.VMEM((slots, TILE, width), F32),
            pltpu.VMEM((DH, TILE), F32),
            pltpu.SemaphoreType.DMA((blocks, 4)),
        ],
        compiler_params=pltpu.CompilerParams(vmem_limit_bytes=56 * 1024 * 1024),
    )(doc_tiles, queries, grad_out, *pieces)

    own = None
    for d in range(reach, -1, -1):
        keep, send = halves[2 * (reach - d)], halves[2 * (reach - d) + 1]
        got = swap_grp(send, 1).astype(F32)
        theirs = to_bf16(keep[1].astype(F32) + got[1])
        mine = keep[0].astype(F32) + got[0] + swap_grp(theirs, 2).astype(F32)
        if d:
            mine = along_ctx(to_bf16(mine), -d).astype(F32)
        own = mine if own is None else own + mine
    grad_kv = to_bf16(jnp.concatenate([own[:, :DH] * scale, own[:, DH:]], axis=1))
    return (grad_queries, grad_kv)


def solution(mesh):
    placed = (P("ctx", "grp"), P(("ctx", "grp"), None), P("ctx", "grp"), P())
    return jax.shard_map(
        shards,
        mesh=mesh,
        in_specs=placed,
        out_specs=(P("ctx", "grp"), P(("ctx", "grp"), None)),
        check_vma=False,
    )
```

```python
import math

import jax
import jax.numpy as jnp
from jax import lax
from jax.experimental import pallas as pl
from jax.experimental.pallas import tpu as pltpu
from jax.sharding import PartitionSpec as P

DH = 128
TILE = 512
MAXT = 12
NEG_FILL = -1e30
HUGE = 2.0**100
F32 = jnp.float32
BF16 = jnp.bfloat16


def to_bf16(x):
    return x.astype(BF16)


def fold_rows(x):
    return x.reshape(x.shape[0] // 8, 8, x.shape[1])


def first_tile_of(doc_ref, doc_count, tile):
    def step(d, carry):
        begin, found = carry
        found = jnp.where(begin <= tile, begin, found)
        return (begin + doc_ref[d], found)

    return lax.fori_loop(0, doc_count, step, (jnp.int32(0), jnp.int32(0)))[1]


def local_kernel(*refs, local_tiles, reach, scale):
    blocks = reach + 1
    doc_ref, q_hbm, g_hbm = refs[:3]
    piece_refs = refs[3 : 3 + 4 * blocks]
    dq_hbm = refs[3 + 4 * blocks]
    out_refs = refs[4 + 4 * blocks : 4 + 6 * blocks]
    q_ref, g_ref, dq_ref, win, kt, scores, dprobs, acc, dqt, sems, io_sems = refs[4 + 6 * blocks :]

    slots = blocks * local_tiles
    c = lax.axis_index("ctx")
    g = lax.axis_index("grp")
    base = (c - reach) * local_tiles
    to_log2 = scale * math.log2(math.e)

    def tile_rows(b, owner):
        return pl.ds(pl.multiple_of((b * local_tiles + owner) * TILE, TILE), TILE)

    copies = [
        pltpu.make_async_copy(q_hbm, q_ref, io_sems.at[0]),
        pltpu.make_async_copy(g_hbm, g_ref, io_sems.at[1]),
    ]
    for b in range(blocks):
        for i in range(4):
            copies.append(
                pltpu.make_async_copy(
                    piece_refs[4 * b + i], win.at[tile_rows(b, g ^ i)], sems.at[b, i]
                )
            )
    for copy in copies:
        copy.start()
    acc[...] = jnp.zeros_like(acc)
    for copy in copies:
        copy.wait()

    doc_count = doc_ref.shape[0]
    low = first_tile_of(doc_ref, doc_count, c * local_tiles) - base

    @pl.loop(low, slots)
    def _(j):
        kt[j] = win[pl.ds(pl.multiple_of(j * TILE, TILE), TILE), :DH].T

    half = TILE // 2
    causal = lax.broadcasted_iota(jnp.int32, (half, half), 0) <= lax.broadcasted_iota(
        jnp.int32, (half, half), 1
    )

    def widen_lanes(x):
        return jnp.concatenate([jnp.zeros_like(x), x], axis=1)

    @pl.loop(0, local_tiles)
    def _(t):
        rows = pl.ds(pl.multiple_of(t * TILE, TILE), TILE)
        q = q_ref[rows, :]
        go = g_ref[rows, :]
        qt = q.T
        gt = go.T
        diag = reach * local_tiles + t
        first = first_tile_of(doc_ref, doc_count, c * local_tiles + t) - base

        def key_rows(j, count):
            return pl.ds(pl.multiple_of(j * TILE, TILE), count * TILE)

        def in_steps(step, carry):
            doubles = (diag - first) // 2
            carry = lax.fori_loop(
                0, doubles, lambda i, x: step(first + 2 * i, 2, x), carry
            )
            return lax.fori_loop(first + 2 * doubles, diag, lambda j, x: step(j, 1, x), carry)

        def raw_scores(at, queries_t):
            return jnp.dot(win[at, :DH], queries_t, preferred_element_type=F32) * to_log2

        upper = pl.ds(pl.multiple_of(diag * TILE, half), half)
        lower = pl.ds(pl.multiple_of(diag * TILE + half, half), half)
        slot = diag - first
        upper_to = pl.ds(pl.multiple_of(slot * TILE, half), half)
        lower_to = pl.ds(pl.multiple_of(slot * TILE + half, half), half)

        def diag_scores():
            s0 = raw_scores(upper, qt)
            s0 = jnp.concatenate(
                [jnp.where(causal, s0[:, :half], NEG_FILL), s0[:, half:]], axis=1
            )
            s1 = jnp.where(causal, raw_scores(lower, qt[:, half:]), NEG_FILL)
            return s0, s1

        def sums_of(p, dp):
            return jnp.sum(fold_rows(p), axis=0), jnp.sum(fold_rows(p * dp), axis=0)

        def forward(ref, s0, s1):
            def step(j, count, carry):
                total, dsum = carry
                at = key_rows(j, count)
                to = key_rows(j - first, count)
                p = jnp.exp2(raw_scores(at, qt) - ref)
                scores[to, :] = p
                dp = jnp.dot(win[at, DH:], gt, preferred_element_type=F32)
                dprobs[to, :] = dp
                more, dmore = sums_of(p, dp)
                return (total + more, dsum + dmore)

            p0 = jnp.exp2(s0 - ref)
            p1 = jnp.exp2(s1 - ref[:, half:])
            dp0 = jnp.dot(win[upper, DH:], gt, preferred_element_type=F32)
            dp1 = jnp.dot(win[lower, DH:], gt[:, half:], preferred_element_type=F32)
            scores[upper_to, :] = p0
            scores[lower_to, half:] = p1
            dprobs[upper_to, :] = dp0
            dprobs[lower_to, half:] = dp1
            total0, dsum0 = sums_of(p0, dp0)
            total1, dsum1 = sums_of(p1, dp1)
            total, dsum = in_steps(
                step, (total0 + widen_lanes(total1), dsum0 + widen_lanes(dsum1))
            )
            return jnp.sum(total, axis=0, keepdims=True), jnp.sum(dsum, axis=0, keepdims=True)

        def diag_top(s0, s1):
            top0 = jnp.max(s0, axis=0, keepdims=True)
            top1 = jnp.max(s1, axis=0, keepdims=True)
            return jnp.concatenate(
                [top0[:, :half], jnp.maximum(top0[:, half:], top1)], axis=1
            )

        def exact():
            def step(j, count, top):
                s = raw_scores(key_rows(j, count), qt)
                return jnp.maximum(top, jnp.max(s, axis=0, keepdims=True))

            s0, s1 = diag_scores()
            return forward(in_steps(step, diag_top(s0, s1)), s0, s1)

        s0, s1 = diag_scores()
        total, dsum = forward(diag_top(s0, s1), s0, s1)
        fits = jnp.max(jnp.where(total < HUGE, 0.0, 1.0)) == 0.0
        total, dsum = lax.cond(fits, lambda: (total, dsum), exact)

        inv = 1.0 / total
        delta = dsum * inv
        dqt[...] = jnp.zeros_like(dqt)

        def grads(p, dp, inv, delta):
            p = p * inv
            return to_bf16(p), to_bf16(p * (dp - delta))

        def add_grads(at, low, ds, q, go):
            acc[at, DH:] += jnp.dot(low, go, preferred_element_type=F32)
            acc[at, :DH] += jnp.dot(ds, q, preferred_element_type=F32)

        def backward(j, count, carry):
            at = key_rows(j, count)
            to = key_rows(j - first, count)
            low, ds = grads(scores[to, :], dprobs[to, :], inv, delta)
            add_grads(at, low, ds, q, go)
            part = dqt[...]
            for i in range(count):
                part += jnp.dot(
                    kt[j + i], ds[i * TILE : (i + 1) * TILE], preferred_element_type=F32
                )
            dqt[...] = part
            return carry

        low0, ds0 = grads(scores[upper_to, :], dprobs[upper_to, :], inv, delta)
        low1, ds1 = grads(
            scores[lower_to, half:], dprobs[lower_to, half:], inv[:, half:], delta[:, half:]
        )
        add_grads(upper, low0, ds0, q, go)
        add_grads(lower, low1, ds1, q[half:], go[half:])
        dqt[...] = jnp.dot(kt[diag, :, :half], ds0, preferred_element_type=F32)
        dqt[:, half:] += jnp.dot(kt[diag, :, half:], ds1, preferred_element_type=F32)
        in_steps(backward, jnp.int32(0))
        dq_ref[rows, :] = to_bf16((dqt[...] * scale).T)

    copies = [pltpu.make_async_copy(dq_ref, dq_hbm, io_sems.at[0])]
    copies[0].start()
    for b in range(blocks):
        for i in range(4):
            at = tile_rows(b, g ^ i)
            win[at, :] = to_bf16(acc[at, :])
            copy = pltpu.make_async_copy(
                win.at[at], out_refs[2 * b + i % 2].at[i // 2], sems.at[b, i]
            )
            copy.start()
            copies.append(copy)
    for copy in copies:
        copy.wait()


def along_ctx(x, by):
    n = lax.axis_size("ctx")
    return lax.ppermute(x, "ctx", [(i, i + by) for i in range(n) if 0 <= i + by < n])


def swap_grp(x, bit):
    n = lax.axis_size("grp")
    return lax.ppermute(x, "grp", [(i, i ^ bit) for i in range(n)])


def shards(queries, kv_cache, grad_out, doc_tiles):
    local_tiles = queries.shape[0] // TILE
    reach = (MAXT - 2) // local_tiles + 1
    assert reach == 3
    blocks = reach + 1
    slots = blocks * local_tiles
    scale = 1.0 / math.sqrt(DH)
    width = 2 * DH

    x0 = kv_cache
    y0 = swap_grp(x0, 2)
    x1 = along_ctx(x0, 1)
    x2 = along_ctx(x0, 2)
    x3 = along_ctx(x1, 2)
    y2 = along_ctx(y0, 2)
    y1 = swap_grp(x1, 2)
    y3 = swap_grp(x3, 2)
    pieces = []
    for x, y in ((x3, y3), (x2, y2), (x1, y1), (x0, y0)):
        pieces += [x, swap_grp(x, 1), y, swap_grp(y, 1)]

    hbm = pl.BlockSpec(memory_space=pl.ANY)
    half = jax.ShapeDtypeStruct((local_tiles // 2, TILE, width), BF16)
    grad_queries, *halves = pl.pallas_call(
        lambda *refs: local_kernel(*refs, local_tiles=local_tiles, reach=reach, scale=scale),
        out_shape=(jax.ShapeDtypeStruct(queries.shape, BF16),) + (half,) * (2 * blocks),
        in_specs=[pl.BlockSpec(memory_space=pltpu.SMEM)] + [hbm] * (2 + 4 * blocks),
        out_specs=(hbm,) * (1 + 2 * blocks),
        scratch_shapes=[
            pltpu.VMEM(queries.shape, BF16),
            pltpu.VMEM(queries.shape, BF16),
            pltpu.VMEM(queries.shape, BF16),
            pltpu.VMEM((slots * TILE, width), BF16),
            pltpu.VMEM((slots, DH, TILE), BF16),
            pltpu.VMEM((MAXT * TILE, TILE), F32),
            pltpu.VMEM((MAXT * TILE, TILE), F32),
            pltpu.VMEM((slots * TILE, width), F32),
            pltpu.VMEM((DH, TILE), F32),
            pltpu.SemaphoreType.DMA((blocks, 4)),
            pltpu.SemaphoreType.DMA((2,)),
        ],
        compiler_params=pltpu.CompilerParams(vmem_limit_bytes=56 * 1024 * 1024),
    )(doc_tiles, queries, grad_out, *pieces)

    mine, theirs = {}, {}
    for d in range(reach, -1, -1):
        keep, send = halves[2 * (reach - d)], halves[2 * (reach - d) + 1]
        got = swap_grp(send, 1)
        mine[d] = keep[0].astype(F32) + got[0].astype(F32)
        theirs[d] = keep[1].astype(F32) + got[1].astype(F32)
    far_theirs = along_ctx(to_bf16(theirs[2]), -2).astype(F32)
    far_mine = along_ctx(to_bf16(mine[2]), -2).astype(F32)
    third = mine[3] + swap_grp(to_bf16(theirs[3]), 2).astype(F32)
    third = along_ctx(to_bf16(third), -3).astype(F32)
    near = mine[1] + swap_grp(to_bf16(theirs[1]), 2).astype(F32)
    near = along_ctx(to_bf16(near), -1).astype(F32)
    own = mine[0] + swap_grp(to_bf16(theirs[0] + far_theirs), 2).astype(F32)
    own = own + far_mine + third + near
    grad_kv = to_bf16(jnp.concatenate([own[:, :DH] * scale, own[:, DH:]], axis=1))
    return (grad_queries, grad_kv)


def solution(mesh):
    placed = (P("ctx", "grp"), P(("ctx", "grp"), None), P("ctx", "grp"), P())
    return jax.shard_map(
        shards,
        mesh=mesh,
        in_specs=placed,
        out_specs=(P("ctx", "grp"), P(("ctx", "grp"), None)),
        check_vma=False,
    )
```

```python
import math

import jax
import jax.numpy as jnp
from jax import lax
from jax.experimental import pallas as pl
from jax.experimental.pallas import tpu as pltpu
from jax.sharding import PartitionSpec as P

DH = 128
TILE = 512
MAXT = 12
NEG_FILL = -1e30
HUGE = 2.0**100
F32 = jnp.float32
BF16 = jnp.bfloat16


def to_bf16(x):
    return x.astype(BF16)


def fold_rows(x):
    return x.reshape(x.shape[0] // 8, 8, x.shape[1])


def first_tile_of(doc_ref, doc_count, tile):
    def step(d, carry):
        begin, found = carry
        found = jnp.where(begin <= tile, begin, found)
        return (begin + doc_ref[d], found)

    return lax.fori_loop(0, doc_count, step, (jnp.int32(0), jnp.int32(0)))[1]


def local_kernel(*refs, local_tiles, reach, scale):
    blocks = reach + 1
    doc_ref, q_hbm, g_hbm = refs[:3]
    piece_refs = refs[3 : 3 + 4 * blocks]
    dq_hbm = refs[3 + 4 * blocks]
    out_refs = refs[4 + 4 * blocks : 4 + 6 * blocks]
    q_ref, g_ref, dq_ref, win, kt, scores, dprobs, acc, dqt, sems, io_sems = refs[4 + 6 * blocks :]

    slots = blocks * local_tiles
    c = lax.axis_index("ctx")
    g = lax.axis_index("grp")
    base = (c - reach) * local_tiles
    to_log2 = scale * math.log2(math.e)

    def tile_rows(b, owner):
        return pl.ds(pl.multiple_of((b * local_tiles + owner) * TILE, TILE), TILE)

    copies = [
        pltpu.make_async_copy(q_hbm, q_ref, io_sems.at[0]),
        pltpu.make_async_copy(g_hbm, g_ref, io_sems.at[1]),
    ]
    for b in range(blocks):
        for i in range(4):
            copies.append(
                pltpu.make_async_copy(
                    piece_refs[4 * b + i], win.at[tile_rows(b, g ^ i)], sems.at[b, i]
                )
            )
    for copy in copies:
        copy.start()
    acc[...] = jnp.zeros_like(acc)
    for copy in copies:
        copy.wait()

    doc_count = doc_ref.shape[0]
    low = first_tile_of(doc_ref, doc_count, c * local_tiles) - base

    @pl.loop(low, slots)
    def _(j):
        kt[j] = win[pl.ds(pl.multiple_of(j * TILE, TILE), TILE), :DH].T

    half = TILE // 2
    causal = lax.broadcasted_iota(jnp.int32, (half, half), 0) <= lax.broadcasted_iota(
        jnp.int32, (half, half), 1
    )

    def widen_lanes(x):
        return jnp.concatenate([jnp.zeros_like(x), x], axis=1)

    @pl.loop(0, local_tiles)
    def _(t):
        rows = pl.ds(pl.multiple_of(t * TILE, TILE), TILE)
        q = q_ref[rows, :]
        go = g_ref[rows, :]
        qt = q.T
        gt = go.T
        diag = reach * local_tiles + t
        first = first_tile_of(doc_ref, doc_count, c * local_tiles + t) - base

        def key_rows(j, count):
            return pl.ds(pl.multiple_of(j * TILE, TILE), count * TILE)

        def in_steps(step, carry):
            doubles = (diag - first) // 2
            carry = lax.fori_loop(
                0, doubles, lambda i, x: step(first + 2 * i, 2, x), carry
            )
            return lax.fori_loop(first + 2 * doubles, diag, lambda j, x: step(j, 1, x), carry)

        def raw_scores(at, queries_t):
            return jnp.dot(win[at, :DH], queries_t, preferred_element_type=F32) * to_log2

        upper = pl.ds(pl.multiple_of(diag * TILE, half), half)
        lower = pl.ds(pl.multiple_of(diag * TILE + half, half), half)
        slot = diag - first
        upper_to = pl.ds(pl.multiple_of(slot * TILE, half), half)
        lower_to = pl.ds(pl.multiple_of(slot * TILE + half, half), half)

        def diag_scores():
            s0 = raw_scores(upper, qt)
            s0 = jnp.concatenate(
                [jnp.where(causal, s0[:, :half], NEG_FILL), s0[:, half:]], axis=1
            )
            s1 = jnp.where(causal, raw_scores(lower, qt[:, half:]), NEG_FILL)
            return s0, s1

        def sums_of(p, dp):
            return jnp.sum(fold_rows(p), axis=0), jnp.sum(fold_rows(p * dp), axis=0)

        def forward(ref, s0, s1):
            def step(j, count, carry):
                total, dsum = carry
                at = key_rows(j, count)
                to = key_rows(j - first, count)
                p = jnp.exp2(raw_scores(at, qt) - ref)
                scores[to, :] = p
                dp = jnp.dot(win[at, DH:], gt, preferred_element_type=F32)
                dprobs[to, :] = dp
                more, dmore = sums_of(p, dp)
                return (total + more, dsum + dmore)

            p0 = jnp.exp2(s0 - ref)
            p1 = jnp.exp2(s1 - ref[:, half:])
            dp0 = jnp.dot(win[upper, DH:], gt, preferred_element_type=F32)
            dp1 = jnp.dot(win[lower, DH:], gt[:, half:], preferred_element_type=F32)
            scores[upper_to, :] = p0
            scores[lower_to, half:] = p1
            dprobs[upper_to, :] = dp0
            dprobs[lower_to, half:] = dp1
            total0, dsum0 = sums_of(p0, dp0)
            total1, dsum1 = sums_of(p1, dp1)
            total, dsum = in_steps(
                step, (total0 + widen_lanes(total1), dsum0 + widen_lanes(dsum1))
            )
            return jnp.sum(total, axis=0, keepdims=True), jnp.sum(dsum, axis=0, keepdims=True)

        def diag_top(s0, s1):
            top0 = jnp.max(s0, axis=0, keepdims=True)
            top1 = jnp.max(s1, axis=0, keepdims=True)
            return jnp.concatenate(
                [top0[:, :half], jnp.maximum(top0[:, half:], top1)], axis=1
            )

        def exact():
            def step(j, count, top):
                s = raw_scores(key_rows(j, count), qt)
                return jnp.maximum(top, jnp.max(s, axis=0, keepdims=True))

            s0, s1 = diag_scores()
            return forward(in_steps(step, diag_top(s0, s1)), s0, s1)

        s0, s1 = diag_scores()
        total, dsum = forward(diag_top(s0, s1), s0, s1)
        fits = jnp.max(jnp.where(total < HUGE, 0.0, 1.0)) == 0.0
        total, dsum = lax.cond(fits, lambda: (total, dsum), exact)

        inv = 1.0 / total
        delta = dsum * inv
        dqt[...] = jnp.zeros_like(dqt)

        def grads(p, dp, inv, delta):
            p = p * inv
            return to_bf16(p), to_bf16(p * (dp - delta))

        def add_grads(at, low, ds, q, go):
            acc[at, DH:] += jnp.dot(low, go, preferred_element_type=F32)
            acc[at, :DH] += jnp.dot(ds, q, preferred_element_type=F32)

        def backward(j, count, carry):
            at = key_rows(j, count)
            to = key_rows(j - first, count)
            low, ds = grads(scores[to, :], dprobs[to, :], inv, delta)
            add_grads(at, low, ds, q, go)
            part = dqt[...]
            for i in range(count):
                part += jnp.dot(
                    kt[j + i], ds[i * TILE : (i + 1) * TILE], preferred_element_type=F32
                )
            dqt[...] = part
            return carry

        low0, ds0 = grads(scores[upper_to, :], dprobs[upper_to, :], inv, delta)
        low1, ds1 = grads(
            scores[lower_to, half:], dprobs[lower_to, half:], inv[:, half:], delta[:, half:]
        )
        add_grads(upper, low0, ds0, q, go)
        add_grads(lower, low1, ds1, q[half:], go[half:])
        dqt[...] = jnp.dot(kt[diag, :, :half], ds0, preferred_element_type=F32)
        dqt[:, half:] += jnp.dot(kt[diag, :, half:], ds1, preferred_element_type=F32)
        in_steps(backward, jnp.int32(0))
        dq_ref[rows, :] = to_bf16((dqt[...] * scale).T)

    copies = [pltpu.make_async_copy(dq_ref, dq_hbm, io_sems.at[0])]
    copies[0].start()
    for b in range(blocks):
        for i in range(4):
            at = tile_rows(b, g ^ i)
            win[at, :] = to_bf16(acc[at, :])
            copy = pltpu.make_async_copy(
                win.at[at], out_refs[2 * b + i % 2].at[i // 2], sems.at[b, i]
            )
            copy.start()
            copies.append(copy)
    for copy in copies:
        copy.wait()


def along_ctx(x, by):
    n = lax.axis_size("ctx")
    return lax.ppermute(x, "ctx", [(i, i + by) for i in range(n) if 0 <= i + by < n])


def swap_grp(x, bit):
    n = lax.axis_size("grp")
    return lax.ppermute(x, "grp", [(i, i ^ bit) for i in range(n)])


def spans_blocks(doc_tiles, local_tiles):
    ids = jnp.arange(doc_tiles.shape[0])
    begins = jnp.sum(jnp.where(ids[None, :] < ids[:, None], doc_tiles[None, :], 0), axis=1)
    lasts = begins + doc_tiles - 1
    return jnp.max(lasts // local_tiles - begins // local_tiles)


def with_window(queries, kv_cache, grad_out, doc_tiles, *, local_tiles, reach):
    blocks = reach + 1
    slots = blocks * local_tiles
    scale = 1.0 / math.sqrt(DH)
    width = 2 * DH

    x = [kv_cache, along_ctx(kv_cache, 1), along_ctx(kv_cache, 2)]
    y = [swap_grp(kv_cache, 2)]
    y += [swap_grp(x[1], 2), along_ctx(y[0], 2)]
    if reach == 3:
        x.append(along_ctx(x[1], 2))
        y.append(swap_grp(x[3], 2))
    pieces = []
    for d in range(reach, -1, -1):
        pieces += [x[d], swap_grp(x[d], 1), y[d], swap_grp(y[d], 1)]

    hbm = pl.BlockSpec(memory_space=pl.ANY)
    half = jax.ShapeDtypeStruct((local_tiles // 2, TILE, width), BF16)
    grad_queries, *halves = pl.pallas_call(
        lambda *refs: local_kernel(*refs, local_tiles=local_tiles, reach=reach, scale=scale),
        out_shape=(jax.ShapeDtypeStruct(queries.shape, BF16),) + (half,) * (2 * blocks),
        in_specs=[pl.BlockSpec(memory_space=pltpu.SMEM)] + [hbm] * (2 + 4 * blocks),
        out_specs=(hbm,) * (1 + 2 * blocks),
        scratch_shapes=[
            pltpu.VMEM(queries.shape, BF16),
            pltpu.VMEM(queries.shape, BF16),
            pltpu.VMEM(queries.shape, BF16),
            pltpu.VMEM((slots * TILE, width), BF16),
            pltpu.VMEM((slots, DH, TILE), BF16),
            pltpu.VMEM((MAXT * TILE, TILE), F32),
            pltpu.VMEM((MAXT * TILE, TILE), F32),
            pltpu.VMEM((slots * TILE, width), F32),
            pltpu.VMEM((DH, TILE), F32),
            pltpu.SemaphoreType.DMA((blocks, 4)),
            pltpu.SemaphoreType.DMA((2,)),
        ],
        compiler_params=pltpu.CompilerParams(vmem_limit_bytes=56 * 1024 * 1024),
    )(doc_tiles, queries, grad_out, *pieces)

    own = None
    for d in range(reach, -1, -1):
        keep, send = halves[2 * (reach - d)], halves[2 * (reach - d) + 1]
        got = swap_grp(send, 1).astype(F32)
        theirs = to_bf16(keep[1].astype(F32) + got[1])
        mine = keep[0].astype(F32) + got[0] + swap_grp(theirs, 2).astype(F32)
        if d:
            mine = along_ctx(to_bf16(mine), -d).astype(F32)
        own = mine if own is None else own + mine
    grad_kv = to_bf16(jnp.concatenate([own[:, :DH] * scale, own[:, DH:]], axis=1))
    return (grad_queries, grad_kv)


def shards(queries, kv_cache, grad_out, doc_tiles):
    local_tiles = queries.shape[0] // TILE
    most = (MAXT - 2) // local_tiles + 1
    assert most == 3
    return lax.cond(
        spans_blocks(doc_tiles, local_tiles) >= most,
        lambda *args: with_window(*args, local_tiles=local_tiles, reach=most),
        lambda *args: with_window(*args, local_tiles=local_tiles, reach=most - 1),
        queries, kv_cache, grad_out, doc_tiles,
    )


def solution(mesh):
    placed = (P("ctx", "grp"), P(("ctx", "grp"), None), P("ctx", "grp"), P())
    return jax.shard_map(
        shards,
        mesh=mesh,
        in_specs=placed,
        out_specs=(P("ctx", "grp"), P(("ctx", "grp"), None)),
        check_vma=False,
    )
```

```python
import math

import jax
import jax.numpy as jnp
from jax import lax
from jax.experimental import pallas as pl
from jax.experimental.pallas import tpu as pltpu
from jax.sharding import PartitionSpec as P

DH = 128
TILE = 512
MAXT = 12
NEG_FILL = -1e30
HUGE = 2.0**100
F32 = jnp.float32
BF16 = jnp.bfloat16


def dot_nt(a, b):
    return lax.dot_general(a, b, (((1,), (1,)), ((), ())), preferred_element_type=F32)


def to_bf16(x):
    return x.astype(BF16)


def fold_rows(x):
    return x.reshape(x.shape[0] // 8, 8, x.shape[1])


def first_tile_of(doc_ref, doc_count, tile):
    def step(d, carry):
        begin, found = carry
        found = jnp.where(begin <= tile, begin, found)
        return (begin + doc_ref[d], found)

    return lax.fori_loop(0, doc_count, step, (jnp.int32(0), jnp.int32(0)))[1]


def local_kernel(*refs, local_tiles, reach, scale):
    blocks = reach + 1
    doc_ref, q_hbm, g_hbm = refs[:3]
    piece_refs = refs[3 : 3 + 4 * blocks]
    dq_hbm = refs[3 + 4 * blocks]
    out_refs = refs[4 + 4 * blocks : 4 + 6 * blocks]
    q_ref, g_ref, dq_ref, win, kt, scores, dprobs, acc, out, dqt, sems, io_sems = refs[4 + 6 * blocks :]

    slots = blocks * local_tiles
    c = lax.axis_index("ctx")
    g = lax.axis_index("grp")
    base = (c - reach) * local_tiles
    to_log2 = scale * math.log2(math.e)

    def tile_rows(b, owner):
        return pl.ds(pl.multiple_of((b * local_tiles + owner) * TILE, TILE), TILE)

    copies = [
        pltpu.make_async_copy(q_hbm, q_ref, io_sems.at[0]),
        pltpu.make_async_copy(g_hbm, g_ref, io_sems.at[1]),
    ]
    for b in range(blocks):
        for i in range(4):
            copies.append(
                pltpu.make_async_copy(
                    piece_refs[4 * b + i], win.at[tile_rows(b, g ^ i)], sems.at[b, i]
                )
            )
    for copy in copies:
        copy.start()
    acc[...] = jnp.zeros_like(acc)
    for copy in copies:
        copy.wait()

    doc_count = doc_ref.shape[0]
    low = first_tile_of(doc_ref, doc_count, c * local_tiles) - base

    @pl.loop(low, slots)
    def _(j):
        kt[j] = win[pl.ds(pl.multiple_of(j * TILE, TILE), TILE), :DH].T

    half = TILE // 2
    causal = lax.broadcasted_iota(jnp.int32, (half, half), 0) <= lax.broadcasted_iota(
        jnp.int32, (half, half), 1
    )

    def widen_lanes(x):
        return jnp.concatenate([jnp.zeros_like(x), x], axis=1)

    @pl.loop(0, local_tiles)
    def _(t):
        rows = pl.ds(pl.multiple_of(t * TILE, TILE), TILE)
        qt = q_ref[rows, :].T
        gt = g_ref[rows, :].T
        diag = reach * local_tiles + t
        first = first_tile_of(doc_ref, doc_count, c * local_tiles + t) - base

        def key_rows(j, count):
            return pl.ds(pl.multiple_of(j * TILE, TILE), count * TILE)

        def in_steps(step, carry):
            doubles = (diag - first) // 2
            carry = lax.fori_loop(
                0, doubles, lambda i, x: step(first + 2 * i, 2, x), carry
            )
            return lax.fori_loop(first + 2 * doubles, diag, lambda j, x: step(j, 1, x), carry)

        def raw_scores(at, queries_t):
            return jnp.dot(win[at, :DH], queries_t, preferred_element_type=F32) * to_log2

        upper = pl.ds(pl.multiple_of(diag * TILE, half), half)
        lower = pl.ds(pl.multiple_of(diag * TILE + half, half), half)
        slot = diag - first
        upper_to = pl.ds(pl.multiple_of(slot * TILE, half), half)
        lower_to = pl.ds(pl.multiple_of(slot * TILE + half, half), half)

        def diag_scores():
            s0 = raw_scores(upper, qt)
            s0 = jnp.concatenate(
                [jnp.where(causal, s0[:, :half], NEG_FILL), s0[:, half:]], axis=1
            )
            s1 = jnp.where(causal, raw_scores(lower, qt[:, half:]), NEG_FILL)
            return s0, s1

        def sums_of(p, dp):
            return jnp.sum(fold_rows(p), axis=0), jnp.sum(fold_rows(p * dp), axis=0)

        def forward(ref, s0, s1):
            def step(j, count, carry):
                total, dsum = carry
                at = key_rows(j, count)
                to = key_rows(j - first, count)
                p = jnp.exp2(raw_scores(at, qt) - ref)
                scores[to, :] = p
                dp = jnp.dot(win[at, DH:], gt, preferred_element_type=F32)
                dprobs[to, :] = dp
                more, dmore = sums_of(p, dp)
                return (total + more, dsum + dmore)

            p0 = jnp.exp2(s0 - ref)
            p1 = jnp.exp2(s1 - ref[:, half:])
            dp0 = jnp.dot(win[upper, DH:], gt, preferred_element_type=F32)
            dp1 = jnp.dot(win[lower, DH:], gt[:, half:], preferred_element_type=F32)
            scores[upper_to, :] = p0
            scores[lower_to, half:] = p1
            dprobs[upper_to, :] = dp0
            dprobs[lower_to, half:] = dp1
            total0, dsum0 = sums_of(p0, dp0)
            total1, dsum1 = sums_of(p1, dp1)
            total, dsum = in_steps(
                step, (total0 + widen_lanes(total1), dsum0 + widen_lanes(dsum1))
            )
            return jnp.sum(total, axis=0, keepdims=True), jnp.sum(dsum, axis=0, keepdims=True)

        def diag_top(s0, s1):
            top0 = jnp.max(s0, axis=0, keepdims=True)
            top1 = jnp.max(s1, axis=0, keepdims=True)
            return jnp.concatenate(
                [top0[:, :half], jnp.maximum(top0[:, half:], top1)], axis=1
            )

        def exact():
            def step(j, count, top):
                s = raw_scores(key_rows(j, count), qt)
                return jnp.maximum(top, jnp.max(s, axis=0, keepdims=True))

            s0, s1 = diag_scores()
            return forward(in_steps(step, diag_top(s0, s1)), s0, s1)

        s0, s1 = diag_scores()
        total, dsum = forward(diag_top(s0, s1), s0, s1)
        fits = jnp.max(jnp.where(total < HUGE, 0.0, 1.0)) == 0.0
        total, dsum = lax.cond(fits, lambda: (total, dsum), exact)

        inv = 1.0 / total
        delta = dsum * inv

        def grads(p, dp, inv, delta):
            p = p * inv
            return to_bf16(p), to_bf16(p * (dp - delta))

        def backward(j, count, carry):
            to = key_rows(j - first, count)
            low, ds = grads(scores[to, :], dprobs[to, :], inv, delta)
            part = dqt[...]
            for i in range(count):
                low_i = low[i * TILE : (i + 1) * TILE]
                ds_i = ds[i * TILE : (i + 1) * TILE]
                acc[j + i, DH:, :] += dot_nt(gt, low_i)
                acc[j + i, :DH, :] += dot_nt(qt, ds_i)
                part += jnp.dot(kt[j + i], ds_i, preferred_element_type=F32)
            dqt[...] = part
            return carry

        low0, ds0 = grads(scores[upper_to, :], dprobs[upper_to, :], inv, delta)
        low1, ds1 = grads(
            scores[lower_to, half:], dprobs[lower_to, half:], inv[:, half:], delta[:, half:]
        )
        acc[diag, DH:, :half] += dot_nt(gt, low0)
        acc[diag, :DH, :half] += dot_nt(qt, ds0)
        acc[diag, DH:, half:] += dot_nt(gt[:, half:], low1)
        acc[diag, :DH, half:] += dot_nt(qt[:, half:], ds1)
        dqt[...] = jnp.dot(kt[diag, :, :half], ds0, preferred_element_type=F32)
        dqt[:, half:] += jnp.dot(kt[diag, :, half:], ds1, preferred_element_type=F32)
        in_steps(backward, jnp.int32(0))
        dq_ref[rows, :] = to_bf16((dqt[...] * scale).T)

    copies = [pltpu.make_async_copy(dq_ref, dq_hbm, io_sems.at[0])]
    copies[0].start()
    for b in range(blocks):
        for i in range(4):
            slot = b * local_tiles + (g ^ i)
            out[slot] = to_bf16(acc[slot])
            copy = pltpu.make_async_copy(
                out.at[slot], out_refs[2 * b + i % 2].at[i // 2], sems.at[b, i]
            )
            copy.start()
            copies.append(copy)
    for copy in copies:
        copy.wait()


def along_ctx(x, by):
    n = lax.axis_size("ctx")
    return lax.ppermute(x, "ctx", [(i, i + by) for i in range(n) if 0 <= i + by < n])


def swap_grp(x, bit):
    n = lax.axis_size("grp")
    return lax.ppermute(x, "grp", [(i, i ^ bit) for i in range(n)])


def spans_blocks(doc_tiles, local_tiles):
    ids = jnp.arange(doc_tiles.shape[0])
    begins = jnp.sum(jnp.where(ids[None, :] < ids[:, None], doc_tiles[None, :], 0), axis=1)
    lasts = begins + doc_tiles - 1
    return jnp.max(lasts // local_tiles - begins // local_tiles)


def with_window(queries, kv_cache, grad_out, doc_tiles, *, local_tiles, reach):
    blocks = reach + 1
    slots = blocks * local_tiles
    scale = 1.0 / math.sqrt(DH)
    width = 2 * DH

    x = [kv_cache, along_ctx(kv_cache, 1), along_ctx(kv_cache, 2)]
    y = [swap_grp(kv_cache, 2)]
    y += [swap_grp(x[1], 2), along_ctx(y[0], 2)]
    if reach == 3:
        x.append(along_ctx(x[1], 2))
        y.append(swap_grp(x[3], 2))
    pieces = []
    for d in range(reach, -1, -1):
        pieces += [x[d], swap_grp(x[d], 1), y[d], swap_grp(y[d], 1)]

    hbm = pl.BlockSpec(memory_space=pl.ANY)
    half = jax.ShapeDtypeStruct((local_tiles // 2, width, TILE), BF16)
    grad_queries, *halves = pl.pallas_call(
        lambda *refs: local_kernel(*refs, local_tiles=local_tiles, reach=reach, scale=scale),
        out_shape=(jax.ShapeDtypeStruct(queries.shape, BF16),) + (half,) * (2 * blocks),
        in_specs=[pl.BlockSpec(memory_space=pltpu.SMEM)] + [hbm] * (2 + 4 * blocks),
        out_specs=(hbm,) * (1 + 2 * blocks),
        scratch_shapes=[
            pltpu.VMEM(queries.shape, BF16),
            pltpu.VMEM(queries.shape, BF16),
            pltpu.VMEM(queries.shape, BF16),
            pltpu.VMEM((slots * TILE, width), BF16),
            pltpu.VMEM((slots, DH, TILE), BF16),
            pltpu.VMEM((MAXT * TILE, TILE), F32),
            pltpu.VMEM((MAXT * TILE, TILE), F32),
            pltpu.VMEM((slots, width, TILE), F32),
            pltpu.VMEM((slots, width, TILE), BF16),
            pltpu.VMEM((DH, TILE), F32),
            pltpu.SemaphoreType.DMA((blocks, 4)),
            pltpu.SemaphoreType.DMA((2,)),
        ],
        compiler_params=pltpu.CompilerParams(vmem_limit_bytes=56 * 1024 * 1024),
    )(doc_tiles, queries, grad_out, *pieces)

    own = None
    for d in range(reach, -1, -1):
        keep, send = halves[2 * (reach - d)], halves[2 * (reach - d) + 1]
        got = swap_grp(send, 1).astype(F32)
        theirs = to_bf16(keep[1].astype(F32) + got[1])
        mine = keep[0].astype(F32) + got[0] + swap_grp(theirs, 2).astype(F32)
        if d:
            mine = along_ctx(to_bf16(mine), -d).astype(F32)
        own = mine if own is None else own + mine
    grad_kv = to_bf16(jnp.concatenate([own[:DH] * scale, own[DH:]], axis=0)).T
    return (grad_queries, grad_kv)


def shards(queries, kv_cache, grad_out, doc_tiles):
    local_tiles = queries.shape[0] // TILE
    most = (MAXT - 2) // local_tiles + 1
    assert most == 3
    return lax.cond(
        spans_blocks(doc_tiles, local_tiles) >= most,
        lambda *args: with_window(*args, local_tiles=local_tiles, reach=most),
        lambda *args: with_window(*args, local_tiles=local_tiles, reach=most - 1),
        queries, kv_cache, grad_out, doc_tiles,
    )


def solution(mesh):
    placed = (P("ctx", "grp"), P(("ctx", "grp"), None), P("ctx", "grp"), P())
    return jax.shard_map(
        shards,
        mesh=mesh,
        in_specs=placed,
        out_specs=(P("ctx", "grp"), P(("ctx", "grp"), None)),
        check_vma=False,
    )
```

```python
import functools
import math

import jax
import jax.numpy as jnp
from jax import lax
from jax.experimental import pallas as pl
from jax.experimental.pallas import tpu as pltpu
from jax.sharding import PartitionSpec as P

DH = 128
TILE = 512
MAXT = 12
NEG_FILL = -1e30
HUGE = 2.0**100
SCALE = 1.0 / math.sqrt(DH)
TO_LOG2 = SCALE * math.log2(math.e)
F32 = jnp.float32
BF16 = jnp.bfloat16


def to_bf16(x):
    return x.astype(BF16)


def fold_rows(x):
    return x.reshape(x.shape[0] // 8, 8, x.shape[1])


def first_tile_of(doc_ref, doc_count, tile):
    def step(d, carry):
        begin, found = carry
        found = jnp.where(begin <= tile, begin, found)
        return (begin + doc_ref[d], found)

    return lax.fori_loop(0, doc_count, step, (jnp.int32(0), jnp.int32(0)))[1]


def rows_at(tile, count=1):
    return pl.ds(pl.multiple_of(tile * TILE, TILE), count * TILE)


def in_steps(lo, hi, sizes, step, carry):
    for size in sizes:
        steps = jnp.maximum(hi - lo, 0) // size
        carry = lax.fori_loop(
            0, steps, lambda i, x, lo=lo, size=size: step(lo + i * size, size, x), carry
        )
        lo = lo + steps * size
    return carry


def raw_scores(keys, queries_t):
    return jnp.dot(keys, queries_t, preferred_element_type=F32) * TO_LOG2


def sums_of(p, dp):
    return jnp.sum(fold_rows(p), axis=0), jnp.sum(fold_rows(p * dp), axis=0)


def grads_of(p, dp, inv, delta):
    p = p * inv
    return to_bf16(p), to_bf16(p * (dp - delta))


def causal_mask(size):
    return lax.broadcasted_iota(jnp.int32, (size, size), 0) <= lax.broadcasted_iota(
        jnp.int32, (size, size), 1
    )


def widen_lanes(x):
    return jnp.concatenate([jnp.zeros_like(x), x], axis=1)


def diagonal_scores(win, t, qt):
    half = TILE // 2
    mask = causal_mask(half)
    upper = pl.ds(pl.multiple_of(t * TILE, half), half)
    lower = pl.ds(pl.multiple_of(t * TILE + half, half), half)
    s0 = raw_scores(win[upper, :DH], qt)
    s0 = jnp.concatenate([jnp.where(mask, s0[:, :half], NEG_FILL), s0[:, half:]], axis=1)
    s1 = jnp.where(mask, raw_scores(win[lower, :DH], qt[:, half:]), NEG_FILL)
    return upper, lower, s0, s1


def overgrown(total):
    return jnp.max(jnp.where(total < HUGE, 0.0, 1.0)) > 0.0


def start_all(copies):
    for copy in copies:
        copy.start()


def wait_all(copies):
    for copy in copies:
        copy.wait()


def window_copies(piece_refs, win, sems, g):
    copies = []
    for i, ref in enumerate(piece_refs):
        b, owner = i // 4, g ^ (i % 4)
        copies.append(pltpu.make_async_copy(ref, win.at[rows_at(4 * b + owner)], sems.at[i]))
    return copies


def send_sums(acc, out, out_refs, sems, g):
    blocks = out_refs[0].shape[0] // 2
    copies = []
    for b in range(blocks):
        for i in range(4):
            at = rows_at(4 * b + (g ^ i))
            out[at, :] = to_bf16(acc[at, :])
            to = out_refs[i % 2].at[b if i // 2 else blocks + b]
            copies.append(pltpu.make_async_copy(out.at[at], to, sems.at[4 * b + i]))
            copies[-1].start()
    return copies


def own_stats_kernel(doc_ref, q_hbm, g_hbm, *refs):
    piece_refs, stats_hbm = refs[:4], refs[4]
    stats_ref, q_ref, g_ref, win, sems, io_sems = refs[5:]
    base = lax.axis_index("ctx") * 4
    g = lax.axis_index("grp")
    copies = [
        pltpu.make_async_copy(q_hbm, q_ref, io_sems.at[0]),
        pltpu.make_async_copy(g_hbm, g_ref, io_sems.at[1]),
    ] + window_copies(piece_refs, win, sems, g)
    start_all(copies)
    wait_all(copies)
    half = TILE // 2

    @pl.loop(0, 4)
    def _(t):
        qt = q_ref[rows_at(t), :].T
        gt = g_ref[rows_at(t), :].T
        first = jnp.maximum(first_tile_of(doc_ref, doc_ref.shape[0], base + t) - base, 0)
        upper, lower, s0, s1 = diagonal_scores(win, t, qt)

        def forward(ref):
            def step(j, count, carry):
                at = rows_at(j, count)
                p = jnp.exp2(raw_scores(win[at, :DH], qt) - ref)
                dp = jnp.dot(win[at, DH:], gt, preferred_element_type=F32)
                more, dmore = sums_of(p, dp)
                return (carry[0] + more, carry[1] + dmore)

            dp0 = jnp.dot(win[upper, DH:], gt, preferred_element_type=F32)
            dp1 = jnp.dot(win[lower, DH:], gt[:, half:], preferred_element_type=F32)
            total0, dsum0 = sums_of(jnp.exp2(s0 - ref), dp0)
            total1, dsum1 = sums_of(jnp.exp2(s1 - ref[:, half:]), dp1)
            carry = (total0 + widen_lanes(total1), dsum0 + widen_lanes(dsum1))
            total, dsum = in_steps(first, t, (2, 1), step, carry)
            return (
                ref,
                jnp.sum(total, axis=0, keepdims=True),
                jnp.sum(dsum, axis=0, keepdims=True),
            )

        top0 = jnp.max(s0, axis=0, keepdims=True)
        top1 = jnp.max(s1, axis=0, keepdims=True)
        ref = jnp.concatenate([top0[:, :half], jnp.maximum(top0[:, half:], top1)], axis=1)

        def exact():
            def step(j, count, top):
                s = raw_scores(win[rows_at(j, count), :DH], qt)
                return jnp.maximum(top, jnp.max(s, axis=0, keepdims=True))

            return forward(in_steps(first, t, (1,), step, ref))

        found = forward(ref)
        ref, total, dsum = lax.cond(overgrown(found[1]), exact, lambda: found)
        stats_ref[t, 0:1, :] = ref
        stats_ref[t, 1:2, :] = total
        stats_ref[t, 2:3, :] = dsum

    copy = pltpu.make_async_copy(stats_ref, stats_hbm, io_sems.at[2])
    copy.start()
    copy.wait()


def far_kernel(reach, doc_ref, q_hbm, g_hbm, in_stats_hbm, *refs):
    piece_refs = refs[: 4 * reach]
    stats_hbm, dqt_hbm = refs[4 * reach : 4 * reach + 2]
    out_refs = refs[4 * reach + 2 : 4 * reach + 4]
    (q_ref, g_ref, in_stats, dqt, win, kt, scores, dprobs, acc, out, sems, io_sems) = refs[
        4 * reach + 4 :
    ]
    slots = 4 * reach
    g = lax.axis_index("grp")
    here = lax.axis_index("ctx") * 4
    base = here - slots
    copies = [
        pltpu.make_async_copy(q_hbm, q_ref, io_sems.at[0]),
        pltpu.make_async_copy(g_hbm, g_ref, io_sems.at[1]),
        pltpu.make_async_copy(in_stats_hbm, in_stats, io_sems.at[2]),
    ] + window_copies(piece_refs, win, sems, g)
    start_all(copies)
    acc[...] = jnp.zeros_like(acc)
    wait_all(copies)
    first = first_tile_of(doc_ref, doc_ref.shape[0], here) - base

    @pl.loop(jnp.minimum(first, slots), slots)
    def _(j):
        kt[j] = win[rows_at(j), :DH].T

    @pl.loop(0, 4)
    def _(t):
        q = q_ref[rows_at(t), :]
        go = g_ref[rows_at(t), :]
        qt = q.T
        gt = go.T
        own_ref = in_stats[t, 0:1, :]
        own_total = in_stats[t, 1:2, :]
        own_dsum = in_stats[t, 2:3, :]
        start = first_tile_of(doc_ref, doc_ref.shape[0], here + t) - base
        start = jnp.minimum(start, slots)

        def forward(ref, sizes):
            def step(j, count, carry):
                at = rows_at(j, count)
                to = rows_at(j - start, count)
                p = jnp.exp2(raw_scores(win[at, :DH], qt) - ref)
                scores[to, :] = p
                dp = jnp.dot(win[at, DH:], gt, preferred_element_type=F32)
                dprobs[to, :] = dp
                more, dmore = sums_of(p, dp)
                return (carry[0] + more, carry[1] + dmore)

            zero = jnp.zeros((8, TILE), F32)
            total, dsum = in_steps(start, slots, sizes, step, (zero, zero))
            fade = jnp.exp2(own_ref - ref)
            return (
                ref,
                own_total * fade + jnp.sum(total, axis=0, keepdims=True),
                own_dsum * fade + jnp.sum(dsum, axis=0, keepdims=True),
            )

        def exact():
            def step(j, count, top):
                s = raw_scores(win[rows_at(j, count), :DH], qt)
                return jnp.maximum(top, jnp.max(s, axis=0, keepdims=True))

            return forward(in_steps(start, slots, (1,), step, own_ref), (1,))

        found = forward(own_ref, (4, 2, 1))
        ref, total, dsum = lax.cond(overgrown(found[1]), exact, lambda: found)
        inv = 1.0 / total
        delta = dsum * inv
        in_stats[t, 0:1, :] = ref
        in_stats[t, 1:2, :] = inv
        in_stats[t, 2:3, :] = delta

        def backward(j, count, carry):
            at = rows_at(j, count)
            to = rows_at(j - start, count)
            low, ds = grads_of(scores[to, :], dprobs[to, :], inv, delta)
            acc[at, DH:] += jnp.dot(low, go, preferred_element_type=F32)
            acc[at, :DH] += jnp.dot(ds, q, preferred_element_type=F32)
            part = dqt[t]
            for i in range(count):
                part += jnp.dot(
                    kt[j + i], ds[i * TILE : (i + 1) * TILE], preferred_element_type=F32
                )
            dqt[t] = part
            return carry

        dqt[t] = jnp.zeros((DH, TILE), F32)
        in_steps(start, slots, (4, 2, 1), backward, jnp.int32(0))

    copies = [
        pltpu.make_async_copy(dqt, dqt_hbm, io_sems.at[0]),
        pltpu.make_async_copy(in_stats, stats_hbm, io_sems.at[2]),
    ]
    start_all(copies)
    wait_all(copies + send_sums(acc, out, out_refs, sems, g))


def own_grads_kernel(doc_ref, q_hbm, g_hbm, stats_hbm, dqt_hbm, *refs):
    piece_refs, (dq_hbm, *out_refs) = refs[:4], refs[4:7]
    (q_ref, g_ref, dq_ref, stats, dqt, win, kt, acc, out, sems, io_sems) = refs[7:]
    base = lax.axis_index("ctx") * 4
    g = lax.axis_index("grp")
    copies = [
        pltpu.make_async_copy(q_hbm, q_ref, io_sems.at[0]),
        pltpu.make_async_copy(g_hbm, g_ref, io_sems.at[1]),
        pltpu.make_async_copy(stats_hbm, stats, io_sems.at[2]),
        pltpu.make_async_copy(dqt_hbm, dqt, io_sems.at[3]),
    ] + window_copies(piece_refs, win, sems, g)
    start_all(copies)
    acc[...] = jnp.zeros_like(acc)
    wait_all(copies)
    half = TILE // 2

    @pl.loop(0, 4)
    def _(j):
        kt[j] = win[rows_at(j), :DH].T

    @pl.loop(0, 4)
    def _(t):
        q = q_ref[rows_at(t), :]
        go = g_ref[rows_at(t), :]
        qt = q.T
        gt = go.T
        ref = stats[t, 0:1, :]
        inv = stats[t, 1:2, :]
        delta = stats[t, 2:3, :]
        first = jnp.maximum(first_tile_of(doc_ref, doc_ref.shape[0], base + t) - base, 0)

        def add(at, low, ds, q, go):
            acc[at, DH:] += jnp.dot(low, go, preferred_element_type=F32)
            acc[at, :DH] += jnp.dot(ds, q, preferred_element_type=F32)

        def step(j, count, carry):
            at = rows_at(j, count)
            p = jnp.exp2(raw_scores(win[at, :DH], qt) - ref)
            dp = jnp.dot(win[at, DH:], gt, preferred_element_type=F32)
            low, ds = grads_of(p, dp, inv, delta)
            add(at, low, ds, q, go)
            part = dqt[t]
            for i in range(count):
                part += jnp.dot(
                    kt[j + i], ds[i * TILE : (i + 1) * TILE], preferred_element_type=F32
                )
            dqt[t] = part
            return carry

        in_steps(first, t, (2, 1), step, jnp.int32(0))
        upper, lower, s0, s1 = diagonal_scores(win, t, qt)
        dp0 = jnp.dot(win[upper, DH:], gt, preferred_element_type=F32)
        dp1 = jnp.dot(win[lower, DH:], gt[:, half:], preferred_element_type=F32)
        low0, ds0 = grads_of(jnp.exp2(s0 - ref), dp0, inv, delta)
        low1, ds1 = grads_of(
            jnp.exp2(s1 - ref[:, half:]), dp1, inv[:, half:], delta[:, half:]
        )
        add(upper, low0, ds0, q, go)
        add(lower, low1, ds1, q[half:], go[half:])
        part = dqt[t] + jnp.dot(kt[t, :, :half], ds0, preferred_element_type=F32)
        part += widen_lanes(jnp.dot(kt[t, :, half:], ds1, preferred_element_type=F32))
        dq_ref[rows_at(t), :] = to_bf16((part * SCALE).T)

    copies = [pltpu.make_async_copy(dq_ref, dq_hbm, io_sems.at[0])]
    start_all(copies)
    wait_all(copies + send_sums(acc, out, out_refs, sems, g))


def along_ctx(x, by):
    n = lax.axis_size("ctx")
    return lax.ppermute(x, "ctx", [(i, i + by) for i in range(n) if 0 <= i + by < n])


def swap_grp(x, bit):
    n = lax.axis_size("grp")
    return lax.ppermute(x, "grp", [(i, i ^ bit) for i in range(n)])


def spans_blocks(doc_tiles, local_tiles):
    ids = jnp.arange(doc_tiles.shape[0])
    begins = jnp.sum(jnp.where(ids[None, :] < ids[:, None], doc_tiles[None, :], 0), axis=1)
    lasts = begins + doc_tiles - 1
    return jnp.max(lasts // local_tiles - begins // local_tiles)


def run_kernel(body, name, pairs, out_shape, scratch, args):
    hbm = pl.BlockSpec(memory_space=pl.ANY)
    return pl.pallas_call(
        body,
        name=name,
        out_shape=out_shape,
        in_specs=[pl.BlockSpec(memory_space=pltpu.SMEM)] + [hbm] * (len(args) - 1),
        out_specs=jax.tree.map(lambda _: hbm, out_shape),
        scratch_shapes=scratch,
        compiler_params=pltpu.CompilerParams(vmem_limit_bytes=56 * 1024 * 1024),
        cost_estimate=pl.CostEstimate(
            flops=pairs * 8 * TILE * TILE * DH, bytes_accessed=1 << 22, transcendentals=0
        ),
    )(*args)


def with_window(queries, kv_cache, grad_out, doc_tiles, *, reach):
    width = 2 * DH

    x = [kv_cache, along_ctx(kv_cache, 1), along_ctx(kv_cache, 2)]
    y = [swap_grp(kv_cache, 2)]
    y += [swap_grp(x[1], 2), along_ctx(y[0], 2)]
    if reach == 3:
        x.append(along_ctx(x[1], 2))
        y.append(swap_grp(x[3], 2))
    rows = pltpu.VMEM(queries.shape, BF16)
    stats = jax.ShapeDtypeStruct((4, 8, TILE), F32)
    stats_rows = pltpu.VMEM((4, 8, TILE), F32)
    dqt = jax.ShapeDtypeStruct((4, DH, TILE), F32)
    given = (doc_tiles, queries, grad_out)

    def tiles(count, dtype):
        return pltpu.VMEM((count * TILE, width), dtype)

    def halves(blocks):
        return (jax.ShapeDtypeStruct((2 * blocks, TILE, width), BF16),) * 2

    def flipped(count):
        return pltpu.VMEM((count, DH, TILE), BF16)

    own_pieces = (x[0], swap_grp(x[0], 1), y[0], swap_grp(y[0], 1))
    own_stats = run_kernel(
        own_stats_kernel, "own_stats", 32, stats,
        [
            pltpu.VMEM((4, 8, TILE), F32), rows, rows, tiles(4, BF16),
            pltpu.SemaphoreType.DMA((4,)), pltpu.SemaphoreType.DMA((3,)),
        ],
        given + own_pieces,
    )
    last = max(reach, 2)
    y[last], own_stats = lax.optimization_barrier((y[last], own_stats))
    far_pieces = []
    for d in range(reach, 0, -1):
        far_pieces += [x[d], swap_grp(x[d], 1), y[d], swap_grp(y[d], 1)]
    slots = 4 * reach
    new_stats, far_dqt, keep, send = run_kernel(
        functools.partial(far_kernel, reach), "far_blocks", 128,
        (stats, dqt) + halves(reach),
        [
            rows, rows, stats_rows, pltpu.VMEM((4, DH, TILE), F32),
            tiles(slots, BF16), flipped(slots),
            pltpu.VMEM((slots * TILE, TILE), F32), pltpu.VMEM((slots * TILE, TILE), F32),
            tiles(slots, F32), tiles(slots, BF16),
            pltpu.SemaphoreType.DMA((slots,)), pltpu.SemaphoreType.DMA((3,)),
        ],
        given + (own_stats, *far_pieces),
    )
    def over_cores(keep, send):
        count = keep.shape[0] // 2
        got = swap_grp(send, 1)
        theirs = to_bf16(keep[:count].astype(F32) + got[:count].astype(F32))
        return keep[count:].astype(F32) + got[count:].astype(F32), theirs

    mine, theirs = over_cores(keep, send)
    theirs, new_stats = lax.optimization_barrier((theirs, new_stats))
    grad_queries, *own_sums = run_kernel(
        own_grads_kernel, "own_grads", 32,
        (jax.ShapeDtypeStruct(queries.shape, BF16),) + halves(1),
        [
            rows, rows, rows, stats_rows, pltpu.VMEM((4, DH, TILE), F32),
            tiles(4, BF16), flipped(4), tiles(4, F32), tiles(4, BF16),
            pltpu.SemaphoreType.DMA((4,)), pltpu.SemaphoreType.DMA((4,)),
        ],
        given + (new_stats, far_dqt) + own_pieces,
    )
    got, own_sums = lax.optimization_barrier((swap_grp(theirs, 2), own_sums))
    mine = mine + got.astype(F32)
    own_mine, own_theirs = over_cores(*own_sums)
    own = own_mine[0] + swap_grp(own_theirs[0], 2).astype(F32)
    for d in range(reach, 0, -1):
        own = own + along_ctx(to_bf16(mine[reach - d]), -d).astype(F32)
    grad_kv = to_bf16(jnp.concatenate([own[:, :DH] * SCALE, own[:, DH:]], axis=1))
    return (grad_queries, grad_kv)


def shards(queries, kv_cache, grad_out, doc_tiles):
    local_tiles = queries.shape[0] // TILE
    most = (MAXT - 2) // local_tiles + 1
    assert (local_tiles, most, lax.axis_size("grp")) == (4, 3, 4)
    return lax.cond(
        spans_blocks(doc_tiles, local_tiles) >= most,
        lambda *args: with_window(*args, reach=most),
        lambda *args: with_window(*args, reach=most - 1),
        queries, kv_cache, grad_out, doc_tiles,
    )


def solution(mesh):
    placed = (P("ctx", "grp"), P(("ctx", "grp"), None), P("ctx", "grp"), P())
    return jax.shard_map(
        shards,
        mesh=mesh,
        in_specs=placed,
        out_specs=(P("ctx", "grp"), P(("ctx", "grp"), None)),
        check_vma=False,
    )
```

```python
import math

import jax
import jax.numpy as jnp
from jax import lax
from jax.experimental import pallas as pl
from jax.experimental.pallas import tpu as pltpu
from jax.sharding import PartitionSpec as P

DH = 128
TILE = 512
MAXT = 12
NEG_FILL = -1e30
HUGE = 2.0**100
F32 = jnp.float32
BF16 = jnp.bfloat16


def to_bf16(x):
    return x.astype(BF16)


def fold_rows(x):
    return x.reshape(x.shape[0] // 8, 8, x.shape[1])


def first_tile_of(doc_ref, doc_count, tile):
    def step(d, carry):
        begin, found = carry
        found = jnp.where(begin <= tile, begin, found)
        return (begin + doc_ref[d], found)

    return lax.fori_loop(0, doc_count, step, (jnp.int32(0), jnp.int32(0)))[1]


def local_kernel(*refs, local_tiles, reach, scale):
    blocks = reach + 1
    doc_ref, q_hbm, g_hbm = refs[:3]
    piece_refs = refs[3 : 3 + 4 * blocks]
    dq_hbm = refs[3 + 4 * blocks]
    out_refs = refs[4 + 4 * blocks : 4 + 6 * blocks]
    q_ref, g_ref, dq_ref, win, kt, scores, dprobs, acc, dqt, sems, io_sems = refs[4 + 6 * blocks :]

    slots = blocks * local_tiles
    c = lax.axis_index("ctx")
    g = lax.axis_index("grp")
    base = (c - reach) * local_tiles
    to_log2 = scale * math.log2(math.e)

    def tile_rows(b, owner):
        return pl.ds(pl.multiple_of((b * local_tiles + owner) * TILE, TILE), TILE)

    copies = [
        pltpu.make_async_copy(q_hbm, q_ref, io_sems.at[0]),
        pltpu.make_async_copy(g_hbm, g_ref, io_sems.at[1]),
    ]
    for b in range(blocks):
        for i in range(4):
            copies.append(
                pltpu.make_async_copy(
                    piece_refs[4 * b + i], win.at[tile_rows(b, g ^ i)], sems.at[b, i]
                )
            )
    for copy in copies:
        copy.start()
    acc[...] = jnp.zeros_like(acc)
    for copy in copies:
        copy.wait()

    doc_count = doc_ref.shape[0]
    low = first_tile_of(doc_ref, doc_count, c * local_tiles) - base

    @pl.loop(low, slots)
    def _(j):
        tile = pl.ds(pl.multiple_of(j * TILE, TILE), TILE)
        kt[:, tile] = win[tile, :DH].T

    half = TILE // 2
    causal = lax.broadcasted_iota(jnp.int32, (half, half), 0) <= lax.broadcasted_iota(
        jnp.int32, (half, half), 1
    )

    def widen_lanes(x):
        return jnp.concatenate([jnp.zeros_like(x), x], axis=1)

    @pl.loop(0, local_tiles)
    def _(t):
        rows = pl.ds(pl.multiple_of(t * TILE, TILE), TILE)
        q = q_ref[rows, :]
        go = g_ref[rows, :]
        qt = q.T
        gt = go.T
        diag = reach * local_tiles + t
        first = first_tile_of(doc_ref, doc_count, c * local_tiles + t) - base

        def key_rows(j, count):
            return pl.ds(pl.multiple_of(j * TILE, TILE), count * TILE)

        def in_steps(step, carry, sizes=(4, 2, 1)):
            lo = first
            for size in sizes:
                steps = (diag - lo) // size
                carry = lax.fori_loop(
                    0, steps, lambda i, x, lo=lo, size=size: step(lo + i * size, size, x), carry
                )
                lo = lo + steps * size
            return carry

        def raw_scores(at, queries_t):
            return jnp.dot(win[at, :DH], queries_t, preferred_element_type=F32) * to_log2

        upper = pl.ds(pl.multiple_of(diag * TILE, half), half)
        lower = pl.ds(pl.multiple_of(diag * TILE + half, half), half)
        slot = diag - first
        upper_to = pl.ds(pl.multiple_of(slot * TILE, half), half)
        lower_to = pl.ds(pl.multiple_of(slot * TILE + half, half), half)

        def diag_scores():
            s0 = raw_scores(upper, qt)
            s0 = jnp.concatenate(
                [jnp.where(causal, s0[:, :half], NEG_FILL), s0[:, half:]], axis=1
            )
            s1 = jnp.where(causal, raw_scores(lower, qt[:, half:]), NEG_FILL)
            return s0, s1

        def sums_of(p, dp):
            return jnp.sum(fold_rows(p), axis=0), jnp.sum(fold_rows(p * dp), axis=0)

        def forward(ref, s0, s1, sizes=(4, 2, 1)):
            def step(j, count, carry):
                total, dsum = carry
                at = key_rows(j, count)
                to = key_rows(j - first, count)
                p = jnp.exp2(raw_scores(at, qt) - ref)
                scores[to, :] = p
                dp = jnp.dot(win[at, DH:], gt, preferred_element_type=F32)
                dprobs[to, :] = dp
                more, dmore = sums_of(p, dp)
                return (total + more, dsum + dmore)

            p0 = jnp.exp2(s0 - ref)
            p1 = jnp.exp2(s1 - ref[:, half:])
            dp0 = jnp.dot(win[upper, DH:], gt, preferred_element_type=F32)
            dp1 = jnp.dot(win[lower, DH:], gt[:, half:], preferred_element_type=F32)
            scores[upper_to, :] = p0
            scores[lower_to, half:] = p1
            dprobs[upper_to, :] = dp0
            dprobs[lower_to, half:] = dp1
            total0, dsum0 = sums_of(p0, dp0)
            total1, dsum1 = sums_of(p1, dp1)
            total, dsum = in_steps(
                step, (total0 + widen_lanes(total1), dsum0 + widen_lanes(dsum1)), sizes
            )
            return jnp.sum(total, axis=0, keepdims=True), jnp.sum(dsum, axis=0, keepdims=True)

        def diag_top(s0, s1):
            top0 = jnp.max(s0, axis=0, keepdims=True)
            top1 = jnp.max(s1, axis=0, keepdims=True)
            return jnp.concatenate(
                [top0[:, :half], jnp.maximum(top0[:, half:], top1)], axis=1
            )

        def exact():
            def step(j, count, top):
                s = raw_scores(key_rows(j, count), qt)
                return jnp.maximum(top, jnp.max(s, axis=0, keepdims=True))

            s0, s1 = diag_scores()
            return forward(in_steps(step, diag_top(s0, s1), (1,)), s0, s1, (1,))

        s0, s1 = diag_scores()
        total, dsum = forward(diag_top(s0, s1), s0, s1)
        fits = jnp.max(jnp.where(total < HUGE, 0.0, 1.0)) == 0.0
        total, dsum = lax.cond(fits, lambda: (total, dsum), exact)

        inv = 1.0 / total
        delta = dsum * inv
        dqt[...] = jnp.zeros_like(dqt)

        def grads(p, dp, inv, delta):
            p = p * inv
            return to_bf16(p), to_bf16(p * (dp - delta))

        def add_grads(at, low, ds, q, go):
            acc[at, DH:] += jnp.dot(low, go, preferred_element_type=F32)
            acc[at, :DH] += jnp.dot(ds, q, preferred_element_type=F32)

        def backward(j, count, carry):
            at = key_rows(j, count)
            to = key_rows(j - first, count)
            low, ds = grads(scores[to, :], dprobs[to, :], inv, delta)
            add_grads(at, low, ds, q, go)
            dqt[...] += jnp.dot(kt[:, at], ds, preferred_element_type=F32)
            return carry

        low0, ds0 = grads(scores[upper_to, :], dprobs[upper_to, :], inv, delta)
        low1, ds1 = grads(
            scores[lower_to, half:], dprobs[lower_to, half:], inv[:, half:], delta[:, half:]
        )
        add_grads(upper, low0, ds0, q, go)
        add_grads(lower, low1, ds1, q[half:], go[half:])
        dqt[...] = jnp.dot(kt[:, upper], ds0, preferred_element_type=F32)
        dqt[:, half:] += jnp.dot(kt[:, lower], ds1, preferred_element_type=F32)
        in_steps(backward, jnp.int32(0))
        dq_ref[rows, :] = to_bf16((dqt[...] * scale).T)

    copies = [pltpu.make_async_copy(dq_ref, dq_hbm, io_sems.at[0])]
    copies[0].start()
    for b in range(blocks):
        for i in range(4):
            at = tile_rows(b, g ^ i)
            win[at, :] = to_bf16(acc[at, :])
            copy = pltpu.make_async_copy(
                win.at[at], out_refs[2 * b + i % 2].at[i // 2], sems.at[b, i]
            )
            copy.start()
            copies.append(copy)
    for copy in copies:
        copy.wait()


def up_ctx(x, by):
    n = lax.axis_size("ctx")
    return lax.ppermute(x, "ctx", [(i, (i + by) % n) for i in range(n)])


def down_ctx(x, by):
    n = lax.axis_size("ctx")
    return lax.ppermute(x, "ctx", [(i, (i - by) % n) for i in range(n)])


def swap_grp(x, bit):
    n = lax.axis_size("grp")
    return lax.ppermute(x, "grp", [(i, i ^ bit) for i in range(n)])


def four_tiles(x, y):
    return [x, swap_grp(x, 1), y, swap_grp(y, 1)]


def spans_blocks(doc_tiles, local_tiles):
    ids = jnp.arange(doc_tiles.shape[0])
    begins = jnp.sum(jnp.where(ids[None, :] < ids[:, None], doc_tiles[None, :], 0), axis=1)
    lasts = begins + doc_tiles - 1
    return jnp.max(lasts // local_tiles - begins // local_tiles)


def with_window(queries, grad_out, doc_tiles, pieces, *, local_tiles, reach):
    blocks = reach + 1
    slots = blocks * local_tiles
    scale = 1.0 / math.sqrt(DH)
    width = 2 * DH

    if reach == 3:
        x3 = up_ctx(pieces[1][0], 2)
        pieces = pieces + [four_tiles(x3, swap_grp(x3, 2))]
    pieces = [tile for block in reversed(pieces) for tile in block]

    hbm = pl.BlockSpec(memory_space=pl.ANY)
    half = jax.ShapeDtypeStruct((local_tiles // 2, TILE, width), BF16)
    grad_queries, *halves = pl.pallas_call(
        lambda *refs: local_kernel(*refs, local_tiles=local_tiles, reach=reach, scale=scale),
        out_shape=(jax.ShapeDtypeStruct(queries.shape, BF16),) + (half,) * (2 * blocks),
        in_specs=[pl.BlockSpec(memory_space=pltpu.SMEM)] + [hbm] * (2 + 4 * blocks),
        out_specs=(hbm,) * (1 + 2 * blocks),
        scratch_shapes=[
            pltpu.VMEM(queries.shape, BF16),
            pltpu.VMEM(queries.shape, BF16),
            pltpu.VMEM(queries.shape, BF16),
            pltpu.VMEM((slots * TILE, width), BF16),
            pltpu.VMEM((DH, slots * TILE), BF16),
            pltpu.VMEM((MAXT * TILE, TILE), F32),
            pltpu.VMEM((MAXT * TILE, TILE), F32),
            pltpu.VMEM((slots * TILE, width), F32),
            pltpu.VMEM((DH, TILE), F32),
            pltpu.SemaphoreType.DMA((blocks, 4)),
            pltpu.SemaphoreType.DMA((2,)),
        ],
        compiler_params=pltpu.CompilerParams(vmem_limit_bytes=(40 + 4 * reach) * 1024 * 1024),
    )(doc_tiles, queries, grad_out, *pieces)

    mine, theirs = {}, {}
    for d in range(reach, -1, -1):
        keep, send = halves[2 * (reach - d)], halves[2 * (reach - d) + 1]
        got = swap_grp(send, 1).astype(F32)
        mine[d] = keep[0].astype(F32) + got[0]
        theirs[d] = keep[1].astype(F32) + got[1]
    far_theirs = down_ctx(to_bf16(theirs[2]), 2).astype(F32)
    own = mine[0] + down_ctx(to_bf16(mine[2]), 2).astype(F32)
    own = own + swap_grp(to_bf16(theirs[0] + far_theirs), 2).astype(F32)
    for d in (1, 3)[: reach - 1]:
        block = mine[d] + swap_grp(to_bf16(theirs[d]), 2).astype(F32)
        own = own + down_ctx(to_bf16(block), d).astype(F32)
    grad_kv = to_bf16(jnp.concatenate([own[:, :DH] * scale, own[:, DH:]], axis=1))
    return (grad_queries, grad_kv)


def shards(queries, kv_cache, grad_out, doc_tiles):
    local_tiles = queries.shape[0] // TILE
    most = (MAXT - 2) // local_tiles + 1
    assert most == 3
    x0 = kv_cache
    y0 = swap_grp(x0, 2)
    x1 = up_ctx(x0, 1)
    x2 = up_ctx(x0, 2)
    y1 = swap_grp(x1, 2)
    y2 = up_ctx(y0, 2)
    pieces = [four_tiles(x0, y0), four_tiles(x1, y1), four_tiles(x2, y2)]
    return lax.cond(
        spans_blocks(doc_tiles, local_tiles) >= most,
        lambda *args: with_window(*args, local_tiles=local_tiles, reach=most),
        lambda *args: with_window(*args, local_tiles=local_tiles, reach=most - 1),
        queries, grad_out, doc_tiles, pieces,
    )


def solution(mesh):
    placed = (P("ctx", "grp"), P(("ctx", "grp"), None), P("ctx", "grp"), P())
    return jax.shard_map(
        shards,
        mesh=mesh,
        in_specs=placed,
        out_specs=(P("ctx", "grp"), P(("ctx", "grp"), None)),
        check_vma=False,
    )
```

```python
import math

import jax
import jax.numpy as jnp
from jax import lax
from jax.experimental import pallas as pl
from jax.experimental.pallas import tpu as pltpu
from jax.sharding import PartitionSpec as P

DH = 128
TILE = 512
MAXT = 12
NEG_FILL = -1e30
HUGE = 2.0**100
F32 = jnp.float32
BF16 = jnp.bfloat16


def to_bf16(x):
    return x.astype(BF16)


def fold_rows(x):
    return x.reshape(x.shape[0] // 8, 8, x.shape[1])


def first_tile_of(doc_ref, doc_count, tile):
    def step(d, carry):
        begin, found = carry
        found = jnp.where(begin <= tile, begin, found)
        return (begin + doc_ref[d], found)

    return lax.fori_loop(0, doc_count, step, (jnp.int32(0), jnp.int32(0)))[1]


def local_kernel(*refs, local_tiles, reach, scale):
    blocks = reach + 1
    doc_ref, q_hbm, g_hbm = refs[:3]
    piece_refs = refs[3 : 3 + 4 * blocks]
    dq_hbm = refs[3 + 4 * blocks]
    out_refs = refs[4 + 4 * blocks : 4 + 6 * blocks]
    q_ref, g_ref, dq_ref, win, kt, scores, dprobs, acc, dqt, totals, sems, io_sems = refs[4 + 6 * blocks :]

    slots = blocks * local_tiles
    c = lax.axis_index("ctx")
    g = lax.axis_index("grp")
    base = (c - reach) * local_tiles
    to_log2 = scale * math.log2(math.e)

    def tile_rows(b, owner):
        return pl.ds(pl.multiple_of((b * local_tiles + owner) * TILE, TILE), TILE)

    copies = [
        pltpu.make_async_copy(q_hbm, q_ref, io_sems.at[0]),
        pltpu.make_async_copy(g_hbm, g_ref, io_sems.at[1]),
    ]
    for b in range(blocks):
        for i in range(4):
            copies.append(
                pltpu.make_async_copy(
                    piece_refs[4 * b + i], win.at[tile_rows(b, g ^ i)], sems.at[b, i]
                )
            )
    for copy in copies:
        copy.start()
    for copy in copies:
        copy.wait()

    doc_count = doc_ref.shape[0]
    low = first_tile_of(doc_ref, doc_count, c * local_tiles) - base

    @pl.loop(low, slots)
    def _(j):
        tile = pl.ds(pl.multiple_of(j * TILE, TILE), TILE)
        kt[:, tile] = win[tile, :DH].T

    half = TILE // 2
    causal = lax.broadcasted_iota(jnp.int32, (half, half), 0) <= lax.broadcasted_iota(
        jnp.int32, (half, half), 1
    )

    def widen_lanes(x):
        return jnp.concatenate([jnp.zeros_like(x), x], axis=1)

    def key_rows(j, count):
        return pl.ds(pl.multiple_of(j * TILE, TILE), count * TILE)

    def in_steps(lo, hi, sizes, step, carry):
        for size in sizes:
            steps = (hi - lo) // size
            carry = lax.fori_loop(
                0, steps, lambda i, x, lo=lo, size=size: step(lo + i * size, size, x), carry
            )
            lo = lo + steps * size
        return carry

    def sums_of(p, dp):
        return jnp.sum(fold_rows(p), axis=0), jnp.sum(fold_rows(p * dp), axis=0)

    def query_tile(t, exact):
        rows = pl.ds(pl.multiple_of(t * TILE, TILE), TILE)
        q = q_ref[rows, :]
        go = g_ref[rows, :]
        qt = q.T
        gt = go.T
        diag = reach * local_tiles + t
        first = first_tile_of(doc_ref, doc_count, c * local_tiles + t) - base

        def raw_scores(at, queries_t):
            return jnp.dot(win[at, :DH], queries_t, preferred_element_type=F32) * to_log2

        upper = pl.ds(pl.multiple_of(diag * TILE, half), half)
        lower = pl.ds(pl.multiple_of(diag * TILE + half, half), half)
        slot = diag - first
        upper_to = pl.ds(pl.multiple_of(slot * TILE, half), half)
        lower_to = pl.ds(pl.multiple_of(slot * TILE + half, half), half)
        s0 = raw_scores(upper, qt)
        s0 = jnp.concatenate([jnp.where(causal, s0[:, :half], NEG_FILL), s0[:, half:]], axis=1)
        s1 = jnp.where(causal, raw_scores(lower, qt[:, half:]), NEG_FILL)
        top0 = jnp.max(s0, axis=0, keepdims=True)
        top1 = jnp.max(s1, axis=0, keepdims=True)
        top = jnp.concatenate([top0[:, :half], jnp.maximum(top0[:, half:], top1)], axis=1)

        def top_step(j, top):
            s = raw_scores(key_rows(j, 1), qt)
            return jnp.maximum(top, jnp.max(s, axis=0, keepdims=True))

        top = lax.fori_loop(first, first + exact * (diag - first), top_step, top)

        def forward(j, count, carry):
            at = key_rows(j, count)
            to = key_rows(j - first, count)
            p = jnp.exp2(raw_scores(at, qt) - top)
            scores[to, :] = p
            dp = jnp.dot(win[at, DH:], gt, preferred_element_type=F32)
            dprobs[to, :] = dp
            more, dmore = sums_of(p, dp)
            return (carry[0] + more, carry[1] + dmore)

        p0 = jnp.exp2(s0 - top)
        p1 = jnp.exp2(s1 - top[:, half:])
        dp0 = jnp.dot(win[upper, DH:], gt, preferred_element_type=F32)
        dp1 = jnp.dot(win[lower, DH:], gt[:, half:], preferred_element_type=F32)
        scores[upper_to, :] = p0
        scores[lower_to, :] = widen_lanes(p1)
        dprobs[upper_to, :] = dp0
        dprobs[lower_to, :] = widen_lanes(dp1)
        total0, dsum0 = sums_of(p0, dp0)
        total1, dsum1 = sums_of(p1, dp1)
        total, dsum = in_steps(
            first, diag, (4, 2, 1), forward,
            (total0 + widen_lanes(total1), dsum0 + widen_lanes(dsum1)),
        )
        total = jnp.sum(total, axis=0, keepdims=True)
        totals[t] = jnp.broadcast_to(total, (8, TILE))
        inv = 1.0 / total
        delta = jnp.sum(dsum, axis=0, keepdims=True) * inv
        dqt[...] = jnp.zeros_like(dqt)

        def backward(j, count, carry):
            at = key_rows(j, count)
            to = key_rows(j - first, count)
            p = scores[to, :] * inv
            ds = to_bf16(p * (dprobs[to, :] - delta))
            acc[at, DH:] += jnp.dot(to_bf16(p), go, preferred_element_type=F32)
            acc[at, :DH] += jnp.dot(ds, q, preferred_element_type=F32)
            dqt[...] += jnp.dot(kt[:, at], ds, preferred_element_type=F32)
            return carry

        in_steps(first, diag + 1, (4, 2, 1), backward, jnp.int32(0))
        dq_ref[rows, :] = to_bf16((dqt[...] * scale).T)

    def all_tiles(carry):
        exact, _ = carry
        acc[...] = jnp.zeros_like(acc)

        @pl.loop(0, local_tiles)
        def _(t):
            query_tile(t, exact)

        outgrown = jnp.max(jnp.where(totals[...] < HUGE, 0.0, 1.0)) > 0.0
        return (exact + 1, outgrown.astype(jnp.int32))

    lax.while_loop(
        lambda carry: carry[0] <= carry[1], all_tiles, (jnp.int32(0), jnp.int32(0))
    )

    copies = [pltpu.make_async_copy(dq_ref, dq_hbm, io_sems.at[0])]
    copies[0].start()
    for b in range(blocks):
        for i in range(4):
            at = tile_rows(b, g ^ i)
            win[at, :] = to_bf16(acc[at, :])
            copy = pltpu.make_async_copy(
                win.at[at], out_refs[2 * b + i % 2].at[i // 2], sems.at[b, i]
            )
            copy.start()
            copies.append(copy)
    for copy in copies:
        copy.wait()


def up_ctx(x, by):
    n = lax.axis_size("ctx")
    return lax.ppermute(x, "ctx", [(i, (i + by) % n) for i in range(n)])


def down_ctx(x, by):
    n = lax.axis_size("ctx")
    return lax.ppermute(x, "ctx", [(i, (i - by) % n) for i in range(n)])


def swap_grp(x, bit):
    n = lax.axis_size("grp")
    return lax.ppermute(x, "grp", [(i, i ^ bit) for i in range(n)])


def four_tiles(x, y):
    return [x, swap_grp(x, 1), y, swap_grp(y, 1)]


def spans_blocks(doc_tiles, local_tiles):
    ids = jnp.arange(doc_tiles.shape[0])
    begins = jnp.sum(jnp.where(ids[None, :] < ids[:, None], doc_tiles[None, :], 0), axis=1)
    lasts = begins + doc_tiles - 1
    return jnp.max(lasts // local_tiles - begins // local_tiles)


def with_window(queries, grad_out, doc_tiles, pieces, *, local_tiles, reach):
    blocks = reach + 1
    slots = blocks * local_tiles
    scale = 1.0 / math.sqrt(DH)
    width = 2 * DH

    if reach == 3:
        x1, _, y1, _ = pieces[1]
        pieces = pieces + [four_tiles(up_ctx(x1, 2), up_ctx(y1, 2))]
    pieces = [tile for block in reversed(pieces) for tile in block]

    hbm = pl.BlockSpec(memory_space=pl.ANY)
    half = jax.ShapeDtypeStruct((local_tiles // 2, TILE, width), BF16)
    grad_queries, *halves = pl.pallas_call(
        lambda *refs: local_kernel(*refs, local_tiles=local_tiles, reach=reach, scale=scale),
        out_shape=(jax.ShapeDtypeStruct(queries.shape, BF16),) + (half,) * (2 * blocks),
        in_specs=[pl.BlockSpec(memory_space=pltpu.SMEM)] + [hbm] * (2 + 4 * blocks),
        out_specs=(hbm,) * (1 + 2 * blocks),
        scratch_shapes=[
            pltpu.VMEM(queries.shape, BF16),
            pltpu.VMEM(queries.shape, BF16),
            pltpu.VMEM(queries.shape, BF16),
            pltpu.VMEM((slots * TILE, width), BF16),
            pltpu.VMEM((DH, slots * TILE), BF16),
            pltpu.VMEM((MAXT * TILE, TILE), F32),
            pltpu.VMEM((MAXT * TILE, TILE), F32),
            pltpu.VMEM((slots * TILE, width), F32),
            pltpu.VMEM((DH, TILE), F32),
            pltpu.VMEM((local_tiles, 8, TILE), F32),
            pltpu.SemaphoreType.DMA((blocks, 4)),
            pltpu.SemaphoreType.DMA((2,)),
        ],
        compiler_params=pltpu.CompilerParams(vmem_limit_bytes=(40 + 4 * reach) * 1024 * 1024),
    )(doc_tiles, queries, grad_out, *pieces)

    mine, theirs = {}, {}
    for d in range(reach, -1, -1):
        keep, send = halves[2 * (reach - d)], halves[2 * (reach - d) + 1]
        got = swap_grp(send, 1).astype(F32)
        mine[d] = keep[0].astype(F32) + got[0]
        theirs[d] = keep[1].astype(F32) + got[1]
    far_theirs, far_mine = lax.optimization_barrier(
        (down_ctx(to_bf16(theirs[2]), 2), to_bf16(mine[2]))
    )
    own = mine[0] + down_ctx(far_mine, 2).astype(F32)
    own = own + swap_grp(to_bf16(theirs[0] + far_theirs.astype(F32)), 2).astype(F32)
    for d in (1, 3)[: reach - 1]:
        block = mine[d] + swap_grp(to_bf16(theirs[d]), 2).astype(F32)
        own = own + down_ctx(to_bf16(block), d).astype(F32)
    grad_kv = to_bf16(jnp.concatenate([own[:, :DH] * scale, own[:, DH:]], axis=1))
    return (grad_queries, grad_kv)


def shards(queries, kv_cache, grad_out, doc_tiles):
    local_tiles = queries.shape[0] // TILE
    most = (MAXT - 2) // local_tiles + 1
    assert most == 3
    x0 = kv_cache
    spans = spans_blocks(doc_tiles, local_tiles)
    y0, spans = lax.optimization_barrier((swap_grp(x0, 2), spans))
    x1 = up_ctx(x0, 1)
    x2 = up_ctx(x0, 2)
    y1 = swap_grp(x1, 2)
    y2 = up_ctx(y0, 2)
    pieces = [four_tiles(x0, y0), four_tiles(x1, y1), four_tiles(x2, y2)]
    return lax.cond(
        spans >= most,
        lambda *args: with_window(*args, local_tiles=local_tiles, reach=most),
        lambda *args: with_window(*args, local_tiles=local_tiles, reach=most - 1),
        queries, grad_out, doc_tiles, pieces,
    )


def solution(mesh):
    placed = (P("ctx", "grp"), P(("ctx", "grp"), None), P("ctx", "grp"), P())
    return jax.shard_map(
        shards,
        mesh=mesh,
        in_specs=placed,
        out_specs=(P("ctx", "grp"), P(("ctx", "grp"), None)),
        check_vma=False,
    )
```

```python
import functools
import math

import jax
import jax.numpy as jnp
from jax import lax
from jax.experimental import pallas as pl
from jax.experimental.pallas import tpu as pltpu
from jax.sharding import PartitionSpec as P

DH = 128
TILE = 512
MAXT = 12
NEG_FILL = -1e30
HUGE = 2.0**100
SCALE = 1.0 / math.sqrt(DH)
TO_LOG2 = SCALE * math.log2(math.e)
F32 = jnp.float32
BF16 = jnp.bfloat16


def to_bf16(x):
    return x.astype(BF16)


def fold_rows(x):
    return x.reshape(x.shape[0] // 8, 8, x.shape[1])


def first_tile_of(doc_ref, doc_count, tile):
    def step(d, carry):
        begin, found = carry
        found = jnp.where(begin <= tile, begin, found)
        return (begin + doc_ref[d], found)

    return lax.fori_loop(0, doc_count, step, (jnp.int32(0), jnp.int32(0)))[1]


def rows_at(tile, count=1):
    return pl.ds(pl.multiple_of(tile * TILE, TILE), count * TILE)


def in_steps(lo, hi, sizes, step, carry):
    for size in sizes:
        steps = jnp.maximum(hi - lo, 0) // size
        carry = lax.fori_loop(
            0, steps, lambda i, x, lo=lo, size=size: step(lo + i * size, size, x), carry
        )
        lo = lo + steps * size
    return carry


def raw_scores(keys, queries_t):
    return jnp.dot(keys, queries_t, preferred_element_type=F32) * TO_LOG2


def sums_of(p, dp):
    return jnp.sum(fold_rows(p), axis=0), jnp.sum(fold_rows(p * dp), axis=0)


def grads_of(p, dp, inv, delta):
    p = p * inv
    return to_bf16(p), to_bf16(p * (dp - delta))


def causal_mask(size):
    return lax.broadcasted_iota(jnp.int32, (size, size), 0) <= lax.broadcasted_iota(
        jnp.int32, (size, size), 1
    )


def widen_lanes(x):
    return jnp.concatenate([jnp.zeros_like(x), x], axis=1)


def diagonal_scores(win, t, qt):
    half = TILE // 2
    mask = causal_mask(half)
    upper = pl.ds(pl.multiple_of(t * TILE, half), half)
    lower = pl.ds(pl.multiple_of(t * TILE + half, half), half)
    s0 = raw_scores(win[upper, :DH], qt)
    s0 = jnp.concatenate([jnp.where(mask, s0[:, :half], NEG_FILL), s0[:, half:]], axis=1)
    s1 = jnp.where(mask, raw_scores(win[lower, :DH], qt[:, half:]), NEG_FILL)
    return upper, lower, s0, s1


def overgrown(total):
    return jnp.max(jnp.where(total < HUGE, 0.0, 1.0)) > 0.0


def start_all(copies):
    for copy in copies:
        copy.start()


def wait_all(copies):
    for copy in copies:
        copy.wait()


def window_copies(piece_refs, win, sems, g):
    copies = []
    for i, ref in enumerate(piece_refs):
        b, owner = i // 4, g ^ (i % 4)
        copies.append(pltpu.make_async_copy(ref, win.at[rows_at(4 * b + owner)], sems.at[i]))
    return copies


def send_sums(acc, out, out_refs, sems, g):
    copies = []
    for b in range(len(out_refs) // 2):
        for i in range(4):
            at = rows_at(4 * b + (g ^ i))
            out[at, :] = to_bf16(acc[at, :])
            to = out_refs[2 * b + i % 2].at[i // 2]
            copies.append(pltpu.make_async_copy(out.at[at], to, sems.at[4 * b + i]))
            copies[-1].start()
    return copies


def own_stats_kernel(doc_ref, q_hbm, g_hbm, *refs):
    piece_refs, stats_hbm = refs[:4], refs[4]
    stats_ref, q_ref, g_ref, win, sems, io_sems = refs[5:]
    base = lax.axis_index("ctx") * 4
    g = lax.axis_index("grp")
    copies = [
        pltpu.make_async_copy(q_hbm, q_ref, io_sems.at[0]),
        pltpu.make_async_copy(g_hbm, g_ref, io_sems.at[1]),
    ] + window_copies(piece_refs, win, sems, g)
    start_all(copies)
    wait_all(copies)
    half = TILE // 2

    @pl.loop(0, 4)
    def _(t):
        qt = q_ref[rows_at(t), :].T
        gt = g_ref[rows_at(t), :].T
        first = jnp.maximum(first_tile_of(doc_ref, doc_ref.shape[0], base + t) - base, 0)
        upper, lower, s0, s1 = diagonal_scores(win, t, qt)

        def forward(ref):
            def step(j, count, carry):
                at = rows_at(j, count)
                p = jnp.exp2(raw_scores(win[at, :DH], qt) - ref)
                dp = jnp.dot(win[at, DH:], gt, preferred_element_type=F32)
                more, dmore = sums_of(p, dp)
                return (carry[0] + more, carry[1] + dmore)

            dp0 = jnp.dot(win[upper, DH:], gt, preferred_element_type=F32)
            dp1 = jnp.dot(win[lower, DH:], gt[:, half:], preferred_element_type=F32)
            total0, dsum0 = sums_of(jnp.exp2(s0 - ref), dp0)
            total1, dsum1 = sums_of(jnp.exp2(s1 - ref[:, half:]), dp1)
            carry = (total0 + widen_lanes(total1), dsum0 + widen_lanes(dsum1))
            total, dsum = in_steps(first, t, (3, 2, 1), step, carry)
            return (
                ref,
                jnp.sum(total, axis=0, keepdims=True),
                jnp.sum(dsum, axis=0, keepdims=True),
            )

        top0 = jnp.max(s0, axis=0, keepdims=True)
        top1 = jnp.max(s1, axis=0, keepdims=True)
        ref = jnp.concatenate([top0[:, :half], jnp.maximum(top0[:, half:], top1)], axis=1)

        def exact():
            def step(j, count, top):
                s = raw_scores(win[rows_at(j, count), :DH], qt)
                return jnp.maximum(top, jnp.max(s, axis=0, keepdims=True))

            return forward(in_steps(first, t, (1,), step, ref))

        found = forward(ref)
        ref, total, dsum = lax.cond(overgrown(found[1]), exact, lambda: found)
        stats_ref[t, 0:1, :] = ref
        stats_ref[t, 1:2, :] = total
        stats_ref[t, 2:3, :] = dsum

    copy = pltpu.make_async_copy(stats_ref, stats_hbm, io_sems.at[2])
    copy.start()
    copy.wait()


def far_kernel(reach, doc_ref, q_hbm, g_hbm, in_stats_hbm, *refs):
    piece_refs = refs[: 4 * reach]
    stats_hbm, dqt_hbm = refs[4 * reach : 4 * reach + 2]
    out_refs = refs[4 * reach + 2 : 6 * reach + 2]
    (q_ref, g_ref, in_stats, dqt, win, kt, scores, dprobs, acc, out, sems, io_sems) = refs[
        6 * reach + 2 :
    ]
    slots = 4 * reach
    g = lax.axis_index("grp")
    here = lax.axis_index("ctx") * 4
    base = here - slots
    copies = [
        pltpu.make_async_copy(q_hbm, q_ref, io_sems.at[0]),
        pltpu.make_async_copy(g_hbm, g_ref, io_sems.at[1]),
        pltpu.make_async_copy(in_stats_hbm, in_stats, io_sems.at[2]),
    ] + window_copies(piece_refs, win, sems, g)
    start_all(copies)
    acc[...] = jnp.zeros_like(acc)
    wait_all(copies)
    first = first_tile_of(doc_ref, doc_ref.shape[0], here) - base

    @pl.loop(jnp.minimum(first, slots), slots)
    def _(j):
        kt[:, rows_at(j)] = win[rows_at(j), :DH].T

    @pl.loop(0, 4)
    def _(t):
        q = q_ref[rows_at(t), :]
        go = g_ref[rows_at(t), :]
        qt = q.T
        gt = go.T
        own_ref = in_stats[t, 0:1, :]
        own_total = in_stats[t, 1:2, :]
        own_dsum = in_stats[t, 2:3, :]
        start = first_tile_of(doc_ref, doc_ref.shape[0], here + t) - base
        start = jnp.minimum(start, slots)

        def forward(ref, sizes):
            def step(j, count, carry):
                at = rows_at(j, count)
                to = rows_at(j - start, count)
                p = jnp.exp2(raw_scores(win[at, :DH], qt) - ref)
                scores[to, :] = p
                dp = jnp.dot(win[at, DH:], gt, preferred_element_type=F32)
                dprobs[to, :] = dp
                more, dmore = sums_of(p, dp)
                return (carry[0] + more, carry[1] + dmore)

            zero = jnp.zeros((8, TILE), F32)
            total, dsum = in_steps(start, slots, sizes, step, (zero, zero))
            fade = jnp.exp2(own_ref - ref)
            return (
                ref,
                own_total * fade + jnp.sum(total, axis=0, keepdims=True),
                own_dsum * fade + jnp.sum(dsum, axis=0, keepdims=True),
            )

        def exact():
            def step(j, count, top):
                s = raw_scores(win[rows_at(j, count), :DH], qt)
                return jnp.maximum(top, jnp.max(s, axis=0, keepdims=True))

            return forward(in_steps(start, slots, (1,), step, own_ref), (1,))

        found = forward(own_ref, (4, 2, 1))
        ref, total, dsum = lax.cond(overgrown(found[1]), exact, lambda: found)
        inv = 1.0 / total
        delta = dsum * inv
        in_stats[t, 0:1, :] = ref
        in_stats[t, 1:2, :] = inv
        in_stats[t, 2:3, :] = delta

        def backward(j, count, carry):
            at = rows_at(j, count)
            to = rows_at(j - start, count)
            low, ds = grads_of(scores[to, :], dprobs[to, :], inv, delta)
            acc[at, DH:] += jnp.dot(low, go, preferred_element_type=F32)
            acc[at, :DH] += jnp.dot(ds, q, preferred_element_type=F32)
            dqt[t] += jnp.dot(kt[:, at], ds, preferred_element_type=F32)
            return carry

        dqt[t] = jnp.zeros((DH, TILE), F32)
        in_steps(start, slots, (4, 2, 1), backward, jnp.int32(0))

    copies = [
        pltpu.make_async_copy(dqt, dqt_hbm, io_sems.at[0]),
        pltpu.make_async_copy(in_stats, stats_hbm, io_sems.at[2]),
    ]
    start_all(copies)
    wait_all(copies + send_sums(acc, out, out_refs, sems, g))


def own_grads_kernel(doc_ref, q_hbm, g_hbm, stats_hbm, dqt_hbm, *refs):
    piece_refs, (dq_hbm, *out_refs) = refs[:4], refs[4:7]
    (q_ref, g_ref, dq_ref, stats, dqt, win, kt, acc, out, sems, io_sems) = refs[7:]
    base = lax.axis_index("ctx") * 4
    g = lax.axis_index("grp")
    copies = [
        pltpu.make_async_copy(q_hbm, q_ref, io_sems.at[0]),
        pltpu.make_async_copy(g_hbm, g_ref, io_sems.at[1]),
        pltpu.make_async_copy(stats_hbm, stats, io_sems.at[2]),
        pltpu.make_async_copy(dqt_hbm, dqt, io_sems.at[3]),
    ] + window_copies(piece_refs, win, sems, g)
    start_all(copies)
    acc[...] = jnp.zeros_like(acc)
    wait_all(copies)
    half = TILE // 2

    @pl.loop(0, 4)
    def _(j):
        kt[:, rows_at(j)] = win[rows_at(j), :DH].T

    @pl.loop(0, 4)
    def _(t):
        q = q_ref[rows_at(t), :]
        go = g_ref[rows_at(t), :]
        qt = q.T
        gt = go.T
        ref = stats[t, 0:1, :]
        inv = stats[t, 1:2, :]
        delta = stats[t, 2:3, :]
        first = jnp.maximum(first_tile_of(doc_ref, doc_ref.shape[0], base + t) - base, 0)

        def add(at, low, ds, q, go):
            acc[at, DH:] += jnp.dot(low, go, preferred_element_type=F32)
            acc[at, :DH] += jnp.dot(ds, q, preferred_element_type=F32)

        def step(j, count, carry):
            at = rows_at(j, count)
            p = jnp.exp2(raw_scores(win[at, :DH], qt) - ref)
            dp = jnp.dot(win[at, DH:], gt, preferred_element_type=F32)
            low, ds = grads_of(p, dp, inv, delta)
            add(at, low, ds, q, go)
            dqt[t] += jnp.dot(kt[:, at], ds, preferred_element_type=F32)
            return carry

        in_steps(first, t, (3, 2, 1), step, jnp.int32(0))
        upper, lower, s0, s1 = diagonal_scores(win, t, qt)
        dp0 = jnp.dot(win[upper, DH:], gt, preferred_element_type=F32)
        dp1 = jnp.dot(win[lower, DH:], gt[:, half:], preferred_element_type=F32)
        low0, ds0 = grads_of(jnp.exp2(s0 - ref), dp0, inv, delta)
        low1, ds1 = grads_of(
            jnp.exp2(s1 - ref[:, half:]), dp1, inv[:, half:], delta[:, half:]
        )
        add(upper, low0, ds0, q, go)
        add(lower, low1, ds1, q[half:], go[half:])
        part = dqt[t] + jnp.dot(kt[:, upper], ds0, preferred_element_type=F32)
        part += widen_lanes(jnp.dot(kt[:, lower], ds1, preferred_element_type=F32))
        dq_ref[rows_at(t), :] = to_bf16((part * SCALE).T)

    copies = [pltpu.make_async_copy(dq_ref, dq_hbm, io_sems.at[0])]
    start_all(copies)
    wait_all(copies + send_sums(acc, out, out_refs, sems, g))


def up_ctx(x, by):
    n = lax.axis_size("ctx")
    return lax.ppermute(x, "ctx", [(i, (i + by) % n) for i in range(n)])


def down_ctx(x, by):
    n = lax.axis_size("ctx")
    return lax.ppermute(x, "ctx", [(i, (i - by) % n) for i in range(n)])


def swap_grp(x, bit):
    n = lax.axis_size("grp")
    return lax.ppermute(x, "grp", [(i, i ^ bit) for i in range(n)])


def four_tiles(x, y):
    return [x, swap_grp(x, 1), y, swap_grp(y, 1)]


def spans_blocks(doc_tiles, local_tiles):
    ids = jnp.arange(doc_tiles.shape[0])
    begins = jnp.sum(jnp.where(ids[None, :] < ids[:, None], doc_tiles[None, :], 0), axis=1)
    lasts = begins + doc_tiles - 1
    return jnp.max(lasts // local_tiles - begins // local_tiles)


def run_kernel(body, name, mib, out_shape, scratch, args):
    hbm = pl.BlockSpec(memory_space=pl.ANY)
    return pl.pallas_call(
        body,
        name=name,
        out_shape=out_shape,
        in_specs=[pl.BlockSpec(memory_space=pltpu.SMEM)] + [hbm] * (len(args) - 1),
        out_specs=jax.tree.map(lambda _: hbm, out_shape),
        scratch_shapes=scratch,
        compiler_params=pltpu.CompilerParams(vmem_limit_bytes=mib * 1024 * 1024),
    )(*args)


def rows_of(queries):
    return pltpu.VMEM(queries.shape, BF16)


def tiles(count, dtype):
    return pltpu.VMEM((count * TILE, 2 * DH), dtype)


def sums_by_core(blocks):
    return (jax.ShapeDtypeStruct((2, TILE, 2 * DH), BF16),) * (2 * blocks)


STATS = jax.ShapeDtypeStruct((4, 8, TILE), F32)


def with_window(queries, grad_out, doc_tiles, own_stats, pieces, *, reach):
    given = (doc_tiles, queries, grad_out)
    if reach == 3:
        x1, _, y1, _ = pieces[1]
        pieces = pieces + [four_tiles(up_ctx(x1, 2), up_ctx(y1, 2))]
    far_pieces = [tile for block in reversed(pieces[1:]) for tile in block]
    rows = rows_of(queries)
    stats_rows = pltpu.VMEM(STATS.shape, F32)
    dqt = jax.ShapeDtypeStruct((4, DH, TILE), F32)
    slots = 4 * reach
    new_stats, far_dqt, *far_sums = run_kernel(
        functools.partial(far_kernel, reach), "far_blocks", 24 + 8 * reach,
        (STATS, dqt) + sums_by_core(reach),
        [
            rows, rows, stats_rows, pltpu.VMEM(dqt.shape, F32),
            tiles(slots, BF16), pltpu.VMEM((DH, slots * TILE), BF16),
            pltpu.VMEM((slots * TILE, TILE), F32), pltpu.VMEM((slots * TILE, TILE), F32),
            tiles(slots, F32), tiles(slots, BF16),
            pltpu.SemaphoreType.DMA((slots,)), pltpu.SemaphoreType.DMA((3,)),
        ],
        given + (own_stats, *far_pieces),
    )

    def over_cores(keep, send):
        got = swap_grp(send, 1).astype(F32)
        return keep[0].astype(F32) + got[0], keep[1].astype(F32) + got[1]

    mine, theirs = {}, {}
    for d in range(reach, 0, -1):
        at = 2 * (reach - d)
        mine[d], half = over_cores(far_sums[at], far_sums[at + 1])
        theirs[d] = to_bf16(half)
        if d == 2:
            both = far_sums[at].astype(F32) + swap_grp(far_sums[at + 1], 1).astype(F32)
            theirs[d] = to_bf16(both)
    theirs, new_stats = lax.optimization_barrier((theirs, new_stats))
    grad_queries, *own_sums = run_kernel(
        own_grads_kernel, "own_grads", 24,
        (jax.ShapeDtypeStruct(queries.shape, BF16),) + sums_by_core(1),
        [
            rows, rows, rows, stats_rows, pltpu.VMEM(dqt.shape, F32),
            tiles(4, BF16), pltpu.VMEM((DH, 4 * TILE), BF16), tiles(4, F32), tiles(4, BF16),
            pltpu.SemaphoreType.DMA((4,)), pltpu.SemaphoreType.DMA((4,)),
        ],
        given + (new_stats, far_dqt, *pieces[0]),
    )
    near_theirs, far, own_sums = lax.optimization_barrier(
        (swap_grp(theirs[1], 2), down_ctx(theirs[2], 2), own_sums)
    )
    own, own_theirs = over_cores(*own_sums)
    own = own + far[0].astype(F32)
    own = own + swap_grp(to_bf16(own_theirs + far[1].astype(F32)), 2).astype(F32)
    near = mine[1] + near_theirs.astype(F32)
    own = own + down_ctx(to_bf16(near), 1).astype(F32)
    if reach == 3:
        third = mine[3] + swap_grp(theirs[3], 2).astype(F32)
        own = own + down_ctx(to_bf16(third), 3).astype(F32)
    grad_kv = to_bf16(jnp.concatenate([own[:, :DH] * SCALE, own[:, DH:]], axis=1))
    return (grad_queries, grad_kv)


def shards(queries, kv_cache, grad_out, doc_tiles):
    local_tiles = queries.shape[0] // TILE
    most = (MAXT - 2) // local_tiles + 1
    assert (local_tiles, most, lax.axis_size("grp")) == (4, 3, 4)
    x0 = kv_cache
    spans = spans_blocks(doc_tiles, local_tiles)
    y0, spans = lax.optimization_barrier((swap_grp(x0, 2), spans))
    x1 = up_ctx(x0, 1)
    x2 = up_ctx(x0, 2)
    y1 = swap_grp(x1, 2)
    y2 = up_ctx(y0, 2)
    own_pieces = four_tiles(x0, y0)
    own_stats = run_kernel(
        own_stats_kernel, "own_stats", 24, STATS,
        [
            pltpu.VMEM(STATS.shape, F32), rows_of(queries), rows_of(queries), tiles(4, BF16),
            pltpu.SemaphoreType.DMA((4,)), pltpu.SemaphoreType.DMA((3,)),
        ],
        (doc_tiles, queries, grad_out, *own_pieces),
    )
    y1, x2, y2, own_stats = lax.optimization_barrier((y1, x2, y2, own_stats))
    pieces = [own_pieces, four_tiles(x1, y1), four_tiles(x2, y2)]
    return lax.cond(
        spans >= most,
        lambda *args: with_window(*args, reach=most),
        lambda *args: with_window(*args, reach=most - 1),
        queries, grad_out, doc_tiles, own_stats, pieces,
    )


def solution(mesh):
    placed = (P("ctx", "grp"), P(("ctx", "grp"), None), P("ctx", "grp"), P())
    return jax.shard_map(
        shards,
        mesh=mesh,
        in_specs=placed,
        out_specs=(P("ctx", "grp"), P(("ctx", "grp"), None)),
        check_vma=False,
    )
```

```python
import functools
import math

import jax
import jax.numpy as jnp
from jax import lax
from jax.experimental import pallas as pl
from jax.experimental.pallas import tpu as pltpu
from jax.sharding import PartitionSpec as P

DH = 128
TILE = 512
MAXT = 12
NEG_FILL = -1e30
HUGE = 2.0**100
SCALE = 1.0 / math.sqrt(DH)
TO_LOG2 = SCALE * math.log2(math.e)
F32 = jnp.float32
BF16 = jnp.bfloat16


def to_bf16(x):
    return x.astype(BF16)


def fold_rows(x):
    return x.reshape(x.shape[0] // 8, 8, x.shape[1])


def first_tile_of(doc_ref, doc_count, tile):
    def step(d, carry):
        begin, found = carry
        found = jnp.where(begin <= tile, begin, found)
        return (begin + doc_ref[d], found)

    return lax.fori_loop(0, doc_count, step, (jnp.int32(0), jnp.int32(0)))[1]


def rows_at(tile, count=1):
    return pl.ds(pl.multiple_of(tile * TILE, TILE), count * TILE)


def in_steps(lo, hi, sizes, step, carry):
    for size in sizes:
        steps = jnp.maximum(hi - lo, 0) // size
        carry = lax.fori_loop(
            0, steps, lambda i, x, lo=lo, size=size: step(lo + i * size, size, x), carry
        )
        lo = lo + steps * size
    return carry


def raw_scores(keys, queries_t):
    return jnp.dot(keys, queries_t, preferred_element_type=F32) * TO_LOG2


def sums_of(p, dp):
    return jnp.sum(fold_rows(p), axis=0), jnp.sum(fold_rows(p * dp), axis=0)


def grads_of(p, dp, inv, delta):
    p = p * inv
    return to_bf16(p), to_bf16(p * (dp - delta))


def causal_mask(size):
    return lax.broadcasted_iota(jnp.int32, (size, size), 0) <= lax.broadcasted_iota(
        jnp.int32, (size, size), 1
    )


def widen_lanes(x):
    return jnp.concatenate([jnp.zeros_like(x), x], axis=1)


def diagonal_scores(win, t, qt):
    half = TILE // 2
    mask = causal_mask(half)
    upper = pl.ds(pl.multiple_of(t * TILE, half), half)
    lower = pl.ds(pl.multiple_of(t * TILE + half, half), half)
    s0 = raw_scores(win[upper, :DH], qt)
    s0 = jnp.concatenate([jnp.where(mask, s0[:, :half], NEG_FILL), s0[:, half:]], axis=1)
    s1 = jnp.where(mask, raw_scores(win[lower, :DH], qt[:, half:]), NEG_FILL)
    return upper, lower, s0, s1


def overgrown(total):
    return jnp.max(jnp.where(total < HUGE, 0.0, 1.0)) > 0.0


def start_all(copies):
    for copy in copies:
        copy.start()


def wait_all(copies):
    for copy in copies:
        copy.wait()


def window_copies(piece_refs, win, sems, g):
    copies = []
    for i, ref in enumerate(piece_refs):
        b, owner = i // 4, g ^ (i % 4)
        copies.append(pltpu.make_async_copy(ref, win.at[rows_at(4 * b + owner)], sems.at[i]))
    return copies


def send_sums(acc, out, out_refs, sems, g):
    copies = []
    for b in range(len(out_refs) // 2):
        for i in range(4):
            at = rows_at(4 * b + (g ^ i))
            out[at, :] = to_bf16(acc[at, :])
            to = out_refs[2 * b + i % 2].at[i // 2]
            copies.append(pltpu.make_async_copy(out.at[at], to, sems.at[4 * b + i]))
            copies[-1].start()
    return copies


def own_stats_kernel(doc_ref, q_hbm, g_hbm, *refs):
    piece_refs, stats_hbm = refs[:4], refs[4]
    stats_ref, q_ref, g_ref, win, sems, io_sems = refs[5:]
    base = lax.axis_index("ctx") * 4
    g = lax.axis_index("grp")
    copies = [
        pltpu.make_async_copy(q_hbm, q_ref, io_sems.at[0]),
        pltpu.make_async_copy(g_hbm, g_ref, io_sems.at[1]),
    ] + window_copies(piece_refs, win, sems, g)
    start_all(copies)
    wait_all(copies)
    half = TILE // 2

    @pl.loop(0, 4)
    def _(t):
        qt = q_ref[rows_at(t), :].T
        gt = g_ref[rows_at(t), :].T
        first = jnp.maximum(first_tile_of(doc_ref, doc_ref.shape[0], base + t) - base, 0)
        upper, lower, s0, s1 = diagonal_scores(win, t, qt)

        def forward(ref):
            def step(j, count, carry):
                at = rows_at(j, count)
                p = jnp.exp2(raw_scores(win[at, :DH], qt) - ref)
                dp = jnp.dot(win[at, DH:], gt, preferred_element_type=F32)
                more, dmore = sums_of(p, dp)
                return (carry[0] + more, carry[1] + dmore)

            dp0 = jnp.dot(win[upper, DH:], gt, preferred_element_type=F32)
            dp1 = jnp.dot(win[lower, DH:], gt[:, half:], preferred_element_type=F32)
            total0, dsum0 = sums_of(jnp.exp2(s0 - ref), dp0)
            total1, dsum1 = sums_of(jnp.exp2(s1 - ref[:, half:]), dp1)
            carry = (total0 + widen_lanes(total1), dsum0 + widen_lanes(dsum1))
            total, dsum = in_steps(first, t, (3, 2, 1), step, carry)
            return (
                ref,
                jnp.sum(total, axis=0, keepdims=True),
                jnp.sum(dsum, axis=0, keepdims=True),
            )

        top0 = jnp.max(s0, axis=0, keepdims=True)
        top1 = jnp.max(s1, axis=0, keepdims=True)
        ref = jnp.concatenate([top0[:, :half], jnp.maximum(top0[:, half:], top1)], axis=1)

        def exact():
            def step(j, count, top):
                s = raw_scores(win[rows_at(j, count), :DH], qt)
                return jnp.maximum(top, jnp.max(s, axis=0, keepdims=True))

            return forward(in_steps(first, t, (1,), step, ref))

        found = forward(ref)
        ref, total, dsum = lax.cond(overgrown(found[1]), exact, lambda: found)
        stats_ref[t, 0:1, :] = ref
        stats_ref[t, 1:2, :] = total
        stats_ref[t, 2:3, :] = dsum

    copy = pltpu.make_async_copy(stats_ref, stats_hbm, io_sems.at[2])
    copy.start()
    copy.wait()


def far_kernel(reach, doc_ref, q_hbm, g_hbm, in_stats_hbm, *refs):
    piece_refs = refs[: 4 * reach]
    stats_hbm, dqt_hbm = refs[4 * reach : 4 * reach + 2]
    out_refs = refs[4 * reach + 2 : 6 * reach + 2]
    (q_ref, g_ref, in_stats, dqt, win, kt, scores, dprobs, acc, out, sems, io_sems) = refs[
        6 * reach + 2 :
    ]
    slots = 4 * reach
    g = lax.axis_index("grp")
    here = lax.axis_index("ctx") * 4
    base = here - slots
    copies = [
        pltpu.make_async_copy(q_hbm, q_ref, io_sems.at[0]),
        pltpu.make_async_copy(g_hbm, g_ref, io_sems.at[1]),
        pltpu.make_async_copy(in_stats_hbm, in_stats, io_sems.at[2]),
    ] + window_copies(piece_refs, win, sems, g)
    start_all(copies)
    acc[...] = jnp.zeros_like(acc)
    wait_all(copies)
    first = first_tile_of(doc_ref, doc_ref.shape[0], here) - base

    @pl.loop(jnp.minimum(first, slots), slots)
    def _(j):
        kt[:, rows_at(j)] = win[rows_at(j), :DH].T

    @pl.loop(0, 4)
    def _(t):
        q = q_ref[rows_at(t), :]
        go = g_ref[rows_at(t), :]
        qt = q.T
        gt = go.T
        own_ref = in_stats[t, 0:1, :]
        own_total = in_stats[t, 1:2, :]
        own_dsum = in_stats[t, 2:3, :]
        start = first_tile_of(doc_ref, doc_ref.shape[0], here + t) - base
        start = jnp.minimum(start, slots)

        def forward(ref, sizes):
            def step(j, count, carry):
                at = rows_at(j, count)
                to = rows_at(j - start, count)
                p = jnp.exp2(raw_scores(win[at, :DH], qt) - ref)
                scores[to, :] = p
                dp = jnp.dot(win[at, DH:], gt, preferred_element_type=F32)
                dprobs[to, :] = dp
                more, dmore = sums_of(p, dp)
                return (carry[0] + more, carry[1] + dmore)

            zero = jnp.zeros((8, TILE), F32)
            total, dsum = in_steps(start, slots, sizes, step, (zero, zero))
            fade = jnp.exp2(own_ref - ref)
            return (
                ref,
                own_total * fade + jnp.sum(total, axis=0, keepdims=True),
                own_dsum * fade + jnp.sum(dsum, axis=0, keepdims=True),
            )

        def exact():
            def step(j, count, top):
                s = raw_scores(win[rows_at(j, count), :DH], qt)
                return jnp.maximum(top, jnp.max(s, axis=0, keepdims=True))

            return forward(in_steps(start, slots, (1,), step, own_ref), (1,))

        found = forward(own_ref, (4, 2, 1))
        ref, total, dsum = lax.cond(overgrown(found[1]), exact, lambda: found)
        inv = 1.0 / total
        delta = dsum * inv
        in_stats[t, 0:1, :] = ref
        in_stats[t, 1:2, :] = inv
        in_stats[t, 2:3, :] = delta

        def backward(j, count, carry):
            at = rows_at(j, count)
            to = rows_at(j - start, count)
            low, ds = grads_of(scores[to, :], dprobs[to, :], inv, delta)
            acc[at, DH:] += jnp.dot(low, go, preferred_element_type=F32)
            acc[at, :DH] += jnp.dot(ds, q, preferred_element_type=F32)
            dqt[t] += jnp.dot(kt[:, at], ds, preferred_element_type=F32)
            return carry

        dqt[t] = jnp.zeros((DH, TILE), F32)
        in_steps(start, slots, (4, 2, 1), backward, jnp.int32(0))

    copies = [
        pltpu.make_async_copy(dqt, dqt_hbm, io_sems.at[0]),
        pltpu.make_async_copy(in_stats, stats_hbm, io_sems.at[2]),
    ]
    start_all(copies)
    wait_all(copies + send_sums(acc, out, out_refs, sems, g))


def own_grads_kernel(doc_ref, q_hbm, g_hbm, stats_hbm, dqt_hbm, *refs):
    piece_refs, (dq_hbm, *out_refs) = refs[:4], refs[4:7]
    (q_ref, g_ref, dq_ref, stats, dqt, win, kt, acc, out, sems, io_sems) = refs[7:]
    base = lax.axis_index("ctx") * 4
    g = lax.axis_index("grp")
    copies = [
        pltpu.make_async_copy(q_hbm, q_ref, io_sems.at[0]),
        pltpu.make_async_copy(g_hbm, g_ref, io_sems.at[1]),
        pltpu.make_async_copy(stats_hbm, stats, io_sems.at[2]),
        pltpu.make_async_copy(dqt_hbm, dqt, io_sems.at[3]),
    ] + window_copies(piece_refs, win, sems, g)
    start_all(copies)
    acc[...] = jnp.zeros_like(acc)
    wait_all(copies)
    half = TILE // 2

    @pl.loop(0, 4)
    def _(j):
        kt[:, rows_at(j)] = win[rows_at(j), :DH].T

    @pl.loop(0, 4)
    def _(t):
        q = q_ref[rows_at(t), :]
        go = g_ref[rows_at(t), :]
        qt = q.T
        gt = go.T
        ref = stats[t, 0:1, :]
        inv = stats[t, 1:2, :]
        delta = stats[t, 2:3, :]
        first = jnp.maximum(first_tile_of(doc_ref, doc_ref.shape[0], base + t) - base, 0)

        def add(at, low, ds, q, go):
            acc[at, DH:] += jnp.dot(low, go, preferred_element_type=F32)
            acc[at, :DH] += jnp.dot(ds, q, preferred_element_type=F32)

        def step(j, count, carry):
            at = rows_at(j, count)
            p = jnp.exp2(raw_scores(win[at, :DH], qt) - ref)
            dp = jnp.dot(win[at, DH:], gt, preferred_element_type=F32)
            low, ds = grads_of(p, dp, inv, delta)
            add(at, low, ds, q, go)
            dqt[t] += jnp.dot(kt[:, at], ds, preferred_element_type=F32)
            return carry

        in_steps(first, t, (3, 2, 1), step, jnp.int32(0))
        upper, lower, s0, s1 = diagonal_scores(win, t, qt)
        dp0 = jnp.dot(win[upper, DH:], gt, preferred_element_type=F32)
        dp1 = jnp.dot(win[lower, DH:], gt[:, half:], preferred_element_type=F32)
        low0, ds0 = grads_of(jnp.exp2(s0 - ref), dp0, inv, delta)
        low1, ds1 = grads_of(
            jnp.exp2(s1 - ref[:, half:]), dp1, inv[:, half:], delta[:, half:]
        )
        add(upper, low0, ds0, q, go)
        add(lower, low1, ds1, q[half:], go[half:])
        part = dqt[t] + jnp.dot(kt[:, upper], ds0, preferred_element_type=F32)
        part += widen_lanes(jnp.dot(kt[:, lower], ds1, preferred_element_type=F32))
        dq_ref[rows_at(t), :] = to_bf16((part * SCALE).T)

    copies = [pltpu.make_async_copy(dq_ref, dq_hbm, io_sems.at[0])]
    start_all(copies)
    wait_all(copies + send_sums(acc, out, out_refs, sems, g))


def up_ctx(x, by):
    n = lax.axis_size("ctx")
    return lax.ppermute(x, "ctx", [(i, (i + by) % n) for i in range(n)])


def down_ctx(x, by):
    n = lax.axis_size("ctx")
    return lax.ppermute(x, "ctx", [(i, (i - by) % n) for i in range(n)])


def swap_grp(x, bit):
    n = lax.axis_size("grp")
    return lax.ppermute(x, "grp", [(i, i ^ bit) for i in range(n)])


def four_tiles(x, y):
    return [x, swap_grp(x, 1), y, swap_grp(y, 1)]


def spans_blocks(doc_tiles, local_tiles):
    ids = jnp.arange(doc_tiles.shape[0])
    begins = jnp.sum(jnp.where(ids[None, :] < ids[:, None], doc_tiles[None, :], 0), axis=1)
    lasts = begins + doc_tiles - 1
    return jnp.max(lasts // local_tiles - begins // local_tiles)


def run_kernel(body, name, mib, out_shape, scratch, args):
    hbm = pl.BlockSpec(memory_space=pl.ANY)
    return pl.pallas_call(
        body,
        name=name,
        out_shape=out_shape,
        in_specs=[pl.BlockSpec(memory_space=pltpu.SMEM)] + [hbm] * (len(args) - 1),
        out_specs=jax.tree.map(lambda _: hbm, out_shape),
        scratch_shapes=scratch,
        compiler_params=pltpu.CompilerParams(vmem_limit_bytes=mib * 1024 * 1024),
    )(*args)


def rows_of(queries):
    return pltpu.VMEM(queries.shape, BF16)


def tiles(count, dtype):
    return pltpu.VMEM((count * TILE, 2 * DH), dtype)


def sums_by_core(blocks):
    return (jax.ShapeDtypeStruct((2, TILE, 2 * DH), BF16),) * (2 * blocks)


STATS = jax.ShapeDtypeStruct((4, 8, TILE), F32)


def with_window(queries, grad_out, doc_tiles, own_stats, pieces, *, reach):
    given = (doc_tiles, queries, grad_out)
    own_pieces, *far = pieces
    if reach == 3:
        x1, _, y1 = far[0]
        x3, y3 = up_ctx(x1, 2), up_ctx(y1, 2)
        far = far + [[x3, swap_grp(x3, 1), y3]]
    far = [block + [swap_grp(block[2], 1)] for block in far]
    far_pieces = [tile for block in reversed(far) for tile in block]
    rows = rows_of(queries)
    stats_rows = pltpu.VMEM(STATS.shape, F32)
    dqt = jax.ShapeDtypeStruct((4, DH, TILE), F32)
    slots = 4 * reach
    new_stats, far_dqt, *far_sums = run_kernel(
        functools.partial(far_kernel, reach), "far_blocks", 24 + 8 * reach,
        (STATS, dqt) + sums_by_core(reach),
        [
            rows, rows, stats_rows, pltpu.VMEM(dqt.shape, F32),
            tiles(slots, BF16), pltpu.VMEM((DH, slots * TILE), BF16),
            pltpu.VMEM((slots * TILE, TILE), F32), pltpu.VMEM((slots * TILE, TILE), F32),
            tiles(slots, F32), tiles(slots, BF16),
            pltpu.SemaphoreType.DMA((slots,)), pltpu.SemaphoreType.DMA((3,)),
        ],
        given + (own_stats, *far_pieces),
    )

    def over_cores(keep, send):
        return keep.astype(F32) + swap_grp(send, 1).astype(F32)

    mine, theirs = {}, {}
    for d in range(reach, 0, -1):
        both = over_cores(*far_sums[2 * (reach - d) : 2 * (reach - d) + 2])
        mine[d], theirs[d] = both[0], to_bf16(both if d == 2 else both[1])
    theirs, new_stats = lax.optimization_barrier((theirs, new_stats))
    grad_queries, *own_sums = run_kernel(
        own_grads_kernel, "own_grads", 24,
        (jax.ShapeDtypeStruct(queries.shape, BF16),) + sums_by_core(1),
        [
            rows, rows, rows, stats_rows, pltpu.VMEM(dqt.shape, F32),
            tiles(4, BF16), pltpu.VMEM((DH, 4 * TILE), BF16), tiles(4, F32), tiles(4, BF16),
            pltpu.SemaphoreType.DMA((4,)), pltpu.SemaphoreType.DMA((4,)),
        ],
        given + (new_stats, far_dqt, *own_pieces),
    )
    far = down_ctx(theirs[2], 2)
    near_theirs, own_sums = lax.optimization_barrier((swap_grp(theirs[1], 2), own_sums))
    both = over_cores(*own_sums) + far.astype(F32)
    own = both[0] + swap_grp(to_bf16(both[1]), 2).astype(F32)
    near = mine[1] + near_theirs.astype(F32)
    own = own + down_ctx(to_bf16(near), 1).astype(F32)
    if reach == 3:
        third = mine[3] + swap_grp(theirs[3], 2).astype(F32)
        own = own + down_ctx(to_bf16(third), 3).astype(F32)
    grad_kv = to_bf16(jnp.concatenate([own[:, :DH] * SCALE, own[:, DH:]], axis=1))
    return (grad_queries, grad_kv)


def shards(queries, kv_cache, grad_out, doc_tiles):
    local_tiles = queries.shape[0] // TILE
    most = (MAXT - 2) // local_tiles + 1
    assert (local_tiles, most, lax.axis_size("grp")) == (4, 3, 4)
    x0 = kv_cache
    spans = spans_blocks(doc_tiles, local_tiles)
    y0, spans = lax.optimization_barrier((swap_grp(x0, 2), spans))
    x1 = up_ctx(x0, 1)
    x2 = up_ctx(x0, 2)
    y1 = swap_grp(x1, 2)
    y0, x2 = lax.optimization_barrier((y0, x2))
    y2 = up_ctx(y0, 2)
    own_pieces = four_tiles(x0, y0)
    own_stats = run_kernel(
        own_stats_kernel, "own_stats", 24, STATS,
        [
            pltpu.VMEM(STATS.shape, F32), rows_of(queries), rows_of(queries), tiles(4, BF16),
            pltpu.SemaphoreType.DMA((4,)), pltpu.SemaphoreType.DMA((3,)),
        ],
        (doc_tiles, queries, grad_out, *own_pieces),
    )
    pieces = [own_pieces, [x1, swap_grp(x1, 1), y1], [x2, swap_grp(x2, 1), y2]]
    return lax.cond(
        spans >= most,
        lambda *args: with_window(*args, reach=most),
        lambda *args: with_window(*args, reach=most - 1),
        queries, grad_out, doc_tiles, own_stats, pieces,
    )


def solution(mesh):
    placed = (P("ctx", "grp"), P(("ctx", "grp"), None), P("ctx", "grp"), P())
    return jax.shard_map(
        shards,
        mesh=mesh,
        in_specs=placed,
        out_specs=(P("ctx", "grp"), P(("ctx", "grp"), None)),
        check_vma=False,
    )
```

```python
import functools
import math

import jax
import jax.numpy as jnp
from jax import lax
from jax.experimental import pallas as pl
from jax.experimental.pallas import tpu as pltpu
from jax.sharding import PartitionSpec as P

DH = 128
TILE = 512
MAXT = 12
NEG_FILL = -1e30
HUGE = 2.0**100
SCALE = 1.0 / math.sqrt(DH)
TO_LOG2 = SCALE * math.log2(math.e)
F32 = jnp.float32
BF16 = jnp.bfloat16


def to_bf16(x):
    return x.astype(BF16)


def fold_rows(x):
    return x.reshape(x.shape[0] // 8, 8, x.shape[1])


def first_tile_of(doc_ref, doc_count, tile):
    def step(d, carry):
        begin, found = carry
        found = jnp.where(begin <= tile, begin, found)
        return (begin + doc_ref[d], found)

    return lax.fori_loop(0, doc_count, step, (jnp.int32(0), jnp.int32(0)))[1]


def rows_at(tile, count=1):
    return pl.ds(pl.multiple_of(tile * TILE, TILE), count * TILE)


def in_steps(lo, hi, sizes, step, carry):
    for size in sizes:
        steps = jnp.maximum(hi - lo, 0) // size
        carry = lax.fori_loop(
            0, steps, lambda i, x, lo=lo, size=size: step(lo + i * size, size, x), carry
        )
        lo = lo + steps * size
    return carry


def raw_scores(keys, queries_t):
    return jnp.dot(keys, queries_t, preferred_element_type=F32) * TO_LOG2


def sums_of(p, dp):
    return jnp.sum(fold_rows(p), axis=0), jnp.sum(fold_rows(p * dp), axis=0)


def grads_of(p, dp, inv, delta):
    p = p * inv
    return to_bf16(p), to_bf16(p * (dp - delta))


def causal_mask(size):
    return lax.broadcasted_iota(jnp.int32, (size, size), 0) <= lax.broadcasted_iota(
        jnp.int32, (size, size), 1
    )


def widen_lanes(x):
    return jnp.concatenate([jnp.zeros_like(x), x], axis=1)


def diagonal_scores(win, t, qt):
    half = TILE // 2
    mask = causal_mask(half)
    upper = pl.ds(pl.multiple_of(t * TILE, half), half)
    lower = pl.ds(pl.multiple_of(t * TILE + half, half), half)
    s0 = raw_scores(win[upper, :DH], qt)
    s0 = jnp.concatenate([jnp.where(mask, s0[:, :half], NEG_FILL), s0[:, half:]], axis=1)
    s1 = jnp.where(mask, raw_scores(win[lower, :DH], qt[:, half:]), NEG_FILL)
    return upper, lower, s0, s1


def overgrown(total):
    return jnp.max(jnp.where(total < HUGE, 0.0, 1.0)) > 0.0


def start_all(copies):
    for copy in copies:
        copy.start()


def wait_all(copies):
    for copy in copies:
        copy.wait()


def window_copies(piece_refs, win, sems, g):
    copies = []
    for i, ref in enumerate(piece_refs):
        b, owner = i // 4, g ^ (i % 4)
        copies.append(pltpu.make_async_copy(ref, win.at[rows_at(4 * b + owner)], sems.at[i]))
    return copies


def send_sums(acc, out, out_refs, sems, g):
    copies = []
    for b in range(len(out_refs) // 2):
        for i in range(4):
            at = rows_at(4 * b + (g ^ i))
            out[at, :] = to_bf16(acc[at, :])
            to = out_refs[2 * b + i % 2].at[i // 2]
            copies.append(pltpu.make_async_copy(out.at[at], to, sems.at[4 * b + i]))
            copies[-1].start()
    return copies


def own_stats_kernel(doc_ref, q_hbm, g_hbm, *refs):
    piece_refs, stats_hbm = refs[:4], refs[4]
    stats_ref, q_ref, g_ref, win, sems, io_sems = refs[5:]
    base = lax.axis_index("ctx") * 4
    g = lax.axis_index("grp")
    copies = [
        pltpu.make_async_copy(q_hbm, q_ref, io_sems.at[0]),
        pltpu.make_async_copy(g_hbm, g_ref, io_sems.at[1]),
    ] + window_copies(piece_refs, win, sems, g)
    start_all(copies)
    wait_all(copies)
    half = TILE // 2

    @pl.loop(0, 4)
    def _(t):
        qt = q_ref[rows_at(t), :].T
        gt = g_ref[rows_at(t), :].T
        first = jnp.maximum(first_tile_of(doc_ref, doc_ref.shape[0], base + t) - base, 0)
        upper, lower, s0, s1 = diagonal_scores(win, t, qt)

        def forward(ref):
            def step(j, count, carry):
                at = rows_at(j, count)
                p = jnp.exp2(raw_scores(win[at, :DH], qt) - ref)
                dp = jnp.dot(win[at, DH:], gt, preferred_element_type=F32)
                more, dmore = sums_of(p, dp)
                return (carry[0] + more, carry[1] + dmore)

            dp0 = jnp.dot(win[upper, DH:], gt, preferred_element_type=F32)
            dp1 = jnp.dot(win[lower, DH:], gt[:, half:], preferred_element_type=F32)
            total0, dsum0 = sums_of(jnp.exp2(s0 - ref), dp0)
            total1, dsum1 = sums_of(jnp.exp2(s1 - ref[:, half:]), dp1)
            carry = (total0 + widen_lanes(total1), dsum0 + widen_lanes(dsum1))
            total, dsum = in_steps(first, t, (3, 2, 1), step, carry)
            return (
                ref,
                jnp.sum(total, axis=0, keepdims=True),
                jnp.sum(dsum, axis=0, keepdims=True),
            )

        top0 = jnp.max(s0, axis=0, keepdims=True)
        top1 = jnp.max(s1, axis=0, keepdims=True)
        ref = jnp.concatenate([top0[:, :half], jnp.maximum(top0[:, half:], top1)], axis=1)

        def exact():
            def step(j, count, top):
                s = raw_scores(win[rows_at(j, count), :DH], qt)
                return jnp.maximum(top, jnp.max(s, axis=0, keepdims=True))

            return forward(in_steps(first, t, (1,), step, ref))

        found = forward(ref)
        ref, total, dsum = lax.cond(overgrown(found[1]), exact, lambda: found)
        stats_ref[t, 0:1, :] = ref
        stats_ref[t, 1:2, :] = total
        stats_ref[t, 2:3, :] = dsum

    copy = pltpu.make_async_copy(stats_ref, stats_hbm, io_sems.at[2])
    copy.start()
    copy.wait()


def far_kernel(reach, doc_ref, q_hbm, g_hbm, in_stats_hbm, *refs):
    piece_refs = refs[: 4 * reach]
    stats_hbm, dqt_hbm = refs[4 * reach : 4 * reach + 2]
    out_refs = refs[4 * reach + 2 : 6 * reach + 2]
    (q_ref, g_ref, in_stats, dqt, win, kt, scores, dprobs, acc, out, sems, io_sems) = refs[
        6 * reach + 2 :
    ]
    slots = 4 * reach
    g = lax.axis_index("grp")
    here = lax.axis_index("ctx") * 4
    base = here - slots
    copies = [
        pltpu.make_async_copy(q_hbm, q_ref, io_sems.at[0]),
        pltpu.make_async_copy(g_hbm, g_ref, io_sems.at[1]),
        pltpu.make_async_copy(in_stats_hbm, in_stats, io_sems.at[2]),
    ] + window_copies(piece_refs, win, sems, g)
    start_all(copies)
    acc[...] = jnp.zeros_like(acc)
    wait_all(copies)
    first = first_tile_of(doc_ref, doc_ref.shape[0], here) - base

    @pl.loop(jnp.minimum(first, slots), slots)
    def _(j):
        kt[:, rows_at(j)] = win[rows_at(j), :DH].T

    @pl.loop(0, 4)
    def _(t):
        q = q_ref[rows_at(t), :]
        go = g_ref[rows_at(t), :]
        qt = q.T
        gt = go.T
        own_ref = in_stats[t, 0:1, :]
        own_total = in_stats[t, 1:2, :]
        own_dsum = in_stats[t, 2:3, :]
        start = first_tile_of(doc_ref, doc_ref.shape[0], here + t) - base
        start = jnp.minimum(start, slots)

        def forward(ref, sizes):
            def step(j, count, carry):
                at = rows_at(j, count)
                to = rows_at(j - start, count)
                p = jnp.exp2(raw_scores(win[at, :DH], qt) - ref)
                scores[to, :] = p
                dp = jnp.dot(win[at, DH:], gt, preferred_element_type=F32)
                dprobs[to, :] = dp
                more, dmore = sums_of(p, dp)
                return (carry[0] + more, carry[1] + dmore)

            zero = jnp.zeros((8, TILE), F32)
            total, dsum = in_steps(start, slots, sizes, step, (zero, zero))
            fade = jnp.exp2(own_ref - ref)
            return (
                ref,
                own_total * fade + jnp.sum(total, axis=0, keepdims=True),
                own_dsum * fade + jnp.sum(dsum, axis=0, keepdims=True),
            )

        def exact():
            def step(j, count, top):
                s = raw_scores(win[rows_at(j, count), :DH], qt)
                return jnp.maximum(top, jnp.max(s, axis=0, keepdims=True))

            return forward(in_steps(start, slots, (1,), step, own_ref), (1,))

        found = forward(own_ref, (4, 2, 1))
        ref, total, dsum = lax.cond(overgrown(found[1]), exact, lambda: found)
        inv = 1.0 / total
        delta = dsum * inv
        in_stats[t, 0:1, :] = ref
        in_stats[t, 1:2, :] = inv
        in_stats[t, 2:3, :] = delta

        def backward(j, count, carry):
            at = rows_at(j, count)
            to = rows_at(j - start, count)
            low, ds = grads_of(scores[to, :], dprobs[to, :], inv, delta)
            acc[at, DH:] += jnp.dot(low, go, preferred_element_type=F32)
            acc[at, :DH] += jnp.dot(ds, q, preferred_element_type=F32)
            dqt[t] += jnp.dot(kt[:, at], ds, preferred_element_type=F32)
            return carry

        dqt[t] = jnp.zeros((DH, TILE), F32)
        in_steps(start, slots, (4, 2, 1), backward, jnp.int32(0))

    copies = [
        pltpu.make_async_copy(dqt, dqt_hbm, io_sems.at[0]),
        pltpu.make_async_copy(in_stats, stats_hbm, io_sems.at[2]),
    ]
    start_all(copies)
    wait_all(copies + send_sums(acc, out, out_refs, sems, g))


def own_grads_kernel(doc_ref, q_hbm, g_hbm, stats_hbm, dqt_hbm, *refs):
    piece_refs, (dq_hbm, *out_refs) = refs[:4], refs[4:7]
    (q_ref, g_ref, dq_ref, stats, dqt, win, kt, acc, out, sems, io_sems) = refs[7:]
    base = lax.axis_index("ctx") * 4
    g = lax.axis_index("grp")
    copies = [
        pltpu.make_async_copy(q_hbm, q_ref, io_sems.at[0]),
        pltpu.make_async_copy(g_hbm, g_ref, io_sems.at[1]),
        pltpu.make_async_copy(stats_hbm, stats, io_sems.at[2]),
        pltpu.make_async_copy(dqt_hbm, dqt, io_sems.at[3]),
    ] + window_copies(piece_refs, win, sems, g)
    start_all(copies)
    acc[...] = jnp.zeros_like(acc)
    wait_all(copies)
    half = TILE // 2

    @pl.loop(0, 4)
    def _(j):
        kt[:, rows_at(j)] = win[rows_at(j), :DH].T

    @pl.loop(0, 4)
    def _(t):
        q = q_ref[rows_at(t), :]
        go = g_ref[rows_at(t), :]
        qt = q.T
        gt = go.T
        ref = stats[t, 0:1, :]
        inv = stats[t, 1:2, :]
        delta = stats[t, 2:3, :]
        first = jnp.maximum(first_tile_of(doc_ref, doc_ref.shape[0], base + t) - base, 0)

        def add(at, low, ds, q, go):
            acc[at, DH:] += jnp.dot(low, go, preferred_element_type=F32)
            acc[at, :DH] += jnp.dot(ds, q, preferred_element_type=F32)

        def step(j, count, carry):
            at = rows_at(j, count)
            p = jnp.exp2(raw_scores(win[at, :DH], qt) - ref)
            dp = jnp.dot(win[at, DH:], gt, preferred_element_type=F32)
            low, ds = grads_of(p, dp, inv, delta)
            add(at, low, ds, q, go)
            dqt[t] += jnp.dot(kt[:, at], ds, preferred_element_type=F32)
            return carry

        in_steps(first, t, (3, 2, 1), step, jnp.int32(0))
        upper, lower, s0, s1 = diagonal_scores(win, t, qt)
        dp0 = jnp.dot(win[upper, DH:], gt, preferred_element_type=F32)
        dp1 = jnp.dot(win[lower, DH:], gt[:, half:], preferred_element_type=F32)
        low0, ds0 = grads_of(jnp.exp2(s0 - ref), dp0, inv, delta)
        low1, ds1 = grads_of(
            jnp.exp2(s1 - ref[:, half:]), dp1, inv[:, half:], delta[:, half:]
        )
        add(upper, low0, ds0, q, go)
        add(lower, low1, ds1, q[half:], go[half:])
        part = dqt[t] + jnp.dot(kt[:, upper], ds0, preferred_element_type=F32)
        part += widen_lanes(jnp.dot(kt[:, lower], ds1, preferred_element_type=F32))
        dq_ref[rows_at(t), :] = to_bf16((part * SCALE).T)

    copies = [pltpu.make_async_copy(dq_ref, dq_hbm, io_sems.at[0])]
    start_all(copies)
    wait_all(copies + send_sums(acc, out, out_refs, sems, g))


def up_ctx(x, by):
    n = lax.axis_size("ctx")
    return lax.ppermute(x, "ctx", [(i, (i + by) % n) for i in range(n)])


def down_ctx(x, by):
    n = lax.axis_size("ctx")
    return lax.ppermute(x, "ctx", [(i, i - by) for i in range(by, n)])


def swap_grp(x, bit):
    n = lax.axis_size("grp")
    return lax.ppermute(x, "grp", [(i, i ^ bit) for i in range(n)])


def four_tiles(x, y):
    return [x, swap_grp(x, 1), y, swap_grp(y, 1)]


def spans_blocks(doc_tiles, local_tiles):
    ids = jnp.arange(doc_tiles.shape[0])
    begins = jnp.sum(jnp.where(ids[None, :] < ids[:, None], doc_tiles[None, :], 0), axis=1)
    lasts = begins + doc_tiles - 1
    return jnp.max(lasts // local_tiles - begins // local_tiles)


def run_kernel(body, name, mib, out_shape, scratch, args):
    hbm = pl.BlockSpec(memory_space=pl.ANY)
    return pl.pallas_call(
        body,
        name=name,
        out_shape=out_shape,
        in_specs=[pl.BlockSpec(memory_space=pltpu.SMEM)] + [hbm] * (len(args) - 1),
        out_specs=jax.tree.map(lambda _: hbm, out_shape),
        scratch_shapes=scratch,
        compiler_params=pltpu.CompilerParams(vmem_limit_bytes=mib * 1024 * 1024),
    )(*args)


def rows_of(queries):
    return pltpu.VMEM(queries.shape, BF16)


def tiles(count, dtype):
    return pltpu.VMEM((count * TILE, 2 * DH), dtype)


def sums_by_core(blocks):
    return (jax.ShapeDtypeStruct((2, TILE, 2 * DH), BF16),) * (2 * blocks)


STATS = jax.ShapeDtypeStruct((4, 8, TILE), F32)


def with_window(queries, grad_out, doc_tiles, own_stats, pieces, *, reach):
    given = (doc_tiles, queries, grad_out)
    own_pieces, *far = pieces
    if reach == 3:
        x1, _, y1 = far[0]
        x3, y3 = up_ctx(x1, 2), up_ctx(y1, 2)
        far = far + [[x3, swap_grp(x3, 1), y3]]
    far = [block + [swap_grp(block[2], 1)] for block in far]
    far_pieces = [tile for block in reversed(far) for tile in block]
    rows = rows_of(queries)
    stats_rows = pltpu.VMEM(STATS.shape, F32)
    dqt = jax.ShapeDtypeStruct((4, DH, TILE), F32)
    slots = 4 * reach
    new_stats, far_dqt, *far_sums = run_kernel(
        functools.partial(far_kernel, reach), "far_blocks", 24 + 8 * reach,
        (STATS, dqt) + sums_by_core(reach),
        [
            rows, rows, stats_rows, pltpu.VMEM(dqt.shape, F32),
            tiles(slots, BF16), pltpu.VMEM((DH, slots * TILE), BF16),
            pltpu.VMEM((slots * TILE, TILE), F32), pltpu.VMEM((slots * TILE, TILE), F32),
            tiles(slots, F32), tiles(slots, BF16),
            pltpu.SemaphoreType.DMA((slots,)), pltpu.SemaphoreType.DMA((3,)),
        ],
        given + (own_stats, *far_pieces),
    )

    def over_cores(keep, send):
        return keep.astype(F32) + swap_grp(send, 1).astype(F32)

    mine, theirs = {}, {}
    for d in range(reach, 0, -1):
        both = over_cores(*far_sums[2 * (reach - d) : 2 * (reach - d) + 2])
        mine[d], theirs[d] = both[0], to_bf16(both if d == 2 else both[1])
    theirs, new_stats = lax.optimization_barrier((theirs, new_stats))
    grad_queries, *own_sums = run_kernel(
        own_grads_kernel, "own_grads", 24,
        (jax.ShapeDtypeStruct(queries.shape, BF16),) + sums_by_core(1),
        [
            rows, rows, rows, stats_rows, pltpu.VMEM(dqt.shape, F32),
            tiles(4, BF16), pltpu.VMEM((DH, 4 * TILE), BF16), tiles(4, F32), tiles(4, BF16),
            pltpu.SemaphoreType.DMA((4,)), pltpu.SemaphoreType.DMA((4,)),
        ],
        given + (new_stats, far_dqt, *own_pieces),
    )
    far = down_ctx(theirs[2], 2)
    near_theirs, own_sums = lax.optimization_barrier((swap_grp(theirs[1], 2), own_sums))
    both = over_cores(*own_sums) + far.astype(F32)
    own = both[0] + swap_grp(to_bf16(both[1]), 2).astype(F32)
    near = mine[1] + near_theirs.astype(F32)
    own = own + down_ctx(to_bf16(near), 1).astype(F32)
    if reach == 3:
        third = mine[3] + swap_grp(theirs[3], 2).astype(F32)
        own = own + down_ctx(to_bf16(third), 3).astype(F32)
    grad_kv = to_bf16(jnp.concatenate([own[:, :DH] * SCALE, own[:, DH:]], axis=1))
    return (grad_queries, grad_kv)


def shards(queries, kv_cache, grad_out, doc_tiles):
    local_tiles = queries.shape[0] // TILE
    most = (MAXT - 2) // local_tiles + 1
    assert (local_tiles, most, lax.axis_size("grp")) == (4, 3, 4)
    x0 = kv_cache
    spans = spans_blocks(doc_tiles, local_tiles)
    y0, spans = lax.optimization_barrier((swap_grp(x0, 2), spans))
    x1 = up_ctx(x0, 1)
    x2 = up_ctx(x0, 2)
    y1 = swap_grp(x1, 2)
    y0, x2 = lax.optimization_barrier((y0, x2))
    y2 = up_ctx(y0, 2)
    own_pieces = four_tiles(x0, y0)
    own_stats = run_kernel(
        own_stats_kernel, "own_stats", 24, STATS,
        [
            pltpu.VMEM(STATS.shape, F32), rows_of(queries), rows_of(queries), tiles(4, BF16),
            pltpu.SemaphoreType.DMA((4,)), pltpu.SemaphoreType.DMA((3,)),
        ],
        (doc_tiles, queries, grad_out, *own_pieces),
    )
    pieces = [own_pieces, [x1, swap_grp(x1, 1), y1], [x2, swap_grp(x2, 1), y2]]
    return lax.cond(
        spans >= most,
        lambda *args: with_window(*args, reach=most),
        lambda *args: with_window(*args, reach=most - 1),
        queries, grad_out, doc_tiles, own_stats, pieces,
    )


def solution(mesh):
    placed = (P("ctx", "grp"), P(("ctx", "grp"), None), P("ctx", "grp"), P())
    return jax.shard_map(
        shards,
        mesh=mesh,
        in_specs=placed,
        out_specs=(P("ctx", "grp"), P(("ctx", "grp"), None)),
        check_vma=False,
    )
```

```python
import math

import jax
import jax.numpy as jnp
from jax import lax
from jax.experimental import pallas as pl
from jax.experimental.pallas import tpu as pltpu
from jax.sharding import PartitionSpec as P

DH = 128
TILE = 512
MAXT = 12
NEG_FILL = -1e30
HUGE = 2.0**100
F32 = jnp.float32
BF16 = jnp.bfloat16


def to_bf16(x):
    return x.astype(BF16)


def fold_rows(x):
    return x.reshape(x.shape[0] // 8, 8, x.shape[1])


def first_tile_of(doc_ref, doc_count, tile):
    def step(d, carry):
        begin, found = carry
        found = jnp.where(begin <= tile, begin, found)
        return (begin + doc_ref[d], found)

    return lax.fori_loop(0, doc_count, step, (jnp.int32(0), jnp.int32(0)))[1]


def local_kernel(*refs, local_tiles, reach, scale):
    blocks = reach + 1
    doc_ref, q_hbm, g_hbm = refs[:3]
    piece_refs = refs[3 : 3 + 4 * blocks]
    dq_hbm = refs[3 + 4 * blocks]
    out_refs = refs[4 + 4 * blocks : 4 + 6 * blocks]
    q_ref, g_ref, dq_ref, win, kt, scores, dprobs, acc, dqt, sems, io_sems = refs[4 + 6 * blocks :]

    slots = blocks * local_tiles
    c = lax.axis_index("ctx")
    g = lax.axis_index("grp")
    base = (c - reach) * local_tiles
    to_log2 = scale * math.log2(math.e)

    def tile_rows(b, owner):
        return pl.ds(pl.multiple_of((b * local_tiles + owner) * TILE, TILE), TILE)

    copies = [
        pltpu.make_async_copy(q_hbm, q_ref, io_sems.at[0]),
        pltpu.make_async_copy(g_hbm, g_ref, io_sems.at[1]),
    ]
    for b in range(blocks):
        for i in range(4):
            copies.append(
                pltpu.make_async_copy(
                    piece_refs[4 * b + i], win.at[tile_rows(b, g ^ i)], sems.at[b, i]
                )
            )
    for copy in copies:
        copy.start()
    acc[...] = jnp.zeros_like(acc)
    for copy in copies:
        copy.wait()

    doc_count = doc_ref.shape[0]
    low = first_tile_of(doc_ref, doc_count, c * local_tiles) - base

    @pl.loop(low, slots)
    def _(j):
        tile = pl.ds(pl.multiple_of(j * TILE, TILE), TILE)
        kt[:, tile] = win[tile, :DH].T

    half = TILE // 2
    causal = lax.broadcasted_iota(jnp.int32, (half, half), 0) <= lax.broadcasted_iota(
        jnp.int32, (half, half), 1
    )

    def widen_lanes(x):
        return jnp.concatenate([jnp.zeros_like(x), x], axis=1)

    @pl.loop(0, local_tiles)
    def _(t):
        rows = pl.ds(pl.multiple_of(t * TILE, TILE), TILE)
        q = q_ref[rows, :]
        go = g_ref[rows, :]
        qt = q.T
        gt = go.T
        diag = reach * local_tiles + t
        first = first_tile_of(doc_ref, doc_count, c * local_tiles + t) - base

        def key_rows(j, count):
            return pl.ds(pl.multiple_of(j * TILE, TILE), count * TILE)

        def in_steps(step, carry, sizes=(4, 2, 1)):
            lo = first
            for size in sizes:
                steps = (diag - lo) // size
                carry = lax.fori_loop(
                    0, steps, lambda i, x, lo=lo, size=size: step(lo + i * size, size, x), carry
                )
                lo = lo + steps * size
            return carry

        def raw_scores(at, queries_t):
            return jnp.dot(win[at, :DH], queries_t, preferred_element_type=F32) * to_log2

        upper = pl.ds(pl.multiple_of(diag * TILE, half), half)
        lower = pl.ds(pl.multiple_of(diag * TILE + half, half), half)
        slot = diag - first
        upper_to = pl.ds(pl.multiple_of(slot * TILE, half), half)
        lower_to = pl.ds(pl.multiple_of(slot * TILE + half, half), half)

        def diag_scores():
            s0 = raw_scores(upper, qt)
            s0 = jnp.concatenate(
                [jnp.where(causal, s0[:, :half], NEG_FILL), s0[:, half:]], axis=1
            )
            s1 = jnp.where(causal, raw_scores(lower, qt[:, half:]), NEG_FILL)
            return s0, s1

        def column_sum(x):
            return jnp.sum(fold_rows(x), axis=0)

        def forward(ref, s0, s1, sizes=(4, 2, 1)):
            def step(j, count, total):
                p = jnp.exp2(raw_scores(key_rows(j, count), qt) - ref)
                scores[key_rows(j - first, count), :] = p
                return total + column_sum(p)

            p0 = jnp.exp2(s0 - ref)
            p1 = jnp.exp2(s1 - ref[:, half:])
            scores[upper_to, :] = p0
            scores[lower_to, half:] = p1
            total = column_sum(p0) + widen_lanes(column_sum(p1))
            return jnp.sum(in_steps(step, total, sizes), axis=0, keepdims=True)

        def diag_top(s0, s1):
            top0 = jnp.max(s0, axis=0, keepdims=True)
            top1 = jnp.max(s1, axis=0, keepdims=True)
            return jnp.concatenate(
                [top0[:, :half], jnp.maximum(top0[:, half:], top1)], axis=1
            )

        def exact():
            def step(j, count, top):
                s = raw_scores(key_rows(j, count), qt)
                return jnp.maximum(top, jnp.max(s, axis=0, keepdims=True))

            s0, s1 = diag_scores()
            return forward(in_steps(step, diag_top(s0, s1), (1,)), s0, s1, (1,))

        s0, s1 = diag_scores()
        total = forward(diag_top(s0, s1), s0, s1)
        fits = jnp.max(jnp.where(total < HUGE, 0.0, 1.0)) == 0.0
        inv = 1.0 / lax.cond(fits, lambda: total, exact)

        def part_of_delta(p, dp, inv):
            return column_sum(to_bf16(p * inv).astype(F32) * dp)

        def delta_step(j, count, delta):
            to = key_rows(j - first, count)
            dp = jnp.dot(win[key_rows(j, count), DH:], gt, preferred_element_type=F32)
            dprobs[to, :] = dp
            return delta + part_of_delta(scores[to, :], dp, inv)

        dp0 = jnp.dot(win[upper, DH:], gt, preferred_element_type=F32)
        dp1 = jnp.dot(win[lower, DH:], gt[:, half:], preferred_element_type=F32)
        dprobs[upper_to, :] = dp0
        dprobs[lower_to, half:] = dp1
        delta = part_of_delta(scores[upper_to, :], dp0, inv)
        delta += widen_lanes(part_of_delta(scores[lower_to, half:], dp1, inv[:, half:]))
        delta = jnp.sum(in_steps(delta_step, delta), axis=0, keepdims=True)
        dqt[...] = jnp.zeros_like(dqt)

        def grads(p, dp, inv, delta):
            p = p * inv
            return to_bf16(p), to_bf16(p * (dp - delta))

        def add_grads(at, low, ds, q, go):
            acc[at, DH:] += jnp.dot(low, go, preferred_element_type=F32)
            acc[at, :DH] += jnp.dot(ds, q, preferred_element_type=F32)

        def backward(j, count, carry):
            at = key_rows(j, count)
            to = key_rows(j - first, count)
            low, ds = grads(scores[to, :], dprobs[to, :], inv, delta)
            add_grads(at, low, ds, q, go)
            dqt[...] += jnp.dot(kt[:, at], ds, preferred_element_type=F32)
            return carry

        low0, ds0 = grads(scores[upper_to, :], dprobs[upper_to, :], inv, delta)
        low1, ds1 = grads(
            scores[lower_to, half:], dprobs[lower_to, half:], inv[:, half:], delta[:, half:]
        )
        add_grads(upper, low0, ds0, q, go)
        add_grads(lower, low1, ds1, q[half:], go[half:])
        dqt[...] = jnp.dot(kt[:, upper], ds0, preferred_element_type=F32)
        dqt[:, half:] += jnp.dot(kt[:, lower], ds1, preferred_element_type=F32)
        in_steps(backward, jnp.int32(0))
        dq_ref[rows, :] = to_bf16((dqt[...] * scale).T)

    copies = [pltpu.make_async_copy(dq_ref, dq_hbm, io_sems.at[0])]
    copies[0].start()
    for b in range(blocks):
        for i in range(4):
            at = tile_rows(b, g ^ i)
            win[at, :] = to_bf16(acc[at, :])
            copy = pltpu.make_async_copy(
                win.at[at], out_refs[2 * b + i % 2].at[i // 2], sems.at[b, i]
            )
            copy.start()
            copies.append(copy)
    for copy in copies:
        copy.wait()


def up_ctx(x, by):
    n = lax.axis_size("ctx")
    return lax.ppermute(x, "ctx", [(i, (i + by) % n) for i in range(n)])


def down_ctx(x, by):
    n = lax.axis_size("ctx")
    return lax.ppermute(x, "ctx", [(i, i - by) for i in range(by, n)])


def swap_grp(x, bit):
    n = lax.axis_size("grp")
    return lax.ppermute(x, "grp", [(i, i ^ bit) for i in range(n)])


def four_tiles(x, y):
    return [x, swap_grp(x, 1), y, swap_grp(y, 1)]


def spans_blocks(doc_tiles, local_tiles):
    ids = jnp.arange(doc_tiles.shape[0])
    begins = jnp.sum(jnp.where(ids[None, :] < ids[:, None], doc_tiles[None, :], 0), axis=1)
    lasts = begins + doc_tiles - 1
    return jnp.max(lasts // local_tiles - begins // local_tiles)


def with_window(queries, grad_out, doc_tiles, pieces, *, local_tiles, reach):
    blocks = reach + 1
    slots = blocks * local_tiles
    scale = 1.0 / math.sqrt(DH)
    width = 2 * DH

    own_pieces, *far = pieces
    if reach == 3:
        x3, y3 = up_ctx(far[0][0], 2), up_ctx(far[0][2], 2)
        far = far + [[x3, swap_grp(x3, 1), y3]]
    pieces = [own_pieces] + [block + [swap_grp(block[2], 1)] for block in far]
    pieces = [tile for block in reversed(pieces) for tile in block]

    hbm = pl.BlockSpec(memory_space=pl.ANY)
    half = jax.ShapeDtypeStruct((local_tiles // 2, TILE, width), BF16)
    grad_queries, *halves = pl.pallas_call(
        lambda *refs: local_kernel(*refs, local_tiles=local_tiles, reach=reach, scale=scale),
        out_shape=(jax.ShapeDtypeStruct(queries.shape, BF16),) + (half,) * (2 * blocks),
        in_specs=[pl.BlockSpec(memory_space=pltpu.SMEM)] + [hbm] * (2 + 4 * blocks),
        out_specs=(hbm,) * (1 + 2 * blocks),
        scratch_shapes=[
            pltpu.VMEM(queries.shape, BF16),
            pltpu.VMEM(queries.shape, BF16),
            pltpu.VMEM(queries.shape, BF16),
            pltpu.VMEM((slots * TILE, width), BF16),
            pltpu.VMEM((DH, slots * TILE), BF16),
            pltpu.VMEM((MAXT * TILE, TILE), F32),
            pltpu.VMEM((MAXT * TILE, TILE), F32),
            pltpu.VMEM((slots * TILE, width), F32),
            pltpu.VMEM((DH, TILE), F32),
            pltpu.SemaphoreType.DMA((blocks, 4)),
            pltpu.SemaphoreType.DMA((2,)),
        ],
        compiler_params=pltpu.CompilerParams(vmem_limit_bytes=(40 + 4 * reach) * 1024 * 1024),
    )(doc_tiles, queries, grad_out, *pieces)

    mine, theirs = {}, {}
    for d in range(reach, -1, -1):
        keep, send = halves[2 * (reach - d)], halves[2 * (reach - d) + 1]
        got = swap_grp(send, 1).astype(F32)
        mine[d] = keep[0].astype(F32) + got[0]
        theirs[d] = keep[1].astype(F32) + got[1]
    far_theirs = down_ctx(to_bf16(theirs[2]), 2).astype(F32)
    own = mine[0] + down_ctx(to_bf16(mine[2]), 2).astype(F32)
    own = own + swap_grp(to_bf16(theirs[0] + far_theirs), 2).astype(F32)
    for d in (1, 3)[: reach - 1]:
        block = mine[d] + swap_grp(to_bf16(theirs[d]), 2).astype(F32)
        own = own + down_ctx(to_bf16(block), d).astype(F32)
    grad_kv = to_bf16(jnp.concatenate([own[:, :DH] * scale, own[:, DH:]], axis=1))
    return (grad_queries, grad_kv)


def shards(queries, kv_cache, grad_out, doc_tiles):
    local_tiles = queries.shape[0] // TILE
    most = (MAXT - 2) // local_tiles + 1
    assert most == 3
    x0 = kv_cache
    spans = spans_blocks(doc_tiles, local_tiles)
    y0, spans = lax.optimization_barrier((swap_grp(x0, 2), spans))
    x1 = up_ctx(x0, 1)
    x2 = up_ctx(x0, 2)
    y1 = swap_grp(x1, 2)
    y2 = up_ctx(y0, 2)
    pieces = [four_tiles(x0, y0), [x1, swap_grp(x1, 1), y1], [x2, swap_grp(x2, 1), y2]]
    return lax.cond(
        spans >= most,
        lambda *args: with_window(*args, local_tiles=local_tiles, reach=most),
        lambda *args: with_window(*args, local_tiles=local_tiles, reach=most - 1),
        queries, grad_out, doc_tiles, pieces,
    )


def solution(mesh):
    placed = (P("ctx", "grp"), P(("ctx", "grp"), None), P("ctx", "grp"), P())
    return jax.shard_map(
        shards,
        mesh=mesh,
        in_specs=placed,
        out_specs=(P("ctx", "grp"), P(("ctx", "grp"), None)),
        check_vma=False,
    )
```

```python
import math

import jax
import jax.numpy as jnp
from jax import lax
from jax.experimental import pallas as pl
from jax.experimental.pallas import tpu as pltpu
from jax.sharding import PartitionSpec as P

DH = 128
TILE = 512
MAXT = 12
NEG_FILL = -1e30
HUGE = 2.0**100
F32 = jnp.float32
BF16 = jnp.bfloat16


def to_bf16(x):
    return x.astype(BF16)


def fold_rows(x):
    return x.reshape(x.shape[0] // 8, 8, x.shape[1])


def first_tile_of(doc_ref, doc_count, tile):
    def step(d, carry):
        begin, found = carry
        found = jnp.where(begin <= tile, begin, found)
        return (begin + doc_ref[d], found)

    return lax.fori_loop(0, doc_count, step, (jnp.int32(0), jnp.int32(0)))[1]


def local_kernel(*refs, local_tiles, reach, scale):
    blocks = reach + 1
    doc_ref, q_hbm, g_hbm = refs[:3]
    piece_refs = refs[3 : 3 + 4 * blocks]
    dq_hbm = refs[3 + 4 * blocks]
    out_refs = refs[4 + 4 * blocks : 4 + 6 * blocks]
    q_ref, g_ref, dq_ref, win, kt, scores, dprobs, acc, dqt, sems, io_sems = refs[4 + 6 * blocks :]

    slots = blocks * local_tiles
    c = lax.axis_index("ctx")
    g = lax.axis_index("grp")
    base = (c - reach) * local_tiles
    to_log2 = scale * math.log2(math.e)

    def tile_rows(b, owner):
        return pl.ds(pl.multiple_of((b * local_tiles + owner) * TILE, TILE), TILE)

    copies = [
        pltpu.make_async_copy(q_hbm, q_ref, io_sems.at[0]),
        pltpu.make_async_copy(g_hbm, g_ref, io_sems.at[1]),
    ]
    for b in range(blocks):
        for i in range(4):
            copies.append(
                pltpu.make_async_copy(
                    piece_refs[4 * b + i], win.at[tile_rows(b, g ^ i)], sems.at[b, i]
                )
            )
    for copy in copies:
        copy.start()
    acc[...] = jnp.zeros_like(acc)
    for copy in copies:
        copy.wait()

    doc_count = doc_ref.shape[0]
    low = first_tile_of(doc_ref, doc_count, c * local_tiles) - base

    @pl.loop(low, slots)
    def _(j):
        tile = pl.ds(pl.multiple_of(j * TILE, TILE), TILE)
        kt[:, tile] = win[tile, :DH].T

    half = TILE // 2
    causal = lax.broadcasted_iota(jnp.int32, (half, half), 0) <= lax.broadcasted_iota(
        jnp.int32, (half, half), 1
    )

    def widen_lanes(x):
        return jnp.concatenate([jnp.zeros_like(x), x], axis=1)

    @pl.loop(0, local_tiles)
    def _(t):
        rows = pl.ds(pl.multiple_of(t * TILE, TILE), TILE)
        q = q_ref[rows, :]
        go = g_ref[rows, :]
        qt = q.T
        gt = go.T
        diag = reach * local_tiles + t
        first = first_tile_of(doc_ref, doc_count, c * local_tiles + t) - base

        def key_rows(j, count):
            return pl.ds(pl.multiple_of(j * TILE, TILE), count * TILE)

        def in_steps(step, carry, sizes=(4, 2, 1)):
            lo = first
            for size in sizes:
                steps = (diag - lo) // size
                carry = lax.fori_loop(
                    0, steps, lambda i, x, lo=lo, size=size: step(lo + i * size, size, x), carry
                )
                lo = lo + steps * size
            return carry

        def raw_scores(at, queries_t):
            return jnp.dot(win[at, :DH], queries_t, preferred_element_type=F32) * to_log2

        upper = pl.ds(pl.multiple_of(diag * TILE, half), half)
        lower = pl.ds(pl.multiple_of(diag * TILE + half, half), half)
        slot = diag - first
        upper_to = pl.ds(pl.multiple_of(slot * TILE, half), half)
        lower_to = pl.ds(pl.multiple_of(slot * TILE + half, half), half)

        def diag_scores():
            s0 = raw_scores(upper, qt)
            s0 = jnp.concatenate(
                [jnp.where(causal, s0[:, :half], NEG_FILL), s0[:, half:]], axis=1
            )
            s1 = jnp.where(causal, raw_scores(lower, qt[:, half:]), NEG_FILL)
            return s0, s1

        def column_sum(x):
            return jnp.sum(fold_rows(x), axis=0)

        def forward(ref, s0, s1, sizes=(4, 2, 1)):
            def step(j, count, total):
                p = jnp.exp2(raw_scores(key_rows(j, count), qt) - ref)
                scores[key_rows(j - first, count), :] = p
                return total + column_sum(p)

            p0 = jnp.exp2(s0 - ref)
            p1 = jnp.exp2(s1 - ref[:, half:])
            scores[upper_to, :] = p0
            scores[lower_to, half:] = p1
            total = column_sum(p0) + widen_lanes(column_sum(p1))
            return jnp.sum(in_steps(step, total, sizes), axis=0, keepdims=True)

        def diag_top(s0, s1):
            top0 = jnp.max(s0, axis=0, keepdims=True)
            top1 = jnp.max(s1, axis=0, keepdims=True)
            return jnp.concatenate(
                [top0[:, :half], jnp.maximum(top0[:, half:], top1)], axis=1
            )

        def exact():
            def step(j, count, top):
                s = raw_scores(key_rows(j, count), qt)
                return jnp.maximum(top, jnp.max(s, axis=0, keepdims=True))

            s0, s1 = diag_scores()
            return forward(in_steps(step, diag_top(s0, s1), (1,)), s0, s1, (1,))

        s0, s1 = diag_scores()
        total = forward(diag_top(s0, s1), s0, s1)
        fits = jnp.max(jnp.where(total < HUGE, 0.0, 1.0)) == 0.0
        inv = 1.0 / lax.cond(fits, lambda: total, exact)

        def part_of_delta(p, dp, inv):
            return column_sum(to_bf16(p * inv).astype(F32) * dp)

        def delta_step(j, count, delta):
            to = key_rows(j - first, count)
            dp = jnp.dot(win[key_rows(j, count), DH:], gt, preferred_element_type=F32)
            dprobs[to, :] = dp
            return delta + part_of_delta(scores[to, :], dp, inv)

        dp0 = jnp.dot(win[upper, DH:], gt, preferred_element_type=F32)
        dp1 = jnp.dot(win[lower, DH:], gt[:, half:], preferred_element_type=F32)
        dprobs[upper_to, :] = dp0
        dprobs[lower_to, half:] = dp1
        delta = part_of_delta(scores[upper_to, :], dp0, inv)
        delta += widen_lanes(part_of_delta(scores[lower_to, half:], dp1, inv[:, half:]))
        delta = jnp.sum(in_steps(delta_step, delta), axis=0, keepdims=True)
        dqt[...] = jnp.zeros_like(dqt)

        def grads(p, dp, inv, delta):
            p = p * inv
            return to_bf16(p), to_bf16(p * (dp - delta))

        def add_grads(at, low, ds, q, go):
            acc[at, DH:] += jnp.dot(low, go, preferred_element_type=F32)
            acc[at, :DH] += jnp.dot(ds, q, preferred_element_type=F32)

        def backward(j, count, carry):
            at = key_rows(j, count)
            to = key_rows(j - first, count)
            low, ds = grads(scores[to, :], dprobs[to, :], inv, delta)
            add_grads(at, low, ds, q, go)
            dqt[...] += jnp.dot(kt[:, at], ds, preferred_element_type=F32)
            return carry

        low0, ds0 = grads(scores[upper_to, :], dprobs[upper_to, :], inv, delta)
        low1, ds1 = grads(
            scores[lower_to, half:], dprobs[lower_to, half:], inv[:, half:], delta[:, half:]
        )
        add_grads(upper, low0, ds0, q, go)
        add_grads(lower, low1, ds1, q[half:], go[half:])
        dqt[...] = jnp.dot(kt[:, upper], ds0, preferred_element_type=F32)
        dqt[:, half:] += jnp.dot(kt[:, lower], ds1, preferred_element_type=F32)
        in_steps(backward, jnp.int32(0))
        dq_ref[rows, :] = to_bf16((dqt[...] * scale).T)

    copies = [pltpu.make_async_copy(dq_ref, dq_hbm, io_sems.at[0])]
    copies[0].start()
    for b in range(blocks):
        for i in range(4):
            at = tile_rows(b, g ^ i)
            win[at, :] = to_bf16(acc[at, :])
            copy = pltpu.make_async_copy(
                win.at[at], out_refs[2 * b + i % 2].at[i // 2], sems.at[b, i]
            )
            copy.start()
            copies.append(copy)
    for copy in copies:
        copy.wait()


def up_ctx(x, by):
    n = lax.axis_size("ctx")
    return lax.ppermute(x, "ctx", [(i, (i + by) % n) for i in range(n)])


def down_ctx(x, by):
    n = lax.axis_size("ctx")
    return lax.ppermute(x, "ctx", [(i, i - by) for i in range(by, n)])


def swap_grp(x, bit):
    n = lax.axis_size("grp")
    return lax.ppermute(x, "grp", [(i, i ^ bit) for i in range(n)])


def four_tiles(x, y):
    return [x, swap_grp(x, 1), y, swap_grp(y, 1)]


def spans_blocks(doc_tiles, local_tiles):
    ids = jnp.arange(doc_tiles.shape[0])
    begins = jnp.sum(jnp.where(ids[None, :] < ids[:, None], doc_tiles[None, :], 0), axis=1)
    lasts = begins + doc_tiles - 1
    return jnp.max(lasts // local_tiles - begins // local_tiles)


def with_window(queries, grad_out, doc_tiles, pieces, *, local_tiles, reach):
    blocks = reach + 1
    slots = blocks * local_tiles
    scale = 1.0 / math.sqrt(DH)
    width = 2 * DH

    if reach == 3:
        x1, y1 = pieces[1]
        pieces = pieces + [(up_ctx(x1, 2), up_ctx(y1, 2))]
    pieces = [four_tiles(x, y) for x, y in pieces]
    pieces = [tile for block in reversed(pieces) for tile in block]

    hbm = pl.BlockSpec(memory_space=pl.ANY)
    half = jax.ShapeDtypeStruct((local_tiles // 2, TILE, width), BF16)
    grad_queries, *halves = pl.pallas_call(
        lambda *refs: local_kernel(*refs, local_tiles=local_tiles, reach=reach, scale=scale),
        out_shape=(jax.ShapeDtypeStruct(queries.shape, BF16),) + (half,) * (2 * blocks),
        in_specs=[pl.BlockSpec(memory_space=pltpu.SMEM)] + [hbm] * (2 + 4 * blocks),
        out_specs=(hbm,) * (1 + 2 * blocks),
        scratch_shapes=[
            pltpu.VMEM(queries.shape, BF16),
            pltpu.VMEM(queries.shape, BF16),
            pltpu.VMEM(queries.shape, BF16),
            pltpu.VMEM((slots * TILE, width), BF16),
            pltpu.VMEM((DH, slots * TILE), BF16),
            pltpu.VMEM((MAXT * TILE, TILE), F32),
            pltpu.VMEM((MAXT * TILE, TILE), F32),
            pltpu.VMEM((slots * TILE, width), F32),
            pltpu.VMEM((DH, TILE), F32),
            pltpu.SemaphoreType.DMA((blocks, 4)),
            pltpu.SemaphoreType.DMA((2,)),
        ],
        compiler_params=pltpu.CompilerParams(vmem_limit_bytes=(40 + 4 * reach) * 1024 * 1024),
    )(doc_tiles, queries, grad_out, *pieces)

    mine, theirs = {}, {}
    for d in range(reach, -1, -1):
        keep, send = halves[2 * (reach - d)], halves[2 * (reach - d) + 1]
        got = swap_grp(send, 1).astype(F32)
        mine[d] = keep[0].astype(F32) + got[0]
        theirs[d] = keep[1].astype(F32) + got[1]
    far_theirs = down_ctx(to_bf16(theirs[2]), 2).astype(F32)
    own = mine[0] + down_ctx(to_bf16(mine[2]), 2).astype(F32)
    own = own + swap_grp(to_bf16(theirs[0] + far_theirs), 2).astype(F32)
    near = to_bf16(theirs[1])
    if reach == 3:
        got, near = lax.optimization_barrier((swap_grp(to_bf16(theirs[3]), 2), near))
        own = own + down_ctx(to_bf16(mine[3] + got.astype(F32)), 3).astype(F32)
    near = mine[1] + swap_grp(near, 2).astype(F32)
    own = own + down_ctx(to_bf16(near), 1).astype(F32)
    grad_kv = to_bf16(jnp.concatenate([own[:, :DH] * scale, own[:, DH:]], axis=1))
    return (grad_queries, grad_kv)


def shards(queries, kv_cache, grad_out, doc_tiles):
    local_tiles = queries.shape[0] // TILE
    most = (MAXT - 2) // local_tiles + 1
    assert most == 3
    x0 = kv_cache
    spans = spans_blocks(doc_tiles, local_tiles)
    y0, spans = lax.optimization_barrier((swap_grp(x0, 2), spans))
    x1 = up_ctx(x0, 1)
    x2 = up_ctx(x0, 2)
    y1 = swap_grp(x1, 2)
    y2 = up_ctx(y0, 2)
    pieces = [(x0, y0), (x1, y1), (x2, y2)]
    return lax.cond(
        spans >= most,
        lambda *args: with_window(*args, local_tiles=local_tiles, reach=most),
        lambda *args: with_window(*args, local_tiles=local_tiles, reach=most - 1),
        queries, grad_out, doc_tiles, pieces,
    )


def solution(mesh):
    placed = (P("ctx", "grp"), P(("ctx", "grp"), None), P("ctx", "grp"), P())
    return jax.shard_map(
        shards,
        mesh=mesh,
        in_specs=placed,
        out_specs=(P("ctx", "grp"), P(("ctx", "grp"), None)),
        check_vma=False,
    )
```

```python
import math

import jax
import jax.numpy as jnp
from jax import lax
from jax.experimental import pallas as pl
from jax.experimental.pallas import tpu as pltpu
from jax.sharding import PartitionSpec as P

DH = 128
TILE = 512
MAXT = 12
NEG_FILL = -1e30
HUGE = 2.0**100
F32 = jnp.float32
BF16 = jnp.bfloat16


def to_bf16(x):
    return x.astype(BF16)


def fold_rows(x):
    return x.reshape(x.shape[0] // 8, 8, x.shape[1])


def first_tile_of(doc_ref, doc_count, tile):
    def step(d, carry):
        begin, found = carry
        found = jnp.where(begin <= tile, begin, found)
        return (begin + doc_ref[d], found)

    return lax.fori_loop(0, doc_count, step, (jnp.int32(0), jnp.int32(0)))[1]


def local_kernel(*refs, local_tiles, reach, scale):
    blocks = reach + 1
    doc_ref, q_hbm, g_hbm = refs[:3]
    piece_refs = refs[3 : 3 + 4 * blocks]
    dq_hbm = refs[3 + 4 * blocks]
    out_refs = refs[4 + 4 * blocks : 4 + 6 * blocks]
    q_ref, g_ref, dq_ref, win, kt, scores, dprobs, acc, dqt, sems, io_sems = refs[4 + 6 * blocks :]

    slots = blocks * local_tiles
    c = lax.axis_index("ctx")
    g = lax.axis_index("grp")
    base = (c - reach) * local_tiles
    to_log2 = scale * math.log2(math.e)

    def tile_rows(b, owner):
        return pl.ds(pl.multiple_of((b * local_tiles + owner) * TILE, TILE), TILE)

    copies = [
        pltpu.make_async_copy(q_hbm, q_ref, io_sems.at[0]),
        pltpu.make_async_copy(g_hbm, g_ref, io_sems.at[1]),
    ]
    for b in range(blocks):
        for i in range(4):
            copies.append(
                pltpu.make_async_copy(
                    piece_refs[4 * b + i], win.at[tile_rows(b, g ^ i)], sems.at[b, i]
                )
            )
    for copy in copies:
        copy.start()
    acc[...] = jnp.zeros_like(acc)
    for copy in copies:
        copy.wait()

    doc_count = doc_ref.shape[0]
    low = first_tile_of(doc_ref, doc_count, c * local_tiles) - base

    @pl.loop(low, slots)
    def _(j):
        tile = pl.ds(pl.multiple_of(j * TILE, TILE), TILE)
        kt[:, tile] = win[tile, :DH].T

    half = TILE // 2
    causal = lax.broadcasted_iota(jnp.int32, (half, half), 0) <= lax.broadcasted_iota(
        jnp.int32, (half, half), 1
    )

    def widen_lanes(x):
        return jnp.concatenate([jnp.zeros_like(x), x], axis=1)

    @pl.loop(0, local_tiles)
    def _(t):
        rows = pl.ds(pl.multiple_of(t * TILE, TILE), TILE)
        q = q_ref[rows, :]
        go = g_ref[rows, :]
        qt = q.T
        gt = go.T
        diag = reach * local_tiles + t
        first = first_tile_of(doc_ref, doc_count, c * local_tiles + t) - base

        def key_rows(j, count):
            return pl.ds(pl.multiple_of(j * TILE, TILE), count * TILE)

        def in_steps(step, carry, sizes=(4, 2, 1)):
            lo = first
            for size in sizes:
                steps = (diag - lo) // size
                carry = lax.fori_loop(
                    0, steps, lambda i, x, lo=lo, size=size: step(lo + i * size, size, x), carry
                )
                lo = lo + steps * size
            return carry

        def raw_scores(at, queries_t):
            return jnp.dot(win[at, :DH], queries_t, preferred_element_type=F32) * to_log2

        upper = pl.ds(pl.multiple_of(diag * TILE, half), half)
        lower = pl.ds(pl.multiple_of(diag * TILE + half, half), half)
        slot = diag - first
        upper_to = pl.ds(pl.multiple_of(slot * TILE, half), half)
        lower_to = pl.ds(pl.multiple_of(slot * TILE + half, half), half)

        def diag_scores():
            s0 = raw_scores(upper, qt)
            s0 = jnp.concatenate(
                [jnp.where(causal, s0[:, :half], NEG_FILL), s0[:, half:]], axis=1
            )
            s1 = jnp.where(causal, raw_scores(lower, qt[:, half:]), NEG_FILL)
            return s0, s1

        def column_sum(x):
            return jnp.sum(fold_rows(x), axis=0)

        def forward(ref, s0, s1, sizes=(4, 2, 1)):
            def step(j, count, total):
                p = jnp.exp2(raw_scores(key_rows(j, count), qt) - ref)
                scores[key_rows(j - first, count), :] = p
                return total + column_sum(p)

            p0 = jnp.exp2(s0 - ref)
            p1 = jnp.exp2(s1 - ref[:, half:])
            scores[upper_to, :] = p0
            scores[lower_to, half:] = p1
            total = column_sum(p0) + widen_lanes(column_sum(p1))
            return jnp.sum(in_steps(step, total, sizes), axis=0, keepdims=True)

        def diag_top(s0, s1):
            top0 = jnp.max(s0, axis=0, keepdims=True)
            top1 = jnp.max(s1, axis=0, keepdims=True)
            return jnp.concatenate(
                [top0[:, :half], jnp.maximum(top0[:, half:], top1)], axis=1
            )

        def exact():
            def step(j, count, top):
                s = raw_scores(key_rows(j, count), qt)
                return jnp.maximum(top, jnp.max(s, axis=0, keepdims=True))

            s0, s1 = diag_scores()
            return forward(in_steps(step, diag_top(s0, s1), (1,)), s0, s1, (1,))

        s0, s1 = diag_scores()
        total = forward(diag_top(s0, s1), s0, s1)
        fits = jnp.max(jnp.where(total < HUGE, 0.0, 1.0)) == 0.0
        inv = 1.0 / lax.cond(fits, lambda: total, exact)

        def part_of_delta(p, dp, inv):
            return column_sum(to_bf16(p * inv).astype(F32) * dp)

        def delta_step(j, count, delta):
            to = key_rows(j - first, count)
            dp = jnp.dot(win[key_rows(j, count), DH:], gt, preferred_element_type=F32)
            dprobs[to, :] = dp
            return delta + part_of_delta(scores[to, :], dp, inv)

        dp0 = jnp.dot(win[upper, DH:], gt, preferred_element_type=F32)
        dp1 = jnp.dot(win[lower, DH:], gt[:, half:], preferred_element_type=F32)
        dprobs[upper_to, :] = dp0
        dprobs[lower_to, half:] = dp1
        delta = part_of_delta(scores[upper_to, :], dp0, inv)
        delta += widen_lanes(part_of_delta(scores[lower_to, half:], dp1, inv[:, half:]))
        delta = jnp.sum(in_steps(delta_step, delta), axis=0, keepdims=True)
        dqt[...] = jnp.zeros_like(dqt)

        def grads(p, dp, inv, delta):
            p = p * inv
            return to_bf16(p), to_bf16(p * (dp - delta))

        def add_grads(at, low, ds, q, go):
            acc[at, DH:] += jnp.dot(low, go, preferred_element_type=F32)
            acc[at, :DH] += jnp.dot(ds, q, preferred_element_type=F32)

        def backward(j, count, carry):
            at = key_rows(j, count)
            to = key_rows(j - first, count)
            low, ds = grads(scores[to, :], dprobs[to, :], inv, delta)
            add_grads(at, low, ds, q, go)
            dqt[...] += jnp.dot(kt[:, at], ds, preferred_element_type=F32)
            return carry

        low0, ds0 = grads(scores[upper_to, :], dprobs[upper_to, :], inv, delta)
        low1, ds1 = grads(
            scores[lower_to, half:], dprobs[lower_to, half:], inv[:, half:], delta[:, half:]
        )
        add_grads(upper, low0, ds0, q, go)
        add_grads(lower, low1, ds1, q[half:], go[half:])
        dqt[...] = jnp.dot(kt[:, upper], ds0, preferred_element_type=F32)
        dqt[:, half:] += jnp.dot(kt[:, lower], ds1, preferred_element_type=F32)
        in_steps(backward, jnp.int32(0))
        dq_ref[rows, :] = to_bf16((dqt[...] * scale).T)

    copies = [pltpu.make_async_copy(dq_ref, dq_hbm, io_sems.at[0])]
    copies[0].start()
    for b in range(blocks):
        for i in range(4):
            at = tile_rows(b, g ^ i)
            win[at, :] = to_bf16(acc[at, :])
            copy = pltpu.make_async_copy(
                win.at[at], out_refs[2 * b + i % 2].at[i // 2], sems.at[b, i]
            )
            copy.start()
            copies.append(copy)
    for copy in copies:
        copy.wait()


def up_ctx(x, by):
    n = lax.axis_size("ctx")
    return lax.ppermute(x, "ctx", [(i, (i + by) % n) for i in range(n)])


def down_ctx(x, by):
    n = lax.axis_size("ctx")
    return lax.ppermute(x, "ctx", [(i, i - by) for i in range(by, n)])


def swap_grp(x, bit):
    n = lax.axis_size("grp")
    return lax.ppermute(x, "grp", [(i, i ^ bit) for i in range(n)])


def four_tiles(x, y):
    return [x, swap_grp(x, 1), y, swap_grp(y, 1)]


def spans_blocks(doc_tiles, local_tiles):
    ids = jnp.arange(doc_tiles.shape[0])
    begins = jnp.sum(jnp.where(ids[None, :] < ids[:, None], doc_tiles[None, :], 0), axis=1)
    lasts = begins + doc_tiles - 1
    return jnp.max(lasts // local_tiles - begins // local_tiles)


def with_window(queries, grad_out, doc_tiles, pieces, *, local_tiles, reach):
    blocks = reach + 1
    slots = blocks * local_tiles
    scale = 1.0 / math.sqrt(DH)
    width = 2 * DH

    *pieces, (x3, _) = pieces
    if reach == 3:
        pieces.append((x3, swap_grp(x3, 2)))
    pieces = [four_tiles(x, y) for x, y in pieces]
    pieces = [tile for block in reversed(pieces) for tile in block]

    hbm = pl.BlockSpec(memory_space=pl.ANY)
    half = jax.ShapeDtypeStruct((local_tiles // 2, TILE, width), BF16)
    grad_queries, *halves = pl.pallas_call(
        lambda *refs: local_kernel(*refs, local_tiles=local_tiles, reach=reach, scale=scale),
        out_shape=(jax.ShapeDtypeStruct(queries.shape, BF16),) + (half,) * (2 * blocks),
        in_specs=[pl.BlockSpec(memory_space=pltpu.SMEM)] + [hbm] * (2 + 4 * blocks),
        out_specs=(hbm,) * (1 + 2 * blocks),
        scratch_shapes=[
            pltpu.VMEM(queries.shape, BF16),
            pltpu.VMEM(queries.shape, BF16),
            pltpu.VMEM(queries.shape, BF16),
            pltpu.VMEM((slots * TILE, width), BF16),
            pltpu.VMEM((DH, slots * TILE), BF16),
            pltpu.VMEM((MAXT * TILE, TILE), F32),
            pltpu.VMEM((MAXT * TILE, TILE), F32),
            pltpu.VMEM((slots * TILE, width), F32),
            pltpu.VMEM((DH, TILE), F32),
            pltpu.SemaphoreType.DMA((blocks, 4)),
            pltpu.SemaphoreType.DMA((2,)),
        ],
        compiler_params=pltpu.CompilerParams(vmem_limit_bytes=(40 + 4 * reach) * 1024 * 1024),
    )(doc_tiles, queries, grad_out, *pieces)

    mine, theirs = {}, {}
    for d in range(reach, -1, -1):
        keep, send = halves[2 * (reach - d)], halves[2 * (reach - d) + 1]
        got = swap_grp(send, 1).astype(F32)
        mine[d] = keep[0].astype(F32) + got[0]
        theirs[d] = keep[1].astype(F32) + got[1]
    far_theirs = down_ctx(to_bf16(theirs[2]), 2).astype(F32)
    own = mine[0] + down_ctx(to_bf16(mine[2]), 2).astype(F32)
    own = own + swap_grp(to_bf16(theirs[0] + far_theirs), 2).astype(F32)
    near = to_bf16(theirs[1])
    if reach == 3:
        got, near = lax.optimization_barrier((swap_grp(to_bf16(theirs[3]), 2), near))
        own = own + down_ctx(to_bf16(mine[3] + got.astype(F32)), 3).astype(F32)
    near = mine[1] + swap_grp(near, 2).astype(F32)
    own = own + down_ctx(to_bf16(near), 1).astype(F32)
    grad_kv = to_bf16(jnp.concatenate([own[:, :DH] * scale, own[:, DH:]], axis=1))
    return (grad_queries, grad_kv)


def shards(queries, kv_cache, grad_out, doc_tiles):
    local_tiles = queries.shape[0] // TILE
    most = (MAXT - 2) // local_tiles + 1
    assert most == 3
    half = TILE // 2
    x0 = kv_cache
    spans = spans_blocks(doc_tiles, local_tiles)
    y0, spans = lax.optimization_barrier((swap_grp(x0, 2), spans))
    x1 = up_ctx(x0, 1)
    x2 = up_ctx(x0, 2)
    y1 = swap_grp(x1, 2)
    y2 = jnp.concatenate([up_ctx(y0[:half], 2), swap_grp(x2[half:], 2)])
    x3 = lax.cond(spans >= most, lambda x: up_ctx(x, 2), lambda x: x, x1)
    pieces = [(x0, y0), (x1, y1), (x2, y2), (x3, x3)]
    return lax.cond(
        spans >= most,
        lambda *args: with_window(*args, local_tiles=local_tiles, reach=most),
        lambda *args: with_window(*args, local_tiles=local_tiles, reach=most - 1),
        queries, grad_out, doc_tiles, pieces,
    )


def solution(mesh):
    placed = (P("ctx", "grp"), P(("ctx", "grp"), None), P("ctx", "grp"), P())
    return jax.shard_map(
        shards,
        mesh=mesh,
        in_specs=placed,
        out_specs=(P("ctx", "grp"), P(("ctx", "grp"), None)),
        check_vma=False,
    )
```

```python
import math

import jax
import jax.numpy as jnp
from jax import lax
from jax.experimental import pallas as pl
from jax.experimental.pallas import tpu as pltpu
from jax.sharding import PartitionSpec as P

DH = 128
TILE = 512
MAXT = 12
NEG_FILL = -1e30
HUGE = 2.0**100
F32 = jnp.float32
BF16 = jnp.bfloat16


def to_bf16(x):
    return x.astype(BF16)


def fold_rows(x):
    return x.reshape(x.shape[0] // 8, 8, x.shape[1])


def first_tile_of(doc_ref, doc_count, tile):
    def step(d, carry):
        begin, found = carry
        found = jnp.where(begin <= tile, begin, found)
        return (begin + doc_ref[d], found)

    return lax.fori_loop(0, doc_count, step, (jnp.int32(0), jnp.int32(0)))[1]


def local_kernel(*refs, local_tiles, reach, scale):
    blocks = reach + 1
    doc_ref, q_hbm, g_hbm = refs[:3]
    piece_refs = refs[3 : 3 + 4 * blocks]
    dq_hbm = refs[3 + 4 * blocks]
    out_refs = refs[4 + 4 * blocks : 4 + 6 * blocks]
    q_ref, g_ref, dq_ref, win, kt, scores, dprobs, acc, dqt, sems, io_sems = refs[4 + 6 * blocks :]

    slots = blocks * local_tiles
    c = lax.axis_index("ctx")
    g = lax.axis_index("grp")
    base = (c - reach) * local_tiles
    to_log2 = scale * math.log2(math.e)

    def tile_rows(b, owner):
        return pl.ds(pl.multiple_of((b * local_tiles + owner) * TILE, TILE), TILE)

    copies = [
        pltpu.make_async_copy(q_hbm, q_ref, io_sems.at[0]),
        pltpu.make_async_copy(g_hbm, g_ref, io_sems.at[1]),
    ]
    for b in range(blocks):
        for i in range(4):
            copies.append(
                pltpu.make_async_copy(
                    piece_refs[4 * b + i], win.at[tile_rows(b, g ^ i)], sems.at[b, i]
                )
            )
    for copy in copies:
        copy.start()
    acc[...] = jnp.zeros_like(acc)
    for copy in copies:
        copy.wait()

    doc_count = doc_ref.shape[0]
    low = first_tile_of(doc_ref, doc_count, c * local_tiles) - base

    @pl.loop(low, slots)
    def _(j):
        tile = pl.ds(pl.multiple_of(j * TILE, TILE), TILE)
        kt[:, tile] = win[tile, :DH].T

    half = TILE // 2
    causal = lax.broadcasted_iota(jnp.int32, (half, half), 0) <= lax.broadcasted_iota(
        jnp.int32, (half, half), 1
    )

    def widen_lanes(x):
        return jnp.concatenate([jnp.zeros_like(x), x], axis=1)

    @pl.loop(0, local_tiles)
    def _(t):
        rows = pl.ds(pl.multiple_of(t * TILE, TILE), TILE)
        q = q_ref[rows, :]
        go = g_ref[rows, :]
        qt = q.T
        gt = go.T
        diag = reach * local_tiles + t
        first = first_tile_of(doc_ref, doc_count, c * local_tiles + t) - base

        def key_rows(j, count):
            return pl.ds(pl.multiple_of(j * TILE, TILE), count * TILE)

        def in_steps(step, carry, sizes=(4, 2, 1)):
            lo = first
            for size in sizes:
                steps = (diag - lo) // size
                carry = lax.fori_loop(
                    0, steps, lambda i, x, lo=lo, size=size: step(lo + i * size, size, x), carry
                )
                lo = lo + steps * size
            return carry

        def raw_scores(at, queries_t):
            return jnp.dot(win[at, :DH], queries_t, preferred_element_type=F32) * to_log2

        upper = pl.ds(pl.multiple_of(diag * TILE, half), half)
        lower = pl.ds(pl.multiple_of(diag * TILE + half, half), half)
        slot = diag - first
        upper_to = pl.ds(pl.multiple_of(slot * TILE, half), half)
        lower_to = pl.ds(pl.multiple_of(slot * TILE + half, half), half)

        def diag_scores():
            s0 = raw_scores(upper, qt)
            s0 = jnp.concatenate(
                [jnp.where(causal, s0[:, :half], NEG_FILL), s0[:, half:]], axis=1
            )
            s1 = jnp.where(causal, raw_scores(lower, qt[:, half:]), NEG_FILL)
            return s0, s1

        def column_sum(x):
            return jnp.sum(fold_rows(x), axis=0)

        def forward(ref, s0, s1, sizes=(4, 2, 1)):
            def step(j, count, total):
                p = jnp.exp2(raw_scores(key_rows(j, count), qt) - ref)
                scores[key_rows(j - first, count), :] = p
                return total + column_sum(p)

            p0 = jnp.exp2(s0 - ref)
            p1 = jnp.exp2(s1 - ref[:, half:])
            scores[upper_to, :] = p0
            scores[lower_to, half:] = p1
            total = column_sum(p0) + widen_lanes(column_sum(p1))
            return jnp.sum(in_steps(step, total, sizes), axis=0, keepdims=True)

        def diag_top(s0, s1):
            top0 = jnp.max(s0, axis=0, keepdims=True)
            top1 = jnp.max(s1, axis=0, keepdims=True)
            return jnp.concatenate(
                [top0[:, :half], jnp.maximum(top0[:, half:], top1)], axis=1
            )

        def exact():
            def step(j, count, top):
                s = raw_scores(key_rows(j, count), qt)
                return jnp.maximum(top, jnp.max(s, axis=0, keepdims=True))

            s0, s1 = diag_scores()
            return forward(in_steps(step, diag_top(s0, s1), (1,)), s0, s1, (1,))

        s0, s1 = diag_scores()
        total = forward(diag_top(s0, s1), s0, s1)
        fits = jnp.max(jnp.where(total < HUGE, 0.0, 1.0)) == 0.0
        inv = 1.0 / lax.cond(fits, lambda: total, exact)

        def part_of_delta(p, dp, inv):
            return column_sum(to_bf16(p * inv).astype(F32) * dp)

        def delta_step(j, count, delta):
            to = key_rows(j - first, count)
            dp = jnp.dot(win[key_rows(j, count), DH:], gt, preferred_element_type=F32)
            dprobs[to, :] = dp
            return delta + part_of_delta(scores[to, :], dp, inv)

        dp0 = jnp.dot(win[upper, DH:], gt, preferred_element_type=F32)
        dp1 = jnp.dot(win[lower, DH:], gt[:, half:], preferred_element_type=F32)
        dprobs[upper_to, :] = dp0
        dprobs[lower_to, half:] = dp1
        delta = part_of_delta(scores[upper_to, :], dp0, inv)
        delta += widen_lanes(part_of_delta(scores[lower_to, half:], dp1, inv[:, half:]))
        delta = jnp.sum(in_steps(delta_step, delta), axis=0, keepdims=True)
        dqt[...] = jnp.zeros_like(dqt)

        def grads(p, dp, inv, delta):
            p = p * inv
            return to_bf16(p), to_bf16(p * (dp - delta))

        def add_grads(at, low, ds, q, go):
            acc[at, DH:] += jnp.dot(low, go, preferred_element_type=F32)
            acc[at, :DH] += jnp.dot(ds, q, preferred_element_type=F32)

        def backward(j, count, carry):
            at = key_rows(j, count)
            to = key_rows(j - first, count)
            low, ds = grads(scores[to, :], dprobs[to, :], inv, delta)
            add_grads(at, low, ds, q, go)
            dqt[...] += jnp.dot(kt[:, at], ds, preferred_element_type=F32)
            return carry

        low0, ds0 = grads(scores[upper_to, :], dprobs[upper_to, :], inv, delta)
        low1, ds1 = grads(
            scores[lower_to, half:], dprobs[lower_to, half:], inv[:, half:], delta[:, half:]
        )
        add_grads(upper, low0, ds0, q, go)
        add_grads(lower, low1, ds1, q[half:], go[half:])
        dqt[...] = jnp.dot(kt[:, upper], ds0, preferred_element_type=F32)
        dqt[:, half:] += jnp.dot(kt[:, lower], ds1, preferred_element_type=F32)
        in_steps(backward, jnp.int32(0))
        dq_ref[rows, :] = to_bf16((dqt[...] * scale).T)

    copies = [pltpu.make_async_copy(dq_ref, dq_hbm, io_sems.at[0])]
    copies[0].start()
    for b in range(blocks):
        for i in range(4):
            at = tile_rows(b, g ^ i)
            win[at, :] = to_bf16(acc[at, :])
            copy = pltpu.make_async_copy(
                win.at[at], out_refs[2 * b + i % 2].at[i // 2], sems.at[b, i]
            )
            copy.start()
            copies.append(copy)
    for copy in copies:
        copy.wait()


def up_ctx(x, by):
    n = lax.axis_size("ctx")
    return lax.ppermute(x, "ctx", [(i, (i + by) % n) for i in range(n)])


def down_ctx(x, by):
    n = lax.axis_size("ctx")
    return lax.ppermute(x, "ctx", [(i, i - by) for i in range(by, n)])


def swap_grp(x, bit):
    n = lax.axis_size("grp")
    return lax.ppermute(x, "grp", [(i, i ^ bit) for i in range(n)])


def four_tiles(x, y):
    return [x, swap_grp(x, 1), y, swap_grp(y, 1)]


def spans_blocks(doc_tiles, local_tiles):
    ids = jnp.arange(doc_tiles.shape[0])
    begins = jnp.sum(jnp.where(ids[None, :] < ids[:, None], doc_tiles[None, :], 0), axis=1)
    lasts = begins + doc_tiles - 1
    return jnp.max(lasts // local_tiles - begins // local_tiles)


def with_window(queries, grad_out, doc_tiles, pieces, *, local_tiles, reach):
    blocks = reach + 1
    slots = blocks * local_tiles
    scale = 1.0 / math.sqrt(DH)
    width = 2 * DH

    *pieces, (x3, _) = pieces
    if reach == 3:
        pieces.append((x3, swap_grp(x3, 2)))
    pieces = [four_tiles(x, y) for x, y in pieces]
    pieces = [tile for block in reversed(pieces) for tile in block]

    hbm = pl.BlockSpec(memory_space=pl.ANY)
    half = jax.ShapeDtypeStruct((local_tiles // 2, TILE, width), BF16)
    grad_queries, *halves = pl.pallas_call(
        lambda *refs: local_kernel(*refs, local_tiles=local_tiles, reach=reach, scale=scale),
        out_shape=(jax.ShapeDtypeStruct(queries.shape, BF16),) + (half,) * (2 * blocks),
        in_specs=[pl.BlockSpec(memory_space=pltpu.SMEM)] + [hbm] * (2 + 4 * blocks),
        out_specs=(hbm,) * (1 + 2 * blocks),
        scratch_shapes=[
            pltpu.VMEM(queries.shape, BF16),
            pltpu.VMEM(queries.shape, BF16),
            pltpu.VMEM(queries.shape, BF16),
            pltpu.VMEM((slots * TILE, width), BF16),
            pltpu.VMEM((DH, slots * TILE), BF16),
            pltpu.VMEM((MAXT * TILE, TILE), F32),
            pltpu.VMEM((MAXT * TILE, TILE), F32),
            pltpu.VMEM((slots * TILE, width), F32),
            pltpu.VMEM((DH, TILE), F32),
            pltpu.SemaphoreType.DMA((blocks, 4)),
            pltpu.SemaphoreType.DMA((2,)),
        ],
        compiler_params=pltpu.CompilerParams(vmem_limit_bytes=(40 + 4 * reach) * 1024 * 1024),
    )(doc_tiles, queries, grad_out, *pieces)

    mine, theirs = {}, {}
    for d in range(reach, -1, -1):
        keep, send = halves[2 * (reach - d)], halves[2 * (reach - d) + 1]
        got = swap_grp(send, 1).astype(F32)
        mine[d] = keep[0].astype(F32) + got[0]
        theirs[d] = keep[1].astype(F32) + got[1]
    far_theirs = down_ctx(to_bf16(theirs[2]), 2).astype(F32)
    own = mine[0] + down_ctx(to_bf16(mine[2]), 2).astype(F32)
    own = own + swap_grp(to_bf16(theirs[0] + far_theirs), 2).astype(F32)
    near = to_bf16(theirs[1])
    if reach == 3:
        got, near = lax.optimization_barrier((swap_grp(to_bf16(theirs[3]), 2), near))
        own = own + down_ctx(to_bf16(mine[3] + got.astype(F32)), 3).astype(F32)
    near = mine[1] + swap_grp(near, 2).astype(F32)
    own = own + down_ctx(to_bf16(near), 1).astype(F32)
    grad_kv = to_bf16(jnp.concatenate([own[:, :DH] * scale, own[:, DH:]], axis=1))
    return (grad_queries, grad_kv)


def shards(queries, kv_cache, grad_out, doc_tiles):
    local_tiles = queries.shape[0] // TILE
    most = (MAXT - 2) // local_tiles + 1
    assert most == 3
    x0 = kv_cache
    spans = spans_blocks(doc_tiles, local_tiles)
    y0, spans = lax.optimization_barrier((swap_grp(x0, 2), spans))
    x1 = up_ctx(x0, 1)
    x2 = up_ctx(x0, 2)
    y1 = swap_grp(x1, 2)
    y2 = up_ctx(y0, 2)
    x3 = lax.cond(spans >= most, lambda x: up_ctx(x, 2), lambda x: x, x1)
    pieces = [(x0, y0), (x1, y1), (x2, y2), (x3, x3)]
    return lax.cond(
        spans >= most,
        lambda *args: with_window(*args, local_tiles=local_tiles, reach=most),
        lambda *args: with_window(*args, local_tiles=local_tiles, reach=most - 1),
        queries, grad_out, doc_tiles, pieces,
    )


def solution(mesh):
    placed = (P("ctx", "grp"), P(("ctx", "grp"), None), P("ctx", "grp"), P())
    return jax.shard_map(
        shards,
        mesh=mesh,
        in_specs=placed,
        out_specs=(P("ctx", "grp"), P(("ctx", "grp"), None)),
        check_vma=False,
    )
```

```python
import math

import jax
import jax.numpy as jnp
from jax import lax
from jax.experimental import pallas as pl
from jax.experimental.pallas import tpu as pltpu
from jax.sharding import PartitionSpec as P

DH = 128
TILE = 512
MAXT = 12
NEG_FILL = -1e30
HUGE = 2.0**100
F32 = jnp.float32
BF16 = jnp.bfloat16


def to_bf16(x):
    return x.astype(BF16)


def fold_rows(x):
    return x.reshape(x.shape[0] // 8, 8, x.shape[1])


def first_tile_of(doc_ref, doc_count, tile):
    def step(d, carry):
        begin, found = carry
        found = jnp.where(begin <= tile, begin, found)
        return (begin + doc_ref[d], found)

    return lax.fori_loop(0, doc_count, step, (jnp.int32(0), jnp.int32(0)))[1]


def local_kernel(*refs, local_tiles, reach, scale):
    blocks = reach + 1
    doc_ref, q_hbm, g_hbm = refs[:3]
    piece_refs = refs[3 : 3 + 4 * blocks]
    dq_hbm = refs[3 + 4 * blocks]
    out_refs = refs[4 + 4 * blocks : 4 + 6 * blocks]
    q_ref, g_ref, dq_ref, win, kt, scores, dprobs, acc, dqt, sems, io_sems = refs[4 + 6 * blocks :]

    slots = blocks * local_tiles
    c = lax.axis_index("ctx")
    g = lax.axis_index("grp")
    base = (c - reach) * local_tiles
    to_log2 = scale * math.log2(math.e)

    def tile_rows(b, owner):
        return pl.ds(pl.multiple_of((b * local_tiles + owner) * TILE, TILE), TILE)

    copies = [
        pltpu.make_async_copy(q_hbm, q_ref, io_sems.at[0]),
        pltpu.make_async_copy(g_hbm, g_ref, io_sems.at[1]),
    ]
    for b in range(blocks):
        for i in range(4):
            copies.append(
                pltpu.make_async_copy(
                    piece_refs[4 * b + i], win.at[tile_rows(b, g ^ i)], sems.at[b, i]
                )
            )
    for copy in copies:
        copy.start()
    acc[...] = jnp.zeros_like(acc)
    for copy in copies:
        copy.wait()

    doc_count = doc_ref.shape[0]
    low = first_tile_of(doc_ref, doc_count, c * local_tiles) - base

    @pl.loop(low, slots)
    def _(j):
        tile = pl.ds(pl.multiple_of(j * TILE, TILE), TILE)
        kt[:, tile] = win[tile, :DH].T

    half = TILE // 2
    causal = lax.broadcasted_iota(jnp.int32, (half, half), 0) <= lax.broadcasted_iota(
        jnp.int32, (half, half), 1
    )

    def widen_lanes(x):
        return jnp.concatenate([jnp.zeros_like(x), x], axis=1)

    @pl.loop(0, local_tiles)
    def _(t):
        rows = pl.ds(pl.multiple_of(t * TILE, TILE), TILE)
        q = q_ref[rows, :]
        go = g_ref[rows, :]
        qt = q.T
        gt = go.T
        diag = reach * local_tiles + t
        first = first_tile_of(doc_ref, doc_count, c * local_tiles + t) - base

        def key_rows(j, count):
            return pl.ds(pl.multiple_of(j * TILE, TILE), count * TILE)

        def in_steps(step, carry, sizes=(4, 2, 1)):
            lo = first
            for size in sizes:
                steps = (diag - lo) // size
                carry = lax.fori_loop(
                    0, steps, lambda i, x, lo=lo, size=size: step(lo + i * size, size, x), carry
                )
                lo = lo + steps * size
            return carry

        def raw_scores(at, queries_t):
            return jnp.dot(win[at, :DH], queries_t, preferred_element_type=F32) * to_log2

        upper = pl.ds(pl.multiple_of(diag * TILE, half), half)
        lower = pl.ds(pl.multiple_of(diag * TILE + half, half), half)
        slot = diag - first
        upper_to = pl.ds(pl.multiple_of(slot * TILE, half), half)
        lower_to = pl.ds(pl.multiple_of(slot * TILE + half, half), half)

        def diag_scores():
            s0 = raw_scores(upper, qt)
            s0 = jnp.concatenate(
                [jnp.where(causal, s0[:, :half], NEG_FILL), s0[:, half:]], axis=1
            )
            s1 = jnp.where(causal, raw_scores(lower, qt[:, half:]), NEG_FILL)
            return s0, s1

        def column_sum(x):
            return jnp.sum(fold_rows(x), axis=0)

        def forward(ref, s0, s1, sizes=(4, 2, 1)):
            def step(j, count, total):
                p = jnp.exp2(raw_scores(key_rows(j, count), qt) - ref)
                scores[key_rows(j - first, count), :] = p
                return total + column_sum(p)

            p0 = jnp.exp2(s0 - ref)
            p1 = jnp.exp2(s1 - ref[:, half:])
            scores[upper_to, :] = p0
            scores[lower_to, half:] = p1
            total = column_sum(p0) + widen_lanes(column_sum(p1))
            return jnp.sum(in_steps(step, total, sizes), axis=0, keepdims=True)

        def diag_top(s0, s1):
            top0 = jnp.max(s0, axis=0, keepdims=True)
            top1 = jnp.max(s1, axis=0, keepdims=True)
            return jnp.concatenate(
                [top0[:, :half], jnp.maximum(top0[:, half:], top1)], axis=1
            )

        def exact():
            def step(j, count, top):
                s = raw_scores(key_rows(j, count), qt)
                return jnp.maximum(top, jnp.max(s, axis=0, keepdims=True))

            s0, s1 = diag_scores()
            return forward(in_steps(step, diag_top(s0, s1), (1,)), s0, s1, (1,))

        s0, s1 = diag_scores()
        total = forward(diag_top(s0, s1), s0, s1)
        fits = jnp.max(jnp.where(total < HUGE, 0.0, 1.0)) == 0.0
        inv = 1.0 / lax.cond(fits, lambda: total, exact)

        def part_of_delta(p, dp, inv):
            return column_sum(to_bf16(p * inv).astype(F32) * dp)

        def delta_step(j, count, delta):
            to = key_rows(j - first, count)
            dp = jnp.dot(win[key_rows(j, count), DH:], gt, preferred_element_type=F32)
            dprobs[to, :] = dp
            return delta + part_of_delta(scores[to, :], dp, inv)

        dp0 = jnp.dot(win[upper, DH:], gt, preferred_element_type=F32)
        dp1 = jnp.dot(win[lower, DH:], gt[:, half:], preferred_element_type=F32)
        dprobs[upper_to, :] = dp0
        dprobs[lower_to, half:] = dp1
        delta = part_of_delta(scores[upper_to, :], dp0, inv)
        delta += widen_lanes(part_of_delta(scores[lower_to, half:], dp1, inv[:, half:]))
        delta = jnp.sum(in_steps(delta_step, delta), axis=0, keepdims=True)
        dqt[...] = jnp.zeros_like(dqt)

        def grads(p, dp, inv, delta):
            p = p * inv
            return to_bf16(p), to_bf16(p * (dp - delta))

        def add_grads(at, low, ds, q, go):
            acc[at, DH:] += jnp.dot(low, go, preferred_element_type=F32)
            acc[at, :DH] += jnp.dot(ds, q, preferred_element_type=F32)

        def backward(j, count, carry):
            at = key_rows(j, count)
            to = key_rows(j - first, count)
            low, ds = grads(scores[to, :], dprobs[to, :], inv, delta)
            add_grads(at, low, ds, q, go)
            dqt[...] += jnp.dot(kt[:, at], ds, preferred_element_type=F32)
            return carry

        low0, ds0 = grads(scores[upper_to, :], dprobs[upper_to, :], inv, delta)
        low1, ds1 = grads(
            scores[lower_to, half:], dprobs[lower_to, half:], inv[:, half:], delta[:, half:]
        )
        add_grads(upper, low0, ds0, q, go)
        add_grads(lower, low1, ds1, q[half:], go[half:])
        dqt[...] = jnp.dot(kt[:, upper], ds0, preferred_element_type=F32)
        dqt[:, half:] += jnp.dot(kt[:, lower], ds1, preferred_element_type=F32)
        in_steps(backward, jnp.int32(0))
        dq_ref[rows, :] = to_bf16((dqt[...] * scale).T)

    copies = [pltpu.make_async_copy(dq_ref, dq_hbm, io_sems.at[0])]
    copies[0].start()
    for b in range(blocks):
        for i in range(4):
            at = tile_rows(b, g ^ i)
            win[at, :] = to_bf16(acc[at, :])
            copy = pltpu.make_async_copy(
                win.at[at], out_refs[2 * b + i % 2].at[i // 2], sems.at[b, i]
            )
            copy.start()
            copies.append(copy)
    for copy in copies:
        copy.wait()


def up_ctx(x, by):
    n = lax.axis_size("ctx")
    return lax.ppermute(x, "ctx", [(i, (i + by) % n) for i in range(n)])


def down_ctx(x, by):
    n = lax.axis_size("ctx")
    return lax.ppermute(x, "ctx", [(i, i - by) for i in range(by, n)])


def swap_grp(x, bit):
    n = lax.axis_size("grp")
    return lax.ppermute(x, "grp", [(i, i ^ bit) for i in range(n)])


def four_tiles(x, y):
    return [x, swap_grp(x, 1), y, swap_grp(y, 1)]


def spans_blocks(doc_tiles, local_tiles):
    ids = jnp.arange(doc_tiles.shape[0])
    begins = jnp.sum(jnp.where(ids[None, :] < ids[:, None], doc_tiles[None, :], 0), axis=1)
    lasts = begins + doc_tiles - 1
    return jnp.max(lasts // local_tiles - begins // local_tiles)


def with_window(queries, grad_out, doc_tiles, pieces, *, local_tiles, reach):
    blocks = reach + 1
    slots = blocks * local_tiles
    scale = 1.0 / math.sqrt(DH)
    width = 2 * DH

    own_pieces, *far, (x3,) = pieces
    if reach == 3:
        far.append([x3, swap_grp(x3, 1), swap_grp(x3, 2)])
    pieces = [own_pieces] + [block + [swap_grp(block[2], 1)] for block in far]
    pieces = [tile for block in reversed(pieces) for tile in block]

    hbm = pl.BlockSpec(memory_space=pl.ANY)
    half = jax.ShapeDtypeStruct((local_tiles // 2, TILE, width), BF16)
    grad_queries, *halves = pl.pallas_call(
        lambda *refs: local_kernel(*refs, local_tiles=local_tiles, reach=reach, scale=scale),
        out_shape=(jax.ShapeDtypeStruct(queries.shape, BF16),) + (half,) * (2 * blocks),
        in_specs=[pl.BlockSpec(memory_space=pltpu.SMEM)] + [hbm] * (2 + 4 * blocks),
        out_specs=(hbm,) * (1 + 2 * blocks),
        scratch_shapes=[
            pltpu.VMEM(queries.shape, BF16),
            pltpu.VMEM(queries.shape, BF16),
            pltpu.VMEM(queries.shape, BF16),
            pltpu.VMEM((slots * TILE, width), BF16),
            pltpu.VMEM((DH, slots * TILE), BF16),
            pltpu.VMEM((MAXT * TILE, TILE), F32),
            pltpu.VMEM((MAXT * TILE, TILE), F32),
            pltpu.VMEM((slots * TILE, width), F32),
            pltpu.VMEM((DH, TILE), F32),
            pltpu.SemaphoreType.DMA((blocks, 4)),
            pltpu.SemaphoreType.DMA((2,)),
        ],
        compiler_params=pltpu.CompilerParams(vmem_limit_bytes=(40 + 4 * reach) * 1024 * 1024),
    )(doc_tiles, queries, grad_out, *pieces)

    mine, theirs = {}, {}
    for d in range(reach, -1, -1):
        keep, send = halves[2 * (reach - d)], halves[2 * (reach - d) + 1]
        got = swap_grp(send, 1).astype(F32)
        mine[d] = keep[0].astype(F32) + got[0]
        theirs[d] = keep[1].astype(F32) + got[1]
    far_theirs = down_ctx(to_bf16(theirs[2]), 2).astype(F32)
    own = mine[0] + down_ctx(to_bf16(mine[2]), 2).astype(F32)
    own = own + swap_grp(to_bf16(theirs[0] + far_theirs), 2).astype(F32)
    near = to_bf16(theirs[1])
    if reach == 3:
        got, near = lax.optimization_barrier((swap_grp(to_bf16(theirs[3]), 2), near))
        own = own + down_ctx(to_bf16(mine[3] + got.astype(F32)), 3).astype(F32)
    near = mine[1] + swap_grp(near, 2).astype(F32)
    own = own + down_ctx(to_bf16(near), 1).astype(F32)
    grad_kv = to_bf16(jnp.concatenate([own[:, :DH] * scale, own[:, DH:]], axis=1))
    return (grad_queries, grad_kv)


def shards(queries, kv_cache, grad_out, doc_tiles):
    local_tiles = queries.shape[0] // TILE
    most = (MAXT - 2) // local_tiles + 1
    assert most == 3
    x0 = kv_cache
    spans = spans_blocks(doc_tiles, local_tiles)
    y0, spans = lax.optimization_barrier((swap_grp(x0, 2), spans))
    x1 = up_ctx(x0, 1)
    x2 = up_ctx(x0, 2)
    y1 = swap_grp(x1, 2)
    y2 = up_ctx(y0, 2)
    x3 = lax.cond(spans >= most, lambda x: up_ctx(x, 2), lambda x: x, x1)
    x0, y0, x1, x3 = lax.optimization_barrier((x0, y0, x1, x3))
    pieces = [four_tiles(x0, y0), [x1, swap_grp(x1, 1), y1], [x2, swap_grp(x2, 1), y2], [x3]]
    return lax.cond(
        spans >= most,
        lambda *args: with_window(*args, local_tiles=local_tiles, reach=most),
        lambda *args: with_window(*args, local_tiles=local_tiles, reach=most - 1),
        queries, grad_out, doc_tiles, pieces,
    )


def solution(mesh):
    placed = (P("ctx", "grp"), P(("ctx", "grp"), None), P("ctx", "grp"), P())
    return jax.shard_map(
        shards,
        mesh=mesh,
        in_specs=placed,
        out_specs=(P("ctx", "grp"), P(("ctx", "grp"), None)),
        check_vma=False,
    )
```

```python
import math

import jax
import jax.numpy as jnp
from jax import lax
from jax.experimental import pallas as pl
from jax.experimental.pallas import tpu as pltpu
from jax.sharding import PartitionSpec as P

DH = 128
TILE = 512
MAXT = 12
NEG_FILL = -1e30
HUGE = 2.0**100
F32 = jnp.float32
BF16 = jnp.bfloat16


def to_bf16(x):
    return x.astype(BF16)


def fold_rows(x):
    return x.reshape(x.shape[0] // 8, 8, x.shape[1])


def first_tile_of(doc_ref, doc_count, tile):
    def step(d, carry):
        begin, found = carry
        found = jnp.where(begin <= tile, begin, found)
        return (begin + doc_ref[d], found)

    return lax.fori_loop(0, doc_count, step, (jnp.int32(0), jnp.int32(0)))[1]


def local_kernel(*refs, local_tiles, reach, scale):
    blocks = reach + 1
    doc_ref, q_hbm, g_hbm = refs[:3]
    piece_refs = refs[3 : 3 + 4 * blocks]
    dq_hbm = refs[3 + 4 * blocks]
    out_refs = refs[4 + 4 * blocks : 4 + 6 * blocks]
    q_ref, g_ref, dq_ref, win, kt, scores, dprobs, acc, dqt, sems, io_sems = refs[4 + 6 * blocks :]

    slots = blocks * local_tiles
    c = lax.axis_index("ctx")
    g = lax.axis_index("grp")
    base = (c - reach) * local_tiles
    to_log2 = scale * math.log2(math.e)

    def tile_rows(b, owner):
        return pl.ds(pl.multiple_of((b * local_tiles + owner) * TILE, TILE), TILE)

    copies = [
        pltpu.make_async_copy(q_hbm, q_ref, io_sems.at[0]),
        pltpu.make_async_copy(g_hbm, g_ref, io_sems.at[1]),
    ]
    for b in range(blocks):
        for i in range(4):
            copies.append(
                pltpu.make_async_copy(
                    piece_refs[4 * b + i], win.at[tile_rows(b, g ^ i)], sems.at[b, i]
                )
            )
    for copy in copies:
        copy.start()
    acc[...] = jnp.zeros_like(acc)
    for copy in copies:
        copy.wait()

    doc_count = doc_ref.shape[0]
    low = first_tile_of(doc_ref, doc_count, c * local_tiles) - base

    @pl.loop(low, slots)
    def _(j):
        tile = pl.ds(pl.multiple_of(j * TILE, TILE), TILE)
        kt[:, tile] = win[tile, :DH].T

    half = TILE // 2
    causal = lax.broadcasted_iota(jnp.int32, (half, half), 0) <= lax.broadcasted_iota(
        jnp.int32, (half, half), 1
    )

    def widen_lanes(x):
        return jnp.concatenate([jnp.zeros_like(x), x], axis=1)

    @pl.loop(0, local_tiles)
    def _(t):
        rows = pl.ds(pl.multiple_of(t * TILE, TILE), TILE)
        q = q_ref[rows, :]
        go = g_ref[rows, :]
        qt = q.T
        gt = go.T
        diag = reach * local_tiles + t
        first = first_tile_of(doc_ref, doc_count, c * local_tiles + t) - base

        def key_rows(j, count):
            return pl.ds(pl.multiple_of(j * TILE, TILE), count * TILE)

        def in_steps(step, carry, sizes=(4, 2, 1)):
            lo = first
            for size in sizes:
                steps = (diag - lo) // size
                carry = lax.fori_loop(
                    0, steps, lambda i, x, lo=lo, size=size: step(lo + i * size, size, x), carry
                )
                lo = lo + steps * size
            return carry

        def raw_scores(at, queries_t):
            return jnp.dot(win[at, :DH], queries_t, preferred_element_type=F32) * to_log2

        upper = pl.ds(pl.multiple_of(diag * TILE, half), half)
        lower = pl.ds(pl.multiple_of(diag * TILE + half, half), half)
        slot = diag - first
        upper_to = pl.ds(pl.multiple_of(slot * TILE, half), half)
        lower_to = pl.ds(pl.multiple_of(slot * TILE + half, half), half)

        def diag_scores():
            s0 = raw_scores(upper, qt)
            s0 = jnp.concatenate(
                [jnp.where(causal, s0[:, :half], NEG_FILL), s0[:, half:]], axis=1
            )
            s1 = jnp.where(causal, raw_scores(lower, qt[:, half:]), NEG_FILL)
            return s0, s1

        def column_sum(x):
            return jnp.sum(fold_rows(x), axis=0)

        def forward(ref, s0, s1, sizes=(4, 2, 1)):
            def step(j, count, total):
                p = jnp.exp2(raw_scores(key_rows(j, count), qt) - ref)
                scores[key_rows(j - first, count), :] = p
                return total + column_sum(p)

            p0 = jnp.exp2(s0 - ref)
            p1 = jnp.exp2(s1 - ref[:, half:])
            scores[upper_to, :] = p0
            scores[lower_to, half:] = p1
            total = column_sum(p0) + widen_lanes(column_sum(p1))
            return jnp.sum(in_steps(step, total, sizes), axis=0, keepdims=True)

        def diag_top(s0, s1):
            top0 = jnp.max(s0, axis=0, keepdims=True)
            top1 = jnp.max(s1, axis=0, keepdims=True)
            return jnp.concatenate(
                [top0[:, :half], jnp.maximum(top0[:, half:], top1)], axis=1
            )

        def exact():
            def step(j, count, top):
                s = raw_scores(key_rows(j, count), qt)
                return jnp.maximum(top, jnp.max(s, axis=0, keepdims=True))

            s0, s1 = diag_scores()
            return forward(in_steps(step, diag_top(s0, s1), (1,)), s0, s1, (1,))

        s0, s1 = diag_scores()
        total = forward(diag_top(s0, s1), s0, s1)
        fits = jnp.max(jnp.where(total < HUGE, 0.0, 1.0)) == 0.0
        inv = 1.0 / lax.cond(fits, lambda: total, exact)

        def part_of_delta(p, dp, inv):
            return column_sum(to_bf16(p * inv).astype(F32) * dp)

        def delta_step(j, count, delta):
            to = key_rows(j - first, count)
            dp = jnp.dot(win[key_rows(j, count), DH:], gt, preferred_element_type=F32)
            dprobs[to, :] = dp
            return delta + part_of_delta(scores[to, :], dp, inv)

        dp0 = jnp.dot(win[upper, DH:], gt, preferred_element_type=F32)
        dp1 = jnp.dot(win[lower, DH:], gt[:, half:], preferred_element_type=F32)
        dprobs[upper_to, :] = dp0
        dprobs[lower_to, half:] = dp1
        delta = part_of_delta(scores[upper_to, :], dp0, inv)
        delta += widen_lanes(part_of_delta(scores[lower_to, half:], dp1, inv[:, half:]))
        delta = jnp.sum(in_steps(delta_step, delta), axis=0, keepdims=True)
        dqt[...] = jnp.zeros_like(dqt)

        def grads(p, dp, inv, delta):
            p = p * inv
            return to_bf16(p), to_bf16(p * (dp - delta))

        def add_grads(at, low, ds, q, go):
            acc[at, DH:] += jnp.dot(low, go, preferred_element_type=F32)
            acc[at, :DH] += jnp.dot(ds, q, preferred_element_type=F32)

        def backward(j, count, carry):
            at = key_rows(j, count)
            to = key_rows(j - first, count)
            low, ds = grads(scores[to, :], dprobs[to, :], inv, delta)
            add_grads(at, low, ds, q, go)
            dqt[...] += jnp.dot(kt[:, at], ds, preferred_element_type=F32)
            return carry

        low0, ds0 = grads(scores[upper_to, :], dprobs[upper_to, :], inv, delta)
        low1, ds1 = grads(
            scores[lower_to, half:], dprobs[lower_to, half:], inv[:, half:], delta[:, half:]
        )
        add_grads(upper, low0, ds0, q, go)
        add_grads(lower, low1, ds1, q[half:], go[half:])
        dqt[...] = jnp.dot(kt[:, upper], ds0, preferred_element_type=F32)
        dqt[:, half:] += jnp.dot(kt[:, lower], ds1, preferred_element_type=F32)
        in_steps(backward, jnp.int32(0))
        dq_ref[rows, :] = to_bf16((dqt[...] * scale).T)

    copies = [pltpu.make_async_copy(dq_ref, dq_hbm, io_sems.at[0])]
    copies[0].start()
    for b in range(blocks):
        for i in range(4):
            at = tile_rows(b, g ^ i)
            win[at, :] = to_bf16(acc[at, :])
            copy = pltpu.make_async_copy(
                win.at[at], out_refs[2 * b + i % 2].at[i // 2], sems.at[b, i]
            )
            copy.start()
            copies.append(copy)
    for copy in copies:
        copy.wait()


def up_ctx(x, by):
    n = lax.axis_size("ctx")
    return lax.ppermute(x, "ctx", [(i, (i + by) % n) for i in range(n)])


def down_ctx(x, by):
    n = lax.axis_size("ctx")
    return lax.ppermute(x, "ctx", [(i, i - by) for i in range(by, n)])


def swap_grp(x, bit):
    n = lax.axis_size("grp")
    return lax.ppermute(x, "grp", [(i, i ^ bit) for i in range(n)])


def four_tiles(x, y):
    return [x, swap_grp(x, 1), y, swap_grp(y, 1)]


def spans_blocks(doc_tiles, local_tiles):
    ids = jnp.arange(doc_tiles.shape[0])
    begins = jnp.sum(jnp.where(ids[None, :] < ids[:, None], doc_tiles[None, :], 0), axis=1)
    lasts = begins + doc_tiles - 1
    return jnp.max(lasts // local_tiles - begins // local_tiles)


def with_window(queries, grad_out, doc_tiles, pieces, *, local_tiles, reach):
    blocks = reach + 1
    slots = blocks * local_tiles
    scale = 1.0 / math.sqrt(DH)
    width = 2 * DH

    own_pieces, *far, (x3,) = pieces
    if reach == 3:
        far.append([x3, swap_grp(x3, 1), swap_grp(x3, 2)])
    pieces = [own_pieces] + [block + [swap_grp(block[2], 1)] for block in far]
    pieces = [tile for block in reversed(pieces) for tile in block]

    hbm = pl.BlockSpec(memory_space=pl.ANY)
    half = jax.ShapeDtypeStruct((local_tiles // 2, TILE, width), BF16)
    grad_queries, *halves = pl.pallas_call(
        lambda *refs: local_kernel(*refs, local_tiles=local_tiles, reach=reach, scale=scale),
        out_shape=(jax.ShapeDtypeStruct(queries.shape, BF16),) + (half,) * (2 * blocks),
        in_specs=[pl.BlockSpec(memory_space=pltpu.SMEM)] + [hbm] * (2 + 4 * blocks),
        out_specs=(hbm,) * (1 + 2 * blocks),
        scratch_shapes=[
            pltpu.VMEM(queries.shape, BF16),
            pltpu.VMEM(queries.shape, BF16),
            pltpu.VMEM(queries.shape, BF16),
            pltpu.VMEM((slots * TILE, width), BF16),
            pltpu.VMEM((DH, slots * TILE), BF16),
            pltpu.VMEM((MAXT * TILE, TILE), F32),
            pltpu.VMEM((MAXT * TILE, TILE), F32),
            pltpu.VMEM((slots * TILE, width), F32),
            pltpu.VMEM((DH, TILE), F32),
            pltpu.SemaphoreType.DMA((blocks, 4)),
            pltpu.SemaphoreType.DMA((2,)),
        ],
        compiler_params=pltpu.CompilerParams(vmem_limit_bytes=(40 + 4 * reach) * 1024 * 1024),
    )(doc_tiles, queries, grad_out, *pieces)

    mine, theirs = {}, {}
    for d in range(reach, -1, -1):
        keep, send = halves[2 * (reach - d)], halves[2 * (reach - d) + 1]
        got = swap_grp(send, 1).astype(F32)
        mine[d] = keep[0].astype(F32) + got[0]
        theirs[d] = keep[1].astype(F32) + got[1]
    far_theirs = down_ctx(to_bf16(theirs[2]), 2).astype(F32)
    own = mine[0] + down_ctx(to_bf16(mine[2]), 2).astype(F32)
    own = own + swap_grp(to_bf16(theirs[0] + far_theirs), 2).astype(F32)
    near = to_bf16(theirs[1])
    if reach == 3:
        got, near = lax.optimization_barrier((swap_grp(to_bf16(theirs[3]), 2), near))
        own = own + down_ctx(to_bf16(mine[3] + got.astype(F32)), 3).astype(F32)
    near = mine[1] + swap_grp(near, 2).astype(F32)
    own = own + down_ctx(to_bf16(near), 1).astype(F32)
    grad_kv = to_bf16(jnp.concatenate([own[:, :DH] * scale, own[:, DH:]], axis=1))
    return (grad_queries, grad_kv)


def shards(queries, kv_cache, grad_out, doc_tiles):
    local_tiles = queries.shape[0] // TILE
    most = (MAXT - 2) // local_tiles + 1
    assert most == 3
    x0 = kv_cache
    spans = spans_blocks(doc_tiles, local_tiles)
    x1, spans = lax.optimization_barrier((up_ctx(x0, 1), spans))
    y0, spans = lax.optimization_barrier((swap_grp(x0, 2), spans))
    x2 = up_ctx(x0, 2)
    y1 = swap_grp(x1, 2)
    y2 = up_ctx(y0, 2)
    x1, x2 = lax.optimization_barrier((x1, x2))
    x3 = lax.cond(spans >= most, lambda x: up_ctx(x, 2), lambda x: x, x1)
    x0, y0, x1, x3 = lax.optimization_barrier((x0, y0, x1, x3))
    pieces = [four_tiles(x0, y0), [x1, swap_grp(x1, 1), y1], [x2, swap_grp(x2, 1), y2], [x3]]
    return lax.cond(
        spans >= most,
        lambda *args: with_window(*args, local_tiles=local_tiles, reach=most),
        lambda *args: with_window(*args, local_tiles=local_tiles, reach=most - 1),
        queries, grad_out, doc_tiles, pieces,
    )


def solution(mesh):
    placed = (P("ctx", "grp"), P(("ctx", "grp"), None), P("ctx", "grp"), P())
    return jax.shard_map(
        shards,
        mesh=mesh,
        in_specs=placed,
        out_specs=(P("ctx", "grp"), P(("ctx", "grp"), None)),
        check_vma=False,
    )
```

```python
import math

import jax
import jax.numpy as jnp
from jax import lax
from jax.experimental import pallas as pl
from jax.experimental.pallas import tpu as pltpu
from jax.sharding import PartitionSpec as P

DH = 128
TILE = 512
MAXT = 12
NEG_FILL = -1e30
HUGE = 2.0**100
F32 = jnp.float32
BF16 = jnp.bfloat16


def to_bf16(x):
    return x.astype(BF16)


def fold_rows(x):
    return x.reshape(x.shape[0] // 8, 8, x.shape[1])


def first_tile_of(doc_ref, doc_count, tile):
    def step(d, carry):
        begin, found = carry
        found = jnp.where(begin <= tile, begin, found)
        return (begin + doc_ref[d], found)

    return lax.fori_loop(0, doc_count, step, (jnp.int32(0), jnp.int32(0)))[1]


def local_kernel(*refs, local_tiles, reach, scale):
    blocks = reach + 1
    doc_ref, q_hbm, g_hbm = refs[:3]
    piece_refs = refs[3 : 3 + 4 * blocks]
    dq_hbm = refs[3 + 4 * blocks]
    out_refs = refs[4 + 4 * blocks : 4 + 6 * blocks]
    q_ref, g_ref, dq_ref, win, kt, scores, dprobs, acc, dqt, sems, io_sems = refs[4 + 6 * blocks :]

    slots = blocks * local_tiles
    c = lax.axis_index("ctx")
    g = lax.axis_index("grp")
    base = (c - reach) * local_tiles
    to_log2 = scale * math.log2(math.e)

    def tile_rows(b, owner):
        return pl.ds(pl.multiple_of((b * local_tiles + owner) * TILE, TILE), TILE)

    copies = [
        pltpu.make_async_copy(q_hbm, q_ref, io_sems.at[0]),
        pltpu.make_async_copy(g_hbm, g_ref, io_sems.at[1]),
    ]
    for b in range(blocks):
        for i in range(4):
            copies.append(
                pltpu.make_async_copy(
                    piece_refs[4 * b + i], win.at[tile_rows(b, g ^ i)], sems.at[b, i]
                )
            )
    for copy in copies:
        copy.start()
    acc[...] = jnp.zeros_like(acc)
    for copy in copies:
        copy.wait()

    doc_count = doc_ref.shape[0]
    low = first_tile_of(doc_ref, doc_count, c * local_tiles) - base

    @pl.loop(low, slots)
    def _(j):
        tile = pl.ds(pl.multiple_of(j * TILE, TILE), TILE)
        kt[:, tile] = win[tile, :DH].T

    half = TILE // 2
    causal = lax.broadcasted_iota(jnp.int32, (half, half), 0) <= lax.broadcasted_iota(
        jnp.int32, (half, half), 1
    )

    def widen_lanes(x):
        return jnp.concatenate([jnp.zeros_like(x), x], axis=1)

    @pl.loop(0, local_tiles)
    def _(t):
        rows = pl.ds(pl.multiple_of(t * TILE, TILE), TILE)
        q = q_ref[rows, :]
        go = g_ref[rows, :]
        qt = q.T
        gt = go.T
        diag = reach * local_tiles + t
        first = first_tile_of(doc_ref, doc_count, c * local_tiles + t) - base

        def key_rows(j, count):
            return pl.ds(pl.multiple_of(j * TILE, TILE), count * TILE)

        def in_steps(step, carry, sizes=(4, 3, 2, 1)):
            lo = first
            for size in sizes:
                steps = (diag - lo) // size
                carry = lax.fori_loop(
                    0, steps, lambda i, x, lo=lo, size=size: step(lo + i * size, size, x), carry
                )
                lo = lo + steps * size
            return carry

        def raw_scores(at, queries_t):
            return jnp.dot(win[at, :DH], queries_t, preferred_element_type=F32) * to_log2

        upper = pl.ds(pl.multiple_of(diag * TILE, half), half)
        lower = pl.ds(pl.multiple_of(diag * TILE + half, half), half)
        slot = diag - first
        upper_to = pl.ds(pl.multiple_of(slot * TILE, half), half)
        lower_to = pl.ds(pl.multiple_of(slot * TILE + half, half), half)

        def diag_scores():
            s0 = raw_scores(upper, qt)
            s0 = jnp.concatenate(
                [jnp.where(causal, s0[:, :half], NEG_FILL), s0[:, half:]], axis=1
            )
            s1 = jnp.where(causal, raw_scores(lower, qt[:, half:]), NEG_FILL)
            return s0, s1

        def column_sum(x):
            return jnp.sum(fold_rows(x), axis=0)

        def forward(ref, s0, s1, sizes=(4, 3, 2, 1)):
            def step(j, count, total):
                p = jnp.exp2(raw_scores(key_rows(j, count), qt) - ref)
                scores[key_rows(j - first, count), :] = p
                return total + column_sum(p)

            p0 = jnp.exp2(s0 - ref)
            p1 = jnp.exp2(s1 - ref[:, half:])
            scores[upper_to, :] = p0
            scores[lower_to, half:] = p1
            total = column_sum(p0) + widen_lanes(column_sum(p1))
            return jnp.sum(in_steps(step, total, sizes), axis=0, keepdims=True)

        def diag_top(s0, s1):
            top0 = jnp.max(s0, axis=0, keepdims=True)
            top1 = jnp.max(s1, axis=0, keepdims=True)
            return jnp.concatenate(
                [top0[:, :half], jnp.maximum(top0[:, half:], top1)], axis=1
            )

        def exact():
            def step(j, count, top):
                s = raw_scores(key_rows(j, count), qt)
                return jnp.maximum(top, jnp.max(s, axis=0, keepdims=True))

            s0, s1 = diag_scores()
            return forward(in_steps(step, diag_top(s0, s1), (1,)), s0, s1, (1,))

        s0, s1 = diag_scores()
        total = forward(diag_top(s0, s1), s0, s1)
        fits = jnp.max(jnp.where(total < HUGE, 0.0, 1.0)) == 0.0
        inv = 1.0 / lax.cond(fits, lambda: total, exact)

        def part_of_delta(p, dp, inv):
            return column_sum(to_bf16(p * inv).astype(F32) * dp)

        def delta_step(j, count, delta):
            to = key_rows(j - first, count)
            dp = jnp.dot(win[key_rows(j, count), DH:], gt, preferred_element_type=F32)
            dprobs[to, :] = dp
            return delta + part_of_delta(scores[to, :], dp, inv)

        dp0 = jnp.dot(win[upper, DH:], gt, preferred_element_type=F32)
        dp1 = jnp.dot(win[lower, DH:], gt[:, half:], preferred_element_type=F32)
        dprobs[upper_to, :] = dp0
        dprobs[lower_to, half:] = dp1
        delta = part_of_delta(scores[upper_to, :], dp0, inv)
        delta += widen_lanes(part_of_delta(scores[lower_to, half:], dp1, inv[:, half:]))
        delta = jnp.sum(in_steps(delta_step, delta), axis=0, keepdims=True)
        dqt[...] = jnp.zeros_like(dqt)

        def grads(p, dp, inv, delta):
            p = p * inv
            return to_bf16(p), to_bf16(p * (dp - delta))

        def add_grads(at, low, ds, q, go):
            acc[at, DH:] += jnp.dot(low, go, preferred_element_type=F32)
            acc[at, :DH] += jnp.dot(ds, q, preferred_element_type=F32)

        def backward(j, count, carry):
            at = key_rows(j, count)
            to = key_rows(j - first, count)
            low, ds = grads(scores[to, :], dprobs[to, :], inv, delta)
            add_grads(at, low, ds, q, go)
            dqt[...] += jnp.dot(kt[:, at], ds, preferred_element_type=F32)
            return carry

        low0, ds0 = grads(scores[upper_to, :], dprobs[upper_to, :], inv, delta)
        low1, ds1 = grads(
            scores[lower_to, half:], dprobs[lower_to, half:], inv[:, half:], delta[:, half:]
        )
        add_grads(upper, low0, ds0, q, go)
        add_grads(lower, low1, ds1, q[half:], go[half:])
        dqt[...] = jnp.dot(kt[:, upper], ds0, preferred_element_type=F32)
        dqt[:, half:] += jnp.dot(kt[:, lower], ds1, preferred_element_type=F32)
        in_steps(backward, jnp.int32(0))
        dq_ref[rows, :] = to_bf16((dqt[...] * scale).T)

    copies = [pltpu.make_async_copy(dq_ref, dq_hbm, io_sems.at[0])]
    copies[0].start()
    for b in range(blocks):
        for i in range(4):
            at = tile_rows(b, g ^ i)
            win[at, :] = to_bf16(acc[at, :])
            copy = pltpu.make_async_copy(
                win.at[at], out_refs[2 * b + i % 2].at[i // 2], sems.at[b, i]
            )
            copy.start()
            copies.append(copy)
    for copy in copies:
        copy.wait()


def up_ctx(x, by):
    n = lax.axis_size("ctx")
    return lax.ppermute(x, "ctx", [(i, (i + by) % n) for i in range(n)])


def down_ctx(x, by):
    n = lax.axis_size("ctx")
    return lax.ppermute(x, "ctx", [(i, i - by) for i in range(by, n)])


def swap_grp(x, bit):
    n = lax.axis_size("grp")
    return lax.ppermute(x, "grp", [(i, i ^ bit) for i in range(n)])


def four_tiles(x, y):
    return [x, swap_grp(x, 1), y, swap_grp(y, 1)]


def spans_blocks(doc_tiles, local_tiles):
    ids = jnp.arange(doc_tiles.shape[0])
    begins = jnp.sum(jnp.where(ids[None, :] < ids[:, None], doc_tiles[None, :], 0), axis=1)
    lasts = begins + doc_tiles - 1
    return jnp.max(lasts // local_tiles - begins // local_tiles)


def with_window(queries, grad_out, doc_tiles, pieces, *, local_tiles, reach):
    blocks = reach + 1
    slots = blocks * local_tiles
    scale = 1.0 / math.sqrt(DH)
    width = 2 * DH

    own_pieces, *far, (x3,) = pieces
    if reach == 3:
        far.append([x3, swap_grp(x3, 1), swap_grp(x3, 2)])
    pieces = [own_pieces] + [block + [swap_grp(block[2], 1)] for block in far]
    pieces = [tile for block in reversed(pieces) for tile in block]

    hbm = pl.BlockSpec(memory_space=pl.ANY)
    half = jax.ShapeDtypeStruct((local_tiles // 2, TILE, width), BF16)
    grad_queries, *halves = pl.pallas_call(
        lambda *refs: local_kernel(*refs, local_tiles=local_tiles, reach=reach, scale=scale),
        out_shape=(jax.ShapeDtypeStruct(queries.shape, BF16),) + (half,) * (2 * blocks),
        in_specs=[pl.BlockSpec(memory_space=pltpu.SMEM)] + [hbm] * (2 + 4 * blocks),
        out_specs=(hbm,) * (1 + 2 * blocks),
        scratch_shapes=[
            pltpu.VMEM(queries.shape, BF16),
            pltpu.VMEM(queries.shape, BF16),
            pltpu.VMEM(queries.shape, BF16),
            pltpu.VMEM((slots * TILE, width), BF16),
            pltpu.VMEM((DH, slots * TILE), BF16),
            pltpu.VMEM((MAXT * TILE, TILE), F32),
            pltpu.VMEM((MAXT * TILE, TILE), F32),
            pltpu.VMEM((slots * TILE, width), F32),
            pltpu.VMEM((DH, TILE), F32),
            pltpu.SemaphoreType.DMA((blocks, 4)),
            pltpu.SemaphoreType.DMA((2,)),
        ],
        compiler_params=pltpu.CompilerParams(vmem_limit_bytes=(40 + 4 * reach) * 1024 * 1024),
    )(doc_tiles, queries, grad_out, *pieces)

    mine, theirs = {}, {}
    for d in range(reach, -1, -1):
        keep, send = halves[2 * (reach - d)], halves[2 * (reach - d) + 1]
        got = swap_grp(send, 1).astype(F32)
        mine[d] = keep[0].astype(F32) + got[0]
        theirs[d] = keep[1].astype(F32) + got[1]
    far_theirs = down_ctx(to_bf16(theirs[2]), 2).astype(F32)
    own = mine[0] + down_ctx(to_bf16(mine[2]), 2).astype(F32)
    own = own + swap_grp(to_bf16(theirs[0] + far_theirs), 2).astype(F32)
    near = to_bf16(theirs[1])
    if reach == 3:
        got, near = lax.optimization_barrier((swap_grp(to_bf16(theirs[3]), 2), near))
        own = own + down_ctx(to_bf16(mine[3] + got.astype(F32)), 3).astype(F32)
    near = mine[1] + swap_grp(near, 2).astype(F32)
    own = own + down_ctx(to_bf16(near), 1).astype(F32)
    grad_kv = to_bf16(jnp.concatenate([own[:, :DH] * scale, own[:, DH:]], axis=1))
    return (grad_queries, grad_kv)


def shards(queries, kv_cache, grad_out, doc_tiles):
    local_tiles = queries.shape[0] // TILE
    most = (MAXT - 2) // local_tiles + 1
    assert most == 3
    x0 = kv_cache
    spans = spans_blocks(doc_tiles, local_tiles)
    x1, spans = lax.optimization_barrier((up_ctx(x0, 1), spans))
    y0, spans = lax.optimization_barrier((swap_grp(x0, 2), spans))
    x2 = up_ctx(x0, 2)
    y1 = swap_grp(x1, 2)
    y2 = up_ctx(y0, 2)
    x1, x2 = lax.optimization_barrier((x1, x2))
    x3 = lax.cond(spans >= most, lambda x: up_ctx(x, 2), lambda x: x, x1)
    x0, y0, x1, x3 = lax.optimization_barrier((x0, y0, x1, x3))
    pieces = [four_tiles(x0, y0), [x1, swap_grp(x1, 1), y1], [x2, swap_grp(x2, 1), y2], [x3]]
    return lax.cond(
        spans >= most,
        lambda *args: with_window(*args, local_tiles=local_tiles, reach=most),
        lambda *args: with_window(*args, local_tiles=local_tiles, reach=most - 1),
        queries, grad_out, doc_tiles, pieces,
    )


def solution(mesh):
    placed = (P("ctx", "grp"), P(("ctx", "grp"), None), P("ctx", "grp"), P())
    return jax.shard_map(
        shards,
        mesh=mesh,
        in_specs=placed,
        out_specs=(P("ctx", "grp"), P(("ctx", "grp"), None)),
        check_vma=False,
    )
```
